128 devices in a mesh: wide: 16 (over y, z), narrow: 8 (over x, core).
Axes of the slice: x: 4, y: 4, z: 4, core: 2. Of those that a mesh axis runs over, the one named last changes fastest.
Arguments:
- stream_hat: bfloat16 [2, 8192, 8192], P(None, ('wide', 'narrow')), may hold values from -2.682209e-07 to 2.682209e-07
- dye: bfloat16 [8192, 8192], P(('wide', 'narrow')), may hold values from -6 to 6
- float_slot: int32 [1048576], P(('wide', 'narrow')), may hold values from 0 to 255, as said below
- float_row: int32 [1048576], P(('wide', 'narrow')), may hold values from 0 to 62
- float_col: int32 [1048576], P(('wide', 'narrow')), may hold values from 0 to 126
- float_frac: float32 [2, 1048576], P(None, ('wide', 'narrow')), may hold values from 0 to 1
- float_dye: float32 [1048576], P(('wide', 'narrow')), may hold values from 0.1 to 10
- tile_lists: int32 [16, 256], replicated, may hold values from -1 to 8191, as said below
Outputs:
- float_velocity: float32 [2, 1048576], P(None, ('wide', 'narrow'))
- dye_hat: float32 [2, 8192, 8192], P(None, ('wide', 'narrow'))
The draws below stay inside these ranges and needn't reach their ends.
Inputs may be any that keep to these rules, and one draw needn't show every extreme that they name: `tile_lists`: row g holds the distinct tiles needed by floats of group g, in no particular order, followed by -1 entries; tile t covers x cells from 128 (t % 64) and y cells from 64 (t // 64), and lies on device t // 64. At most 2 entries of a row lie on one device, every row has exactly 2 on some device, and some row has no -1 entry. `float_slot`: float f names a used entry of row f // 65536 of tile_lists.
All inputs are finite; a program needn't handle non-finite values.
Results may differ from the reference program's by a relative error of at most 0.0065.
Values may be sent and summed in bfloat16 or wider, within the bound.
No kernel may reach another device: no remote copies, remote signals or barrier semaphores. Data moves between devices by JAX's collectives and lax.ppermute only.
A program may use at most 192 MiB of HBM per device.

```python
import math
import jax
import jax.numpy as jnp
from jax import lax

N = 8192
TX = 128
TY = 64
CAPO = 2
FL = 8192
GROUP_FLOATS = 65536
FLOATS = 1048576
N_WIDE = 16
N_NARROW = 8
DEVICES = 128


def tile_plan(key):
    keys = jax.random.split(key, 7)
    groups = N_WIDE
    owners = DEVICES
    per_owner = N // DEVICES // TY * (N // TX)
    slots = owners * CAPO
    level = jax.random.randint(keys[0], (groups, 1), 1, 5)
    active = jax.random.randint(keys[1], (groups, owners), 0, 4) < level
    amount = jax.random.randint(keys[2], (groups, owners), 1, CAPO + 1)
    counts = jnp.where(active, amount, 0)
    topmost = jax.random.randint(keys[3], (groups,), 0, owners)
    counts = jnp.where(jnp.arange(owners)[None, :] == topmost[:, None], CAPO, counts)
    fullest = jax.random.randint(keys[4], (), 0, groups)
    counts = jnp.where(jnp.arange(groups)[:, None] == fullest, CAPO, counts)
    scores = jax.random.randint(keys[5], (groups, owners, per_owner), 0, 2 ** 20) * per_owner + jnp.arange(per_owner)[None, None, :]
    chosen = jnp.argsort(scores, axis=-1)[:, :, :CAPO]
    tiles = jnp.arange(owners)[None, :, None] * per_owner + chosen
    valid = jnp.arange(CAPO)[None, None, :] < counts[:, :, None]
    tiles = jnp.where(valid, tiles, -1).reshape(groups, slots)
    valid = valid.reshape(groups, slots)
    ranks = jax.random.randint(keys[6], (groups, slots), 0, 2 ** 20) * slots + jnp.arange(slots)[None, :]
    ranks = jnp.where(valid, ranks, ranks + 2 ** 30)
    order = jnp.argsort(ranks, axis=-1)
    lists = jnp.take_along_axis(tiles, order, axis=-1).astype(jnp.int32)
    return (lists, jnp.sum(counts, axis=-1).astype(jnp.int32))


def draw_tile_lists(key, part):
    lists, totals = tile_plan(key)
    return lists


def draw_float_slot(key, part):
    lists, totals = tile_plan(key)
    key = jax.random.fold_in(key, 3)
    group = jnp.arange(FL * DEVICES) // (FL * N_NARROW)
    return jax.random.randint(key, (FL * DEVICES,), 0, totals[group]).astype(jnp.int32)


def touch_ends(drawn, own_key, low, top_value):
    index_at = [jax.random.randint(jax.random.fold_in(own_key, axis), (), 0, length) for axis, length in enumerate(drawn.shape)]
    widest = drawn.shape.index(max(drawn.shape))
    beside = index_at[:widest] + [(index_at[widest] + 1) % drawn.shape[widest]] + index_at[widest + 1:]
    return drawn.at[tuple(index_at)].set(low).at[tuple(beside)].set(top_value)


def shard_levels(rng, dims, cuts, low, top_value):
    def one(axis_at, blocks):
        draws = jax.random.uniform(jax.random.fold_in(jax.random.fold_in(rng, 6), axis_at), (blocks,), jnp.float32, low / len(cuts), top_value / len(cuts))
        return jnp.repeat(jnp.exp(draws), dims[axis_at] // blocks).reshape((-1,) + (1,) * (len(dims) - axis_at - 1))

    factor_of = one(*cuts[0])
    for cut in cuts[1:]:
        factor_of = factor_of * one(*cut)
    return factor_of


def noise(rng, dims, deviation, reach, pieces=(), kind=jnp.bfloat16):
    values = deviation * jax.random.normal(rng, dims, jnp.float32)
    if pieces:
        values = values * shard_levels(rng, dims, pieces, -0.22, 0.18)
    return jnp.clip(values, -reach, reach).astype(kind)


def setup_inputs(seed: int = 0) -> dict:
    arg_keys = jax.random.split(jax.random.key(seed), 9)
    return {
        "stream_hat": noise(arg_keys[0], (2, N, N), (3.0 / (N * N)), 2.682209014892578e-07, ((1, 128),)),
        "dye": noise(arg_keys[1], (N, N), 1.0, 6.0, ((0, 128),)),
        "float_slot": draw_float_slot(jax.random.fold_in(arg_keys[8], 71), 0),
        "float_row": touch_ends(jax.random.randint(arg_keys[3], (FLOATS,), 0, TY - 1), jax.random.fold_in(arg_keys[3], 1), 0, (TY - 1) - 1).astype(jnp.int32),
        "float_col": touch_ends(jax.random.randint(arg_keys[4], (FLOATS,), 0, TX - 1), jax.random.fold_in(arg_keys[4], 1), 0, (TX - 1) - 1).astype(jnp.int32),
        "float_frac": jnp.clip(1.0 * jax.random.uniform(arg_keys[5], (2, FLOATS), jnp.float32) ** shard_levels(arg_keys[5], (2, FLOATS), ((1, 128),), -0.2, 0.2), 0.0, 1.0),
        "float_dye": jnp.clip(jnp.exp(math.log(10.0) - 4.6051702 * jax.random.uniform(arg_keys[6], (FLOATS,), jnp.float32) ** shard_levels(arg_keys[6], (FLOATS,), ((0, 128),), -0.2, 0.2)), 0.1, 10.0),
        "tile_lists": draw_tile_lists(jax.random.fold_in(arg_keys[8], 71), 0),
    }


def signed_wave(length):
    index = jnp.arange(length)
    return jnp.where(index >= length // 2, index - length, index).astype(jnp.float32)


def reference(stream_hat, dye, float_slot, float_row, float_col, float_frac, float_dye, tile_lists):
    spec_re = stream_hat[0].astype(jnp.float32)
    spec_im = stream_hat[1].astype(jnp.float32)
    wave = signed_wave(N)
    spectrum = lax.complex(spec_re, spec_im)
    u_field = (jnp.real(jnp.fft.ifft2(-1j * wave[None, :] * spectrum)) * (N * N)).astype(jnp.bfloat16)
    v_field = (jnp.real(jnp.fft.ifft2(1j * wave[:, None] * spectrum)) * (N * N)).astype(jnp.bfloat16)
    group = (jnp.arange(FLOATS) // GROUP_FLOATS).astype(jnp.int32)
    tile = tile_lists[group, float_slot]
    cell_x = TX * (tile % (N // TX)) + float_col
    cell_y = TY * (tile // (N // TX)) + float_row
    frac_y = float_frac[0]
    frac_x = float_frac[1]
    weights = [(1.0 - frac_x) * (1.0 - frac_y), (1.0 - frac_x) * frac_y, frac_x * (1.0 - frac_y), frac_x * frac_y]
    corner_x = [cell_x, cell_x, cell_x + 1, cell_x + 1]
    corner_y = [cell_y, cell_y + 1, cell_y, cell_y + 1]
    speed_u = jnp.zeros((FLOATS,), jnp.float32)
    speed_v = jnp.zeros((FLOATS,), jnp.float32)
    for weight, pos_x, pos_y in zip(weights, corner_x, corner_y):
        speed_u = speed_u + weight * u_field[pos_x, pos_y].astype(jnp.float32)
        speed_v = speed_v + weight * v_field[pos_x, pos_y].astype(jnp.float32)
    float_velocity = jnp.stack([speed_u, speed_v])
    all_x = jnp.concatenate(corner_x)
    all_y = jnp.concatenate(corner_y)
    all_w = jnp.concatenate([float_dye * weight for weight in weights])
    deposit = jnp.zeros((N, N), jnp.float32).at[all_x, all_y].add(all_w)
    total = dye.astype(jnp.float32) + deposit.T
    spectral = jnp.fft.fft2(total)
    dye_hat = jnp.stack([jnp.real(spectral).T, jnp.imag(spectral).T]).astype(jnp.float32) / N
    return float_velocity, dye_hat
```

```python
import numpy as np, math

import jax, jax.numpy as jnp
from jax import lax
from jax.sharding import PartitionSpec as P
from jax.experimental import pallas as pl
from jax.experimental.pallas import tpu as pltpu

BF = jnp.bfloat16
F32 = jnp.float32
VLIM = 60 * 1024 * 1024
NT = (((1,), (1,)), ((), ()))


def cs(num, den, sign):
    ang = sign * 2.0 * math.pi * (num % den) / den
    return np.cos(ang), np.sin(ang)


def cplx(c, s):
    return np.stack([np.stack([c, -s]), np.stack([s, c])])


def bf(x):
    return np.asarray(x, np.float32).astype(jnp.bfloat16)


def send_tables(sign, stream):
    p = np.arange(64)
    q = np.arange(128)
    c, s = cs(p[:, None] * p[None, :], 64, sign)
    w = cplx(c, s).transpose(0, 2, 1, 3)
    if stream:
        a = w.reshape(128, 128)
        signed = np.where(p >= 32, p - 64, p) * 128.0
        b = (w * signed).reshape(128, 128)
        g = np.concatenate([a, b])
    else:
        g = w[:, :, 0, :].reshape(128, 64)
    tc, ts = cs(p[:, None] * q[None, :], 8192, sign)
    c, s = cs(q[:, None] * q[None, :], 128, sign)
    w2 = cplx(c, s).transpose(2, 0, 1, 3).reshape(256, 256)
    return bf(g), np.float32(tc), np.float32(ts), bf(w2)


def recv_tables(sign, stream):
    k = np.arange(128)
    r = np.arange(64)
    c, s = cs(k[:, None] * k[None, :], 128, sign)
    w1 = cplx(c, s).transpose(0, 2, 3, 1).reshape(256, 256)
    tc, ts = cs(k[:, None] * r[None, :], 8192, sign)
    tc = np.concatenate([tc, tc], 1)
    ts = np.concatenate([ts, ts], 1)
    c, s = cs(r[:, None] * r[None, :], 64, sign)
    w = cplx(c, s)
    v = np.zeros((2, 2, 64, 2, 2, 64))
    for e in range(2):
        v[:, e, :, :, e, :] = w.transpose(0, 2, 1, 3)
    if stream:
        v = v[0].reshape(128, 256)
    else:
        v = v.reshape(256, 256) / 8192.0
    return bf(w1), np.float32(tc), np.float32(ts), bf(v)


def stream_send_kernel(wa_ref, s_ref, g_ref, tc_ref, ts_ref, w2_ref, o_ref, xs, tre, tim, of):
    def load(p, carry):
        at = pl.multiple_of(p * 128, 128)
        for c in range(2):
            row = pl.multiple_of((c * 64 + p) * 64, 64)
            xs[pl.ds(row, 64), :] = s_ref[c, :, pl.ds(at, 128)].astype(F32)
        return carry

    lax.fori_loop(0, 64, load, 0, unroll=4)
    q = lax.broadcasted_iota(jnp.int32, (64, 128), 1).astype(F32)

    def rows(r, carry):
        x = xs[pl.ds(r, 128, stride=64), :].astype(BF)
        z = jnp.dot(g_ref[...], x, preferred_element_type=F32)
        tc = tc_ref[...]
        ts = ts_ref[...]
        are, aim, bre, bim = z[:64], z[64:128], z[128:192], z[192:]
        ure = bre + q * are
        uim = bim + q * aim
        wa = wa_ref[0, r]
        base = pl.multiple_of(r * 128, 128)
        vre = are * tc - aim * ts
        vim = are * ts + aim * tc
        tre[pl.ds(base, 64), :] = ure * ts + uim * tc
        tim[pl.ds(base, 64), :] = uim * ts - ure * tc
        tre[pl.ds(base + 64, 64), :] = -wa * vim
        tim[pl.ds(base + 64, 64), :] = wa * vre
        return carry

    lax.fori_loop(0, 64, rows, 0, unroll=2)

    def cols(t, carry):
        parts = []
        for f in range(2):
            at = pl.ds(f * 64 + t, 64, stride=128)
            parts.append(jnp.concatenate([tre[at, :].astype(BF), tim[at, :].astype(BF)], axis=1))
        m = jnp.concatenate(parts, axis=0)
        of[pl.ds(t, 256, stride=64), :] = lax.dot_general(w2_ref[...], m, NT, preferred_element_type=F32)
        return carry

    lax.fori_loop(0, 64, cols, 0, unroll=2)

    def store(i, carry):
        o_ref[i] = of[pl.ds(pl.multiple_of(i * 64, 64), 64), :].astype(BF)
        return carry

    lax.fori_loop(0, 256, store, 0, unroll=8)


VM = pl.BlockSpec(memory_space=pltpu.VMEM)
SM = pl.BlockSpec(memory_space=pltpu.SMEM)


def call(kernel, outs, specs, scratch, cost, name, *args):
    return pl.pallas_call(
        kernel,
        out_shape=outs,
        in_specs=specs,
        out_specs=jax.tree.map(lambda _: VM, outs),
        scratch_shapes=scratch,
        compiler_params=pltpu.CompilerParams(vmem_limit_bytes=VLIM),
        cost_estimate=pl.CostEstimate(flops=cost, bytes_accessed=1 << 20, transcendentals=0),
        name=name,
    )(*args)


def stream_send(stream, wa):
    return call(
        stream_send_kernel,
        jax.ShapeDtypeStruct((256, 64, 128), BF),
        [SM] + [VM] * 5,
        [pltpu.VMEM((8192, 128), F32)] * 3 + [pltpu.VMEM((16384, 128), F32)],
        int(6e9), "stream_send",
        wa, stream, *send_tables(1.0, True),
    )


def stream_recv_kernel(x_ref, w1_ref, tc_ref, ts_ref, v_ref, o_ref, xf, of):
    def load(i, carry):
        xf[pl.ds(pl.multiple_of(i * 64, 64), 64), :] = x_ref[i].astype(F32)
        return carry

    lax.fori_loop(0, 256, load, 0, unroll=8)

    def step(t, carry):
        d = xf[pl.ds(t, 256, stride=64), :].astype(BF)
        z = jnp.dot(w1_ref[...], d, preferred_element_type=F32)
        re, im = z[:128], z[128:]
        tc = tc_ref[...]
        ts = ts_ref[...]
        m = jnp.concatenate([(re * tc - im * ts).astype(BF), (re * ts + im * tc).astype(BF)], axis=1)
        out = lax.dot_general(v_ref[...], m, NT, preferred_element_type=F32)
        for f in range(2):
            of[pl.ds(2 * t + f, 64, stride=128), :] = out[f * 64 : f * 64 + 64]
        return carry

    lax.fori_loop(0, 64, step, 0, unroll=2)

    def store(i, carry):
        o_ref[i] = of[pl.ds(pl.multiple_of(i * 128, 128), 128), :].astype(BF)
        return carry

    lax.fori_loop(0, 64, store, 0, unroll=4)


def stream_recv(x):
    return call(
        stream_recv_kernel,
        jax.ShapeDtypeStruct((64, 128, 128), BF),
        [VM] * 5,
        [pltpu.VMEM((16384, 128), F32), pltpu.VMEM((8192, 128), F32)],
        int(6e9), "stream_recv",
        x, *recv_tables(1.0, True),
    )


def dye_send_kernel(idx_ref, dye_ref, ret_ref, g_ref, tc_ref, ts_ref, w2_ref, o_ref, xs, tre, tim, of):
    def load(p, carry):
        at = pl.multiple_of(p * 128, 128)
        xs[pl.ds(pl.multiple_of(p * 64, 64), 64), :] = dye_ref[:, pl.ds(at, 128)].astype(F32)
        return carry

    lax.fori_loop(0, 64, load, 0, unroll=4)

    def place(n, carry):
        tile = idx_ref[0, n]

        @pl.when(tile >= 0)
        def _():
            g = n // 2
            e = n % 2
            total = ret_ref[g * 8 + e].astype(F32)
            for x in range(1, 4):
                total = total + ret_ref[g * 8 + 2 * x + e].astype(F32)
            at = pl.ds(pl.multiple_of(tile * 64, 64), 64)
            xs[at, :] = xs[at, :] + total

        return carry

    lax.fori_loop(0, 32, place, 0)

    def rows(r, carry):
        x = xs[pl.ds(r, 64, stride=64), :].astype(BF)
        z = jnp.dot(g_ref[...], x, preferred_element_type=F32)
        re, im = z[:64], z[64:]
        tc = tc_ref[...]
        ts = ts_ref[...]
        base = pl.multiple_of(r * 64, 64)
        tre[pl.ds(base, 64), :] = re * tc - im * ts
        tim[pl.ds(base, 64), :] = re * ts + im * tc
        return carry

    lax.fori_loop(0, 64, rows, 0, unroll=2)

    def cols(t, carry):
        parts = []
        for e in range(2):
            at = pl.ds(2 * t + e, 64, stride=64)
            parts.append(jnp.concatenate([tre[at, :].astype(BF), tim[at, :].astype(BF)], axis=1))
        m = jnp.concatenate(parts, axis=0)
        of[pl.ds(t, 256, stride=32), :] = lax.dot_general(w2_ref[...], m, NT, preferred_element_type=F32)
        return carry

    lax.fori_loop(0, 32, cols, 0, unroll=2)

    def store(i, carry):
        o_ref[i] = of[pl.ds(pl.multiple_of(i * 32, 32), 32), :].astype(BF)
        return carry

    lax.fori_loop(0, 256, store, 0, unroll=8)


def dye_send(idx, dye, ret):
    return call(
        dye_send_kernel,
        jax.ShapeDtypeStruct((256, 32, 128), BF),
        [SM] + [VM] * 6,
        [pltpu.VMEM((4096, 128), F32)] * 3 + [pltpu.VMEM((8192, 128), F32)],
        int(4e9), "dye_send",
        idx, dye, ret, *send_tables(-1.0, False),
    )


def dye_recv_kernel(x_ref, w1_ref, tc_ref, ts_ref, v_ref, o_ref, xf, of):
    def load(i, carry):
        xf[pl.ds(pl.multiple_of(i * 32, 32), 32), :] = x_ref[i].astype(F32)
        return carry

    lax.fori_loop(0, 256, load, 0, unroll=8)

    def step(t, carry):
        d = xf[pl.ds(t, 256, stride=32), :].astype(BF)
        z = jnp.dot(w1_ref[...], d, preferred_element_type=F32)
        re, im = z[:128], z[128:]
        tc = tc_ref[...]
        ts = ts_ref[...]
        m = jnp.concatenate([(re * tc - im * ts).astype(BF), (re * ts + im * tc).astype(BF)], axis=1)
        out = lax.dot_general(v_ref[...], m, NT, preferred_element_type=F32)
        for c in range(2):
            for e in range(2):
                row = c * 4096 + (t // 4) * 512 + (2 * t + e) % 8
                of[pl.ds(row, 64, stride=8), :] = out[(2 * c + e) * 64 : (2 * c + e) * 64 + 64]
        return carry

    lax.fori_loop(0, 32, step, 0, unroll=2)

    def store(n, carry):
        c = n // 8
        t8 = n % 8
        base = pl.multiple_of(n * 512, 512)
        at = pl.ds(pl.multiple_of(t8 * 8, 8), 8)
        for j in range(64):
            o_ref[c, at, j * 128 : j * 128 + 128] = of[pl.ds(base + j * 8, 8), :]
        return carry

    lax.fori_loop(0, 16, store, 0)


def dye_recv(x):
    return call(
        dye_recv_kernel,
        jax.ShapeDtypeStruct((2, 64, 8192), F32),
        [VM] * 5,
        [pltpu.VMEM((8192, 128), F32)] * 2,
        int(4e9), "dye_recv",
        x, *recv_tables(-1.0, False),
    )

CAPO = 2


def deposit_kernel(mb_ref, nb_ref, fy_ref, fx_ref, am_ref, o_ref, m_ref, acc):
    step = pl.program_id(0)
    width = mb_ref.shape[1]
    am = am_ref[...]
    hi = am * fy_ref[...]
    lo = am - hi
    mb = mb_ref[...]
    nb = nb_ref[...]
    fx = fx_ref[...]
    gx = 1.0 - fx

    def build_m(i, carry):
        at = pl.multiple_of(i * 64, 64)
        d = lax.broadcasted_iota(jnp.int32, (64, width), 0) + (i * 64 - mb)
        w = jnp.where(d == 0, lo, jnp.where(d == 1, hi, 0.0))
        m_ref[pl.ds(at, 64), :] = w.astype(BF)
        return carry

    lax.fori_loop(0, 16, build_m, 0)

    def part(i, first):
        d = lax.broadcasted_iota(jnp.int32, (256, width), 0) + (i * 256 - nb)
        w = jnp.where(d == 0, gx, jnp.where(d == 1, fx, 0.0)).astype(BF)
        z = lax.dot_general(m_ref[...], w, NT, preferred_element_type=F32)
        acc[i] = z if first else acc[i] + z

    @pl.when(step == 0)
    def _():
        lax.fori_loop(0, 8, lambda i, c: (part(i, True), c)[1], 0)

    @pl.when(step > 0)
    def _():
        lax.fori_loop(0, 8, lambda i, c: (part(i, False), c)[1], 0)

    @pl.when(step == pl.num_programs(0) - 1)
    def _():
        def store(p, carry):
            row = pl.multiple_of((p // 8) * 64, 64)
            for h in range(2):
                o_ref[p // 8 * 16 + p % 8 * 2 + h] = acc[p % 8, pl.ds(row, 64), h * 128 : h * 128 + 128].astype(BF)
            return carry

        lax.fori_loop(0, 128, store, 0, unroll=4)


def deposit(mb, nb, fy, fx, am, width=1024):
    blk = pl.BlockSpec((1, width), lambda i: (0, i))
    return pl.pallas_call(
        deposit_kernel,
        grid=(8192 // width,),
        out_shape=jax.ShapeDtypeStruct((256, 64, 128), BF),
        in_specs=[blk] * 5,
        out_specs=pl.BlockSpec((256, 64, 128), lambda i: (0, 0, 0)),
        scratch_shapes=[pltpu.VMEM((1024, width), BF), pltpu.VMEM((8, 1024, 256), F32)],
        compiler_params=pltpu.CompilerParams(vmem_limit_bytes=VLIM),
        cost_estimate=pl.CostEstimate(flops=int(34e9), bytes_accessed=4 << 20, transcendentals=0),
        name="deposit",
    )(mb, nb, fy, fx, am)


def gather_kernel(base_ref, a_ref, b_ref, col_ref, fy_ref, fx_ref, o_ref, st, g):
    def load(i, carry):
        at = pl.multiple_of(i * 128, 128)
        st[pl.ds(at, 128), :] = a_ref[i].astype(F32)
        st[pl.ds(at + 16384, 128), :] = b_ref[i].astype(F32)
        return carry

    lax.fori_loop(0, 128, load, 0, unroll=2)
    sub = lax.broadcasted_iota(jnp.int32, (8, 128), 0)
    off = lax.broadcasted_iota(jnp.int32, (8, 128), 1) - sub // 4
    upper = sub % 4 >= 2
    odd = sub % 2 == 1
    xs = lax.broadcasted_iota(jnp.int32, (128, 128), 0)

    def chunk(n, carry):
        for f in range(128):
            g[f * 4 : f * 4 + 4, :] = st[pl.ds(base_ref[n, f], 4), :]
        at = pl.ds(pl.multiple_of(n * 128, 128), 128)
        col = col_ref[:, at]
        fy = fy_ref[:, at]
        fx = fx_ref[:, at]
        d = xs - col
        w = jnp.where(d == 0, 1.0 - fx, jnp.where(d == 1, fx, 0.0))
        hi = w.astype(BF)
        lo = (w - hi.astype(F32)).astype(BF)
        rows = g[...].astype(BF)
        z = jnp.dot(rows, hi, preferred_element_type=F32) + jnp.dot(rows, lo, preferred_element_type=F32)
        total = jnp.zeros((8, 128), F32)
        for i in range(64):
            total = total + jnp.where(off == 2 * i, z[8 * i : 8 * i + 8], 0.0)
        total = total * jnp.where(upper, fy, 1.0 - fy)
        o_ref[0:1, at] = jnp.sum(jnp.where(odd, 0.0, total), axis=0, keepdims=True)
        o_ref[1:2, at] = jnp.sum(jnp.where(odd, total, 0.0), axis=0, keepdims=True)
        return carry

    lax.fori_loop(0, 64, chunk, 0)


def gather(base, a, b, col, fy, fx):
    return call(
        gather_kernel,
        jax.ShapeDtypeStruct((2, 8192), F32),
        [SM] + [VM] * 5,
        [pltpu.VMEM((32768, 128), F32), pltpu.VMEM((512, 128), F32)],
        int(2e10), "gather",
        base, a, b, col, fy, fx,
    )


AXES = ("wide", "narrow")


def spread(blocks):
    return lax.all_to_all(blocks, AXES, split_axis=0, concat_axis=0, tiled=True)


def swap_cores(x):
    n = lax.axis_size("narrow")
    return lax.ppermute(x, "narrow", [(i, i ^ 1) for i in range(n)])


def shards(stream_hat, dye, float_slot, float_row, float_col, float_frac, float_dye, tile_lists):
    device = lax.axis_index(AXES)
    group = lax.axis_index("wide")
    core = lax.axis_index("narrow") % 2
    wave = device * 64 + jnp.arange(64)
    wave = jnp.where(wave >= 4096, wave - 8192, wave).astype(F32)[None]
    slot = float_slot.reshape(64, 128)
    row = float_row.reshape(64, 128)
    col = float_col.reshape(64, 128)

    mine = (tile_lists >= 0) & (tile_lists // 64 == device)
    place = jnp.cumsum(mine.astype(jnp.int32), axis=1) - 1
    local = tile_lists % 64 + 1
    send_index = jnp.stack(
        [jnp.sum(jnp.where(mine & (place == e), local, 0), axis=1) for e in range(CAPO)], axis=1
    ) - 1

    own_list = lax.dynamic_index_in_dim(tile_lists, group, 0, keepdims=False)
    holder = own_list // 64
    before = jnp.arange(256)[:, None] > jnp.arange(256)[None, :]
    rank = jnp.sum((before & (holder[:, None] == holder[None, :])).astype(jnp.int32), axis=1)
    position = jnp.where(own_list >= 0, jnp.where(rank == core, 0, 128) + holder, 0)
    pos = jnp.sum(
        jnp.where(jnp.arange(256)[:, None, None] == slot[None], position[:, None, None], 0), axis=0
    )

    flat = lambda x: x.reshape(1, 8192)
    fy = float_frac[0:1]
    fx = float_frac[1:2]
    dep = deposit(
        flat(pos // 16 * 64 + row), flat(pos % 16 * 128 + col), fy, fx, flat(float_dye)
    )
    dep = (dep[:128].astype(F32) + swap_cores(dep[128:]).astype(F32)).astype(BF)
    returned = spread(dep)

    spec = stream_send(stream_hat, wave)
    spec = spread(spec.reshape(128, 2, 64, 128)).reshape(256, 64, 128)
    tiles = stream_recv(spec)
    outgoing = tiles[jnp.maximum(send_index, 0)]
    outgoing = jnp.broadcast_to(outgoing[:, None], (16, 4, 2, 128, 128)).reshape(128, 128, 128)
    own = spread(outgoing)
    other = swap_cores(own)

    front = dye_send(send_index.reshape(1, 32), dye, returned)
    front = spread(front.reshape(128, 2, 32, 128)).reshape(256, 32, 128)
    dye_hat = dye_recv(front)

    velocity = gather(pos * 128 + 2 * row, own, other, flat(float_col), fy, fx)
    return (velocity, dye_hat)


def solution(mesh):
    return jax.shard_map(
        shards,
        mesh=mesh,
        in_specs=(
            P(None, AXES, None),
            P(AXES, None),
            P(AXES),
            P(AXES),
            P(AXES),
            P(None, AXES),
            P(AXES),
            P(),
        ),
        out_specs=(P(None, AXES), P(None, AXES, None)),
        check_vma=False,
    )
```

```python
import numpy as np, math

import jax, jax.numpy as jnp
from jax import lax
from jax.sharding import PartitionSpec as P
from jax.experimental import pallas as pl
from jax.experimental.pallas import tpu as pltpu

BF = jnp.bfloat16
F32 = jnp.float32
VLIM = 60 * 1024 * 1024
NT = (((1,), (1,)), ((), ()))
PAD = 72
PAD2 = 136
PAD3 = 40


def cs(num, den, sign):
    ang = sign * 2.0 * math.pi * (num % den) / den
    return np.cos(ang), np.sin(ang)


def cplx(c, s):
    return np.stack([np.stack([c, -s]), np.stack([s, c])])


def bf(x):
    return np.asarray(x, np.float32).astype(jnp.bfloat16)


def send_tables(sign, stream):
    p = np.arange(64)
    q = np.arange(128)
    c, s = cs(p[:, None] * p[None, :], 64, sign)
    w = cplx(c, s).transpose(0, 2, 1, 3)
    if stream:
        a = w.reshape(128, 128)
        signed = np.where(p >= 32, p - 64, p) * 128.0
        b = (w * signed).reshape(128, 128)
        g = np.concatenate([a, b])
    else:
        g = w[:, :, 0, :].reshape(128, 64)
    tc, ts = cs(p[:, None] * q[None, :], 8192, sign)
    c, s = cs(q[:, None] * q[None, :], 128, sign)
    w2 = cplx(c, s).transpose(2, 0, 1, 3).reshape(256, 256)
    return bf(g), np.float32(tc), np.float32(ts), bf(w2)


def recv_tables(sign, stream):
    k = np.arange(128)
    r = np.arange(64)
    c, s = cs(k[:, None] * k[None, :], 128, sign)
    w1 = cplx(c, s).transpose(0, 2, 3, 1).reshape(256, 256)
    tc, ts = cs(k[:, None] * r[None, :], 8192, sign)
    tc = np.concatenate([tc, tc], 1)
    ts = np.concatenate([ts, ts], 1)
    c, s = cs(r[:, None] * r[None, :], 64, sign)
    w = cplx(c, s)
    v = np.zeros((2, 2, 64, 2, 2, 64))
    for e in range(2):
        v[:, e, :, :, e, :] = w.transpose(0, 2, 1, 3)
    if stream:
        v = v[0].reshape(128, 256)
    else:
        v = v.reshape(256, 256) / 8192.0
    return bf(w1), np.float32(tc), np.float32(ts), bf(v)


def stream_send_kernel(wa_ref, s_ref, g_ref, tc_ref, ts_ref, w2_ref, o_ref, xs, tre, tim, of):
    def load(p, carry):
        at = pl.multiple_of(p * 128, 128)
        for c in range(2):
            row = pl.multiple_of((c * 64 + p) * PAD, 8)
            xs[pl.ds(row, 64), :] = s_ref[c, :, pl.ds(at, 128)].astype(F32)
        return carry

    lax.fori_loop(0, 64, load, 0, unroll=4)
    q = lax.broadcasted_iota(jnp.int32, (64, 128), 1).astype(F32)

    def rows(n, carry):
        x = jnp.concatenate([xs[pl.ds(2 * n + h, 128, stride=PAD), :].astype(BF) for h in range(2)], axis=1)
        both = jnp.dot(g_ref[...], x, preferred_element_type=F32)
        tc = tc_ref[...]
        ts = ts_ref[...]
        for h in range(2):
            r = 2 * n + h
            z = both[:, h * 128 : h * 128 + 128]
            are, aim, bre, bim = z[:64], z[64:128], z[128:192], z[192:]
            ure = bre + q * are
            uim = bim + q * aim
            wa = wa_ref[0, r]
            base = pl.multiple_of(r * PAD2, 8)
            vre = are * tc - aim * ts
            vim = are * ts + aim * tc
            tre[pl.ds(base, 64), :] = ure * ts + uim * tc
            tim[pl.ds(base, 64), :] = uim * ts - ure * tc
            tre[pl.ds(base + 64, 64), :] = -wa * vim
            tim[pl.ds(base + 64, 64), :] = wa * vre
        return carry

    lax.fori_loop(0, 32, rows, 0, unroll=2)

    def cols(n, carry):
        parts = []
        for h in range(2):
            for f in range(2):
                at = pl.ds(f * 64 + 2 * n + h, 64, stride=PAD2)
                parts.append(jnp.concatenate([tre[at, :].astype(BF), tim[at, :].astype(BF)], axis=1))
        m = jnp.concatenate(parts, axis=0)
        out = lax.dot_general(w2_ref[...], m, NT, preferred_element_type=F32)
        for h in range(2):
            of[pl.ds(2 * n + h, 256, stride=PAD), :] = out[:, h * 128 : h * 128 + 128]
        return carry

    lax.fori_loop(0, 32, cols, 0, unroll=2)

    def store(i, carry):
        o_ref[i] = of[pl.ds(pl.multiple_of(i * PAD, 8), 64), :].astype(BF)
        return carry

    lax.fori_loop(0, 256, store, 0, unroll=8)


VM = pl.BlockSpec(memory_space=pltpu.VMEM)
SM = pl.BlockSpec(memory_space=pltpu.SMEM)


def call(kernel, outs, specs, scratch, cost, name, *args):
    return pl.pallas_call(
        kernel,
        out_shape=outs,
        in_specs=specs,
        out_specs=jax.tree.map(lambda _: VM, outs),
        scratch_shapes=scratch,
        compiler_params=pltpu.CompilerParams(vmem_limit_bytes=VLIM),
        cost_estimate=pl.CostEstimate(flops=cost, bytes_accessed=1 << 20, transcendentals=0),
        name=name,
    )(*args)


def stream_send(stream, wa):
    return call(
        stream_send_kernel,
        jax.ShapeDtypeStruct((256, 64, 128), BF),
        [SM] + [VM] * 5,
        [pltpu.VMEM((128 * PAD, 128), F32)] + [pltpu.VMEM((64 * PAD2, 128), F32)] * 2
        + [pltpu.VMEM((256 * PAD, 128), F32)],
        int(6e9), "stream_send",
        wa, stream, *send_tables(1.0, True),
    )


def stream_recv_kernel(x_ref, w1_ref, tc_ref, ts_ref, v_ref, o_ref, xf, of):
    def load(i, carry):
        xf[pl.ds(pl.multiple_of(i * PAD, 8), 64), :] = x_ref[i].astype(F32)
        return carry

    lax.fori_loop(0, 256, load, 0, unroll=8)

    def step(n, carry):
        d = jnp.concatenate([xf[pl.ds(2 * n + h, 256, stride=PAD), :].astype(BF) for h in range(2)], axis=1)
        z = jnp.dot(w1_ref[...], d, preferred_element_type=F32)
        tc = tc_ref[...]
        ts = ts_ref[...]
        parts = []
        for h in range(2):
            re = z[:128, h * 128 : h * 128 + 128]
            im = z[128:, h * 128 : h * 128 + 128]
            parts.append(
                jnp.concatenate([(re * tc - im * ts).astype(BF), (re * ts + im * tc).astype(BF)], axis=1)
            )
        m = jnp.concatenate(parts, axis=0)
        out = lax.dot_general(v_ref[...], m, NT, preferred_element_type=F32)
        for h in range(2):
            for f in range(2):
                of[pl.ds(4 * n + 2 * h + f, 64, stride=PAD2), :] = out[f * 64 : f * 64 + 64, h * 128 : h * 128 + 128]
        return carry

    lax.fori_loop(0, 32, step, 0, unroll=2)

    def store(i, carry):
        o_ref[i] = of[pl.ds(pl.multiple_of(i * PAD2, 8), 128), :].astype(BF)
        return carry

    lax.fori_loop(0, 64, store, 0, unroll=4)


def stream_recv(x):
    return call(
        stream_recv_kernel,
        jax.ShapeDtypeStruct((64, 128, 128), BF),
        [VM] * 5,
        [pltpu.VMEM((256 * PAD, 128), F32), pltpu.VMEM((64 * PAD2, 128), F32)],
        int(6e9), "stream_recv",
        x, *recv_tables(1.0, True),
    )


def dye_send_kernel(idx_ref, dye_ref, ret_ref, g_ref, tc_ref, ts_ref, w2_ref, o_ref, xs, tre, tim, of):
    def load(p, carry):
        at = pl.multiple_of(p * 128, 128)
        xs[pl.ds(pl.multiple_of(p * PAD, 8), 64), :] = dye_ref[:, pl.ds(at, 128)].astype(F32)
        return carry

    lax.fori_loop(0, 64, load, 0, unroll=4)

    def place(n, carry):
        tile = idx_ref[0, n]

        @pl.when(tile >= 0)
        def _():
            g = n // 2
            e = n % 2
            total = ret_ref[g * 8 + e].astype(F32)
            for x in range(1, 4):
                total = total + ret_ref[g * 8 + 2 * x + e].astype(F32)
            at = pl.ds(pl.multiple_of(tile * PAD, 8), 64)
            xs[at, :] = xs[at, :] + total

        return carry

    lax.fori_loop(0, 32, place, 0)

    def rows(n, carry):
        x = jnp.concatenate([xs[pl.ds(4 * n + h, 64, stride=PAD), :].astype(BF) for h in range(4)], axis=1)
        z = jnp.dot(g_ref[...], x, preferred_element_type=F32)
        tc = tc_ref[...]
        ts = ts_ref[...]
        for h in range(4):
            re = z[:64, h * 128 : h * 128 + 128]
            im = z[64:, h * 128 : h * 128 + 128]
            base = pl.multiple_of((4 * n + h) * PAD, 8)
            tre[pl.ds(base, 64), :] = re * tc - im * ts
            tim[pl.ds(base, 64), :] = re * ts + im * tc
        return carry

    lax.fori_loop(0, 16, rows, 0, unroll=2)

    def cols(n, carry):
        parts = []
        for e in range(4):
            at = pl.ds(4 * n + e, 64, stride=PAD)
            parts.append(jnp.concatenate([tre[at, :].astype(BF), tim[at, :].astype(BF)], axis=1))
        m = jnp.concatenate(parts, axis=0)
        out = lax.dot_general(w2_ref[...], m, NT, preferred_element_type=F32)
        for h in range(2):
            of[pl.ds(2 * n + h, 256, stride=PAD3), :] = out[:, h * 128 : h * 128 + 128]
        return carry

    lax.fori_loop(0, 16, cols, 0, unroll=2)

    def store(i, carry):
        o_ref[i] = of[pl.ds(pl.multiple_of(i * PAD3, 8), 32), :].astype(BF)
        return carry

    lax.fori_loop(0, 256, store, 0, unroll=8)


def dye_send(idx, dye, ret):
    return call(
        dye_send_kernel,
        jax.ShapeDtypeStruct((256, 32, 128), BF),
        [SM] + [VM] * 6,
        [pltpu.VMEM((64 * PAD, 128), F32)] * 3 + [pltpu.VMEM((256 * PAD3, 128), F32)],
        int(4e9), "dye_send",
        idx, dye, ret, *send_tables(-1.0, False),
    )


def dye_recv_kernel(x_ref, w1_ref, tc_ref, ts_ref, v_ref, o_ref, xf, of):
    def load(i, carry):
        xf[pl.ds(pl.multiple_of(i * PAD3, 8), 32), :] = x_ref[i].astype(F32)
        return carry

    lax.fori_loop(0, 256, load, 0, unroll=8)

    def step(n, carry):
        d = jnp.concatenate([xf[pl.ds(2 * n + h, 256, stride=PAD3), :].astype(BF) for h in range(2)], axis=1)
        z = jnp.dot(w1_ref[...], d, preferred_element_type=F32)
        tc = tc_ref[...]
        ts = ts_ref[...]
        parts = []
        for h in range(2):
            re = z[:128, h * 128 : h * 128 + 128]
            im = z[128:, h * 128 : h * 128 + 128]
            parts.append(
                jnp.concatenate([(re * tc - im * ts).astype(BF), (re * ts + im * tc).astype(BF)], axis=1)
            )
        m = jnp.concatenate(parts, axis=0)
        out = lax.dot_general(v_ref[...], m, NT, preferred_element_type=F32)
        for h in range(2):
            for c in range(2):
                for e in range(2):
                    row = c * 4096 + (n // 2) * 512 + (4 * n + 2 * h + e) % 8
                    of[pl.ds(row, 64, stride=8), :] = out[
                        (2 * c + e) * 64 : (2 * c + e) * 64 + 64, h * 128 : h * 128 + 128
                    ]
        return carry

    lax.fori_loop(0, 16, step, 0, unroll=2)

    def store(n, carry):
        c = n // 8
        t8 = n % 8
        base = pl.multiple_of(n * 512, 512)
        at = pl.ds(pl.multiple_of(t8 * 8, 8), 8)
        for j in range(64):
            o_ref[c, at, j * 128 : j * 128 + 128] = of[pl.ds(base + j * 8, 8), :]
        return carry

    lax.fori_loop(0, 16, store, 0)


def dye_recv(x):
    return call(
        dye_recv_kernel,
        jax.ShapeDtypeStruct((2, 64, 8192), F32),
        [VM] * 5,
        [pltpu.VMEM((256 * PAD3, 128), F32), pltpu.VMEM((8192, 128), F32)],
        int(4e9), "dye_recv",
        x, *recv_tables(-1.0, False),
    )

CAPO = 2


def deposit_kernel(mb_ref, nb_ref, fy_ref, fx_ref, am_ref, keep_ref, send_ref, m_ref, acc):
    step = pl.program_id(0)
    width = mb_ref.shape[1]
    am = am_ref[...]
    hi = am * fy_ref[...]
    lo = am - hi
    mb = mb_ref[...]
    nb = nb_ref[...]
    fx = fx_ref[...]
    gx = 1.0 - fx

    def build_m(i, carry):
        at = pl.multiple_of(i * 64, 64)
        d = lax.broadcasted_iota(jnp.int32, (64, width), 0) + (i * 64 - mb)
        w = jnp.where(d == 0, lo, jnp.where(d == 1, hi, 0.0))
        m_ref[pl.ds(at, 64), :] = w.astype(BF)
        return carry

    lax.fori_loop(0, 16, build_m, 0)

    def part(i, first):
        d = lax.broadcasted_iota(jnp.int32, (256, width), 0) + (i * 256 - nb)
        w = jnp.where(d == 0, gx, jnp.where(d == 1, fx, 0.0)).astype(BF)
        z = lax.dot_general(m_ref[...], w, NT, preferred_element_type=F32)
        acc[i] = z if first else acc[i] + z

    @pl.when(step == 0)
    def _():
        lax.fori_loop(0, 8, lambda i, c: (part(i, True), c)[1], 0, unroll=2)

    @pl.when(step > 0)
    def _():
        lax.fori_loop(0, 8, lambda i, c: (part(i, False), c)[1], 0, unroll=2)

    @pl.when(step == pl.num_programs(0) - 1)
    def _():
        def store(p, carry):
            row = pl.multiple_of((p // 8) * 64, 64)
            for h in range(2):
                lanes = slice(h * 128, h * 128 + 128)
                at = p // 8 * 16 + p % 8 * 2 + h
                keep_ref[at] = acc[p % 8, pl.ds(row, 64), lanes].astype(BF)
                send_ref[at] = acc[p % 8, pl.ds(row + 512, 64), lanes].astype(BF)
            return carry

        lax.fori_loop(0, 64, store, 0, unroll=4)


def deposit(mb, nb, fy, fx, am, width=2048):
    blk = pl.BlockSpec((1, width), lambda i: (0, i))
    return pl.pallas_call(
        deposit_kernel,
        grid=(8192 // width,),
        out_shape=[jax.ShapeDtypeStruct((128, 64, 128), BF)] * 2,
        in_specs=[blk] * 5,
        out_specs=[pl.BlockSpec((128, 64, 128), lambda i: (0, 0, 0))] * 2,
        scratch_shapes=[pltpu.VMEM((1024, width), BF), pltpu.VMEM((8, 1024, 256), F32)],
        compiler_params=pltpu.CompilerParams(vmem_limit_bytes=VLIM),
        cost_estimate=pl.CostEstimate(flops=int(34e9), bytes_accessed=4 << 20, transcendentals=0),
        name="deposit",
    )(mb, nb, fy, fx, am)


def gather_kernel(base_ref, a_ref, b_ref, col_ref, fy_ref, fx_ref, o_ref, st, g):
    def load(i, carry):
        at = pl.multiple_of(i * 128, 128)
        st[pl.ds(at, 128), :] = a_ref[i].astype(F32)
        st[pl.ds(at + 16384, 128), :] = b_ref[i].astype(F32)
        return carry

    lax.fori_loop(0, 128, load, 0, unroll=2)
    sub = lax.broadcasted_iota(jnp.int32, (8, 128), 0)
    off = lax.broadcasted_iota(jnp.int32, (8, 128), 1) - sub // 4
    upper = sub % 4 >= 2
    odd = sub % 2 == 1
    xs = lax.broadcasted_iota(jnp.int32, (128, 128), 0)

    def chunk(n, carry):
        for f in range(128):
            g[f * 4 : f * 4 + 4, :] = st[pl.ds(base_ref[n, f], 4), :]
        at = pl.ds(pl.multiple_of(n * 128, 128), 128)
        col = col_ref[:, at]
        fy = fy_ref[:, at]
        fx = fx_ref[:, at]
        d = xs - col
        w = jnp.where(d == 0, 1.0 - fx, jnp.where(d == 1, fx, 0.0))
        hi = w.astype(BF)
        lo = (w - hi.astype(F32)).astype(BF)
        rows = g[...].astype(BF)
        z = jnp.dot(rows, hi, preferred_element_type=F32) + jnp.dot(rows, lo, preferred_element_type=F32)
        total = jnp.zeros((8, 128), F32)
        for i in range(64):
            total = total + jnp.where(off == 2 * i, z[8 * i : 8 * i + 8], 0.0)
        total = total * jnp.where(upper, fy, 1.0 - fy)
        o_ref[0:1, at] = jnp.sum(jnp.where(odd, 0.0, total), axis=0, keepdims=True)
        o_ref[1:2, at] = jnp.sum(jnp.where(odd, total, 0.0), axis=0, keepdims=True)
        return carry

    lax.fori_loop(0, 64, chunk, 0)


def gather(base, a, b, col, fy, fx):
    return call(
        gather_kernel,
        jax.ShapeDtypeStruct((2, 8192), F32),
        [SM] + [VM] * 5,
        [pltpu.VMEM((32768, 128), F32), pltpu.VMEM((512, 128), F32)],
        int(2e10), "gather",
        base, a, b, col, fy, fx,
    )


AXES = ("wide", "narrow")


def spread(blocks):
    return lax.all_to_all(blocks, AXES, split_axis=0, concat_axis=0, tiled=True)


def swap_cores(x):
    n = lax.axis_size("narrow")
    return lax.ppermute(x, "narrow", [(i, i ^ 1) for i in range(n)])


def shards(stream_hat, dye, float_slot, float_row, float_col, float_frac, float_dye, tile_lists):
    device = lax.axis_index(AXES)
    group = lax.axis_index("wide")
    core = lax.axis_index("narrow") % 2
    wave = device * 64 + jnp.arange(64)
    wave = jnp.where(wave >= 4096, wave - 8192, wave).astype(F32)[None]
    slot = float_slot.reshape(64, 128)
    row = float_row.reshape(64, 128)
    col = float_col.reshape(64, 128)

    mine = (tile_lists >= 0) & (tile_lists // 64 == device)
    place = jnp.cumsum(mine.astype(jnp.int32), axis=1) - 1
    local = tile_lists % 64 + 1
    send_index = jnp.stack(
        [jnp.sum(jnp.where(mine & (place == e), local, 0), axis=1) for e in range(CAPO)], axis=1
    ) - 1

    own_list = lax.dynamic_index_in_dim(tile_lists, group, 0, keepdims=False)
    holder = own_list // 64
    before = jnp.arange(256)[:, None] > jnp.arange(256)[None, :]
    rank = jnp.sum((before & (holder[:, None] == holder[None, :])).astype(jnp.int32), axis=1)
    position = jnp.where(own_list >= 0, jnp.where(rank == core, 0, 128) + holder, 0)
    pos = jnp.sum(
        jnp.where(jnp.arange(256)[:, None, None] == slot[None], position[:, None, None], 0), axis=0
    )

    flat = lambda x: x.reshape(1, 8192)
    fy = float_frac[0:1]
    fx = float_frac[1:2]
    rows = flat(pos // 16 * 64 + row)
    cols = flat(pos % 16 * 128 + col)

    spec = stream_send(stream_hat, wave)
    spec, rows, cols = lax.optimization_barrier((spec, rows, cols))
    spec = spread(spec.reshape(128, 2, 64, 128)).reshape(256, 64, 128)
    keep, send = deposit(rows, cols, fy, fx, flat(float_dye))
    dep = (keep.astype(F32) + swap_cores(send).astype(F32)).astype(BF)
    spec, dep = lax.optimization_barrier((spec, dep))
    returned = spread(dep)

    tiles = stream_recv(spec)
    outgoing = tiles[jnp.maximum(send_index, 0)]
    outgoing = jnp.broadcast_to(outgoing[:, None], (16, 4, 2, 128, 128)).reshape(128, 128, 128)
    outgoing, returned = lax.optimization_barrier((outgoing, returned))
    own = spread(outgoing)
    front = dye_send(send_index.reshape(1, 32), dye, returned)
    own, front = lax.optimization_barrier((own, front))
    other = swap_cores(own)
    front = spread(front.reshape(128, 2, 32, 128)).reshape(256, 32, 128)
    velocity = gather(pos * 128 + 2 * row, own, other, flat(float_col), fy, fx)
    velocity, front = lax.optimization_barrier((velocity, front))
    dye_hat = dye_recv(front)
    return (velocity, dye_hat)


def solution(mesh):
    return jax.shard_map(
        shards,
        mesh=mesh,
        in_specs=(
            P(None, AXES, None),
            P(AXES, None),
            P(AXES),
            P(AXES),
            P(AXES),
            P(None, AXES),
            P(AXES),
            P(),
        ),
        out_specs=(P(None, AXES), P(None, AXES, None)),
        check_vma=False,
    )
```

```python
import numpy as np, math

import jax, jax.numpy as jnp
from jax import lax
from jax.sharding import PartitionSpec as P
from jax.experimental import pallas as pl
from jax.experimental.pallas import tpu as pltpu

BF = jnp.bfloat16
F32 = jnp.float32
NT = (((1,), (1,)), ((), ()))
PAD = 72
PAD2 = 136
PAD3 = 40


def cs(num, den, sign):
    ang = sign * 2.0 * math.pi * (num % den) / den
    return np.cos(ang), np.sin(ang)


def cplx(c, s):
    return np.stack([np.stack([c, -s]), np.stack([s, c])])


def bf(x):
    return np.asarray(x, np.float32).astype(jnp.bfloat16)


def send_tables(sign, stream):
    p = np.arange(64)
    q = np.arange(128)
    c, s = cs(p[:, None] * p[None, :], 64, sign)
    w = cplx(c, s).transpose(0, 2, 1, 3)
    if stream:
        a = w.reshape(128, 128)
        signed = np.where(p >= 32, p - 64, p) * 128.0
        b = (w * signed).reshape(128, 128)
        g = np.concatenate([a, b])
    else:
        g = w[:, :, 0, :].reshape(128, 64)
    tc, ts = cs(p[:, None] * q[None, :], 8192, sign)
    c, s = cs(q[:, None] * q[None, :], 128, sign)
    w2 = cplx(c, s).transpose(2, 0, 1, 3).reshape(256, 256)
    return bf(g), np.float32(tc), np.float32(ts), bf(w2)


def recv_tables(sign, stream):
    k = np.arange(128)
    r = np.arange(64)
    c, s = cs(k[:, None] * k[None, :], 128, sign)
    w1 = cplx(c, s).transpose(0, 2, 3, 1).reshape(256, 256)
    tc, ts = cs(k[:, None] * r[None, :], 8192, sign)
    tc = np.concatenate([tc, tc], 1)
    ts = np.concatenate([ts, ts], 1)
    c, s = cs(r[:, None] * r[None, :], 64, sign)
    w = cplx(c, s)
    v = np.zeros((2, 2, 64, 2, 2, 64))
    for e in range(2):
        v[:, e, :, :, e, :] = w.transpose(0, 2, 1, 3)
    if stream:
        v = v[0].reshape(128, 256)
    else:
        v = v.reshape(256, 256) / 8192.0
    return bf(w1), np.float32(tc), np.float32(ts), bf(v)


def stream_send_kernel(wa_ref, s_ref, g_ref, tc_ref, ts_ref, w2_ref, o_ref, xs, tre, tim, of):
    def load(p, carry):
        at = pl.multiple_of(p * 128, 128)
        for c in range(2):
            row = pl.multiple_of((c * 64 + p) * PAD, 8)
            xs[pl.ds(row, 64), :] = s_ref[c, :, pl.ds(at, 128)].astype(F32)
        return carry

    lax.fori_loop(0, 64, load, 0, unroll=4)
    q = lax.broadcasted_iota(jnp.int32, (64, 128), 1).astype(F32)

    def rows(n, carry):
        x = jnp.concatenate([xs[pl.ds(2 * n + h, 128, stride=PAD), :].astype(BF) for h in range(2)], axis=1)
        both = jnp.dot(g_ref[...], x, preferred_element_type=F32)
        tc = tc_ref[...]
        ts = ts_ref[...]
        for h in range(2):
            r = 2 * n + h
            z = both[:, h * 128 : h * 128 + 128]
            are, aim, bre, bim = z[:64], z[64:128], z[128:192], z[192:]
            ure = bre + q * are
            uim = bim + q * aim
            wa = wa_ref[0, r]
            base = pl.multiple_of(r * PAD2, 8)
            vre = are * tc - aim * ts
            vim = are * ts + aim * tc
            tre[pl.ds(base, 64), :] = ure * ts + uim * tc
            tim[pl.ds(base, 64), :] = uim * ts - ure * tc
            tre[pl.ds(base + 64, 64), :] = -wa * vim
            tim[pl.ds(base + 64, 64), :] = wa * vre
        return carry

    lax.fori_loop(0, 32, rows, 0, unroll=2)

    def cols(n, carry):
        parts = []
        for h in range(2):
            for f in range(2):
                at = pl.ds(f * 64 + 2 * n + h, 64, stride=PAD2)
                parts.append(jnp.concatenate([tre[at, :].astype(BF), tim[at, :].astype(BF)], axis=1))
        m = jnp.concatenate(parts, axis=0)
        out = lax.dot_general(w2_ref[...], m, NT, preferred_element_type=F32)
        for h in range(2):
            of[pl.ds(2 * n + h, 256, stride=PAD), :] = out[:, h * 128 : h * 128 + 128]
        return carry

    lax.fori_loop(0, 32, cols, 0, unroll=2)

    def store(i, carry):
        o_ref[i] = of[pl.ds(pl.multiple_of(i * PAD, 8), 64), :].astype(BF)
        return carry

    lax.fori_loop(0, 256, store, 0, unroll=8)


VM = pl.BlockSpec(memory_space=pltpu.VMEM)
SM = pl.BlockSpec(memory_space=pltpu.SMEM)


def call(kernel, outs, specs, scratch, cost, mib, name, *args):
    return pl.pallas_call(
        kernel,
        out_shape=outs,
        in_specs=specs,
        out_specs=jax.tree.map(lambda _: VM, outs),
        scratch_shapes=scratch,
        compiler_params=pltpu.CompilerParams(vmem_limit_bytes=mib << 20),
        cost_estimate=pl.CostEstimate(flops=cost, bytes_accessed=1 << 20, transcendentals=0),
        name=name,
    )(*args)


def stream_send(stream, wa):
    return call(
        stream_send_kernel,
        jax.ShapeDtypeStruct((256, 64, 128), BF),
        [SM] + [VM] * 5,
        [pltpu.VMEM((128 * PAD, 128), F32)] + [pltpu.VMEM((64 * PAD2, 128), F32)] * 2
        + [pltpu.VMEM((256 * PAD, 128), F32)],
        int(6e9), 36, "stream_send",
        wa, stream, *send_tables(1.0, True),
    )


def stream_recv_kernel(idx_ref, x_ref, w1_ref, tc_ref, ts_ref, v_ref, o_ref, xf, of):
    def load(i, carry):
        xf[pl.ds(pl.multiple_of(i * PAD, 8), 64), :] = x_ref[i].astype(F32)
        return carry

    lax.fori_loop(0, 256, load, 0, unroll=8)

    def step(n, carry):
        d = jnp.concatenate([xf[pl.ds(2 * n + h, 256, stride=PAD), :].astype(BF) for h in range(2)], axis=1)
        z = jnp.dot(w1_ref[...], d, preferred_element_type=F32)
        tc = tc_ref[...]
        ts = ts_ref[...]
        parts = []
        for h in range(2):
            re = z[:128, h * 128 : h * 128 + 128]
            im = z[128:, h * 128 : h * 128 + 128]
            parts.append(
                jnp.concatenate([(re * tc - im * ts).astype(BF), (re * ts + im * tc).astype(BF)], axis=1)
            )
        m = jnp.concatenate(parts, axis=0)
        out = lax.dot_general(v_ref[...], m, NT, preferred_element_type=F32)
        for h in range(2):
            for f in range(2):
                of[pl.ds(4 * n + 2 * h + f, 64, stride=PAD2), :] = out[f * 64 : f * 64 + 64, h * 128 : h * 128 + 128]
        return carry

    lax.fori_loop(0, 32, step, 0, unroll=2)

    def store(n, carry):
        tile = jnp.maximum(idx_ref[0, n], 0)
        data = of[pl.ds(pl.multiple_of(tile * PAD2, 8), 128), :].astype(BF)
        for x in range(4):
            o_ref[n // 2 * 8 + 2 * x + n % 2] = data
        return carry

    lax.fori_loop(0, 32, store, 0, unroll=2)


def stream_recv(idx, x):
    return call(
        stream_recv_kernel,
        jax.ShapeDtypeStruct((128, 128, 128), BF),
        [SM] + [VM] * 5,
        [pltpu.VMEM((256 * PAD, 128), F32), pltpu.VMEM((64 * PAD2, 128), F32)],
        int(6e9), 28, "stream_recv",
        idx, x, *recv_tables(1.0, True),
    )


def dye_send_kernel(idx_ref, dye_ref, ret_ref, g_ref, tc_ref, ts_ref, w2_ref, o_ref, xs, tre, tim, of):
    def load(p, carry):
        at = pl.multiple_of(p * 128, 128)
        xs[pl.ds(pl.multiple_of(p * PAD, 8), 64), :] = dye_ref[:, pl.ds(at, 128)].astype(F32)
        return carry

    lax.fori_loop(0, 64, load, 0, unroll=4)

    def place(n, carry):
        tile = idx_ref[0, n]

        @pl.when(tile >= 0)
        def _():
            g = n // 2
            e = n % 2
            total = ret_ref[g * 8 + e].astype(F32)
            for x in range(1, 4):
                total = total + ret_ref[g * 8 + 2 * x + e].astype(F32)
            at = pl.ds(pl.multiple_of(tile * PAD, 8), 64)
            xs[at, :] = xs[at, :] + total

        return carry

    lax.fori_loop(0, 32, place, 0)

    def rows(n, carry):
        x = jnp.concatenate([xs[pl.ds(4 * n + h, 64, stride=PAD), :].astype(BF) for h in range(4)], axis=1)
        z = jnp.dot(g_ref[...], x, preferred_element_type=F32)
        tc = tc_ref[...]
        ts = ts_ref[...]
        for h in range(4):
            re = z[:64, h * 128 : h * 128 + 128]
            im = z[64:, h * 128 : h * 128 + 128]
            base = pl.multiple_of((4 * n + h) * PAD, 8)
            tre[pl.ds(base, 64), :] = re * tc - im * ts
            tim[pl.ds(base, 64), :] = re * ts + im * tc
        return carry

    lax.fori_loop(0, 16, rows, 0, unroll=2)

    def cols(n, carry):
        parts = []
        for e in range(4):
            at = pl.ds(4 * n + e, 64, stride=PAD)
            parts.append(jnp.concatenate([tre[at, :].astype(BF), tim[at, :].astype(BF)], axis=1))
        m = jnp.concatenate(parts, axis=0)
        out = lax.dot_general(w2_ref[...], m, NT, preferred_element_type=F32)
        for h in range(2):
            of[pl.ds(2 * n + h, 256, stride=PAD3), :] = out[:, h * 128 : h * 128 + 128]
        return carry

    lax.fori_loop(0, 16, cols, 0, unroll=2)

    def store(i, carry):
        o_ref[i] = of[pl.ds(pl.multiple_of(i * PAD3, 8), 32), :].astype(BF)
        return carry

    lax.fori_loop(0, 256, store, 0, unroll=8)


def dye_send(idx, dye, ret):
    return call(
        dye_send_kernel,
        jax.ShapeDtypeStruct((256, 32, 128), BF),
        [SM] + [VM] * 6,
        [pltpu.VMEM((64 * PAD, 128), F32)] * 3 + [pltpu.VMEM((256 * PAD3, 128), F32)],
        int(4e9), 24, "dye_send",
        idx, dye, ret, *send_tables(-1.0, False),
    )


def dye_recv_kernel(x_ref, w1_ref, tc_ref, ts_ref, v_ref, o_ref, xf, of):
    def load(i, carry):
        xf[pl.ds(pl.multiple_of(i * PAD3, 8), 32), :] = x_ref[i].astype(F32)
        return carry

    lax.fori_loop(0, 256, load, 0, unroll=8)

    def step(n, carry):
        d = jnp.concatenate([xf[pl.ds(2 * n + h, 256, stride=PAD3), :].astype(BF) for h in range(2)], axis=1)
        z = jnp.dot(w1_ref[...], d, preferred_element_type=F32)
        tc = tc_ref[...]
        ts = ts_ref[...]
        parts = []
        for h in range(2):
            re = z[:128, h * 128 : h * 128 + 128]
            im = z[128:, h * 128 : h * 128 + 128]
            parts.append(
                jnp.concatenate([(re * tc - im * ts).astype(BF), (re * ts + im * tc).astype(BF)], axis=1)
            )
        m = jnp.concatenate(parts, axis=0)
        out = lax.dot_general(v_ref[...], m, NT, preferred_element_type=F32)
        for h in range(2):
            for c in range(2):
                for e in range(2):
                    row = c * 4096 + (n // 2) * 512 + (4 * n + 2 * h + e) % 8
                    of[pl.ds(row, 64, stride=8), :] = out[
                        (2 * c + e) * 64 : (2 * c + e) * 64 + 64, h * 128 : h * 128 + 128
                    ]
        return carry

    lax.fori_loop(0, 16, step, 0, unroll=2)

    def store(n, carry):
        c = n // 8
        t8 = n % 8
        base = pl.multiple_of(n * 512, 512)
        at = pl.ds(pl.multiple_of(t8 * 8, 8), 8)
        for j in range(64):
            o_ref[c, at, j * 128 : j * 128 + 128] = of[pl.ds(base + j * 8, 8), :]
        return carry

    lax.fori_loop(0, 16, store, 0)


def dye_recv(x):
    return call(
        dye_recv_kernel,
        jax.ShapeDtypeStruct((2, 64, 8192), F32),
        [VM] * 5,
        [pltpu.VMEM((256 * PAD3, 128), F32), pltpu.VMEM((8192, 128), F32)],
        int(4e9), 20, "dye_recv",
        x, *recv_tables(-1.0, False),
    )

CAPO = 2


def deposit_kernel(idx_ref, col_ref, fy_ref, fx_ref, am_ref, keep_ref, send_ref, wa, wb, *accs):
    ways = len(accs)

    def clear(i, carry):
        for acc in accs:
            acc[pl.ds(pl.multiple_of(i * 64, 64), 64), :] = jnp.zeros((64, 128), F32)
        return carry

    lax.fori_loop(0, 256, clear, 0, unroll=2)

    def weights(n, dst):
        xs = lax.broadcasted_iota(jnp.int32, (128, 128), 0)
        rows = lax.broadcasted_iota(jnp.int32, (256, 128), 0)
        off = rows // 2 - lax.broadcasted_iota(jnp.int32, (256, 128), 1)
        odd = rows % 2 == 1
        at = pl.ds(pl.multiple_of(n * 128, 128), 128)
        fx = fx_ref[:, at]
        am = am_ref[:, at]
        hi = am * fy_ref[:, at]
        lo = am - hi
        d = xs - col_ref[:, at]
        w = jnp.where(d == 0, 1.0 - fx, jnp.where(d == 1, fx, 0.0)).astype(BF)
        e = jnp.where(off == 0, jnp.where(odd, hi, lo), 0.0).astype(BF)
        dst[...] = lax.dot_general(e, w, NT, preferred_element_type=F32)

    def add(n, src):
        for f in range(0, 128, ways):
            at = [pl.ds(idx_ref[n, f + k], 2) for k in range(ways)]
            new = [accs[k][at[k], :] + src[2 * (f + k) : 2 * (f + k) + 2, :] for k in range(ways)]
            for k in range(ways):
                accs[k][at[k], :] = new[k]

    weights(0, wa)

    def chunk(n, carry):
        weights(2 * n + 1, wb)
        add(2 * n, wa)
        weights(jnp.minimum(2 * n + 2, 63), wa)
        add(2 * n + 1, wb)
        return carry

    lax.fori_loop(0, 32, chunk, 0)

    def store(i, carry):
        for ref, base in ((keep_ref, 0), (send_ref, 8192)):
            at = pl.ds(pl.multiple_of(i * 64 + base, 64), 64)
            total = accs[0][at, :]
            for acc in accs[1:]:
                total = total + acc[at, :]
            ref[i] = total.astype(BF)
        return carry

    lax.fori_loop(0, 128, store, 0, unroll=2)


def deposit(idx, col, fy, fx, am):
    return call(
        deposit_kernel,
        [jax.ShapeDtypeStruct((128, 64, 128), BF)] * 2,
        [SM] + [VM] * 4,
        [pltpu.VMEM((256, 128), F32)] * 2 + [pltpu.VMEM((16384, 128), F32)] * 4,
        int(1.2e10), 44, "deposit",
        idx, col, fy, fx, am,
    )


def gather_kernel(base_ref, a_ref, b_ref, col_ref, fy_ref, fx_ref, o_ref, st, ga, gb):
    def load(i, carry):
        at = pl.multiple_of(i * 128, 128)
        st[pl.ds(at, 128), :] = a_ref[i].astype(F32)
        st[pl.ds(at + 16384, 128), :] = b_ref[i].astype(F32)
        return carry

    lax.fori_loop(0, 128, load, 0, unroll=4)

    def fetch(n, g):
        for f in range(128):
            g[f * 4 : f * 4 + 4, :] = st[pl.ds(base_ref[n, f], 4), :]

    def mix(n, g):
        sub = lax.broadcasted_iota(jnp.int32, (8, 128), 0)
        off = lax.broadcasted_iota(jnp.int32, (8, 128), 1) - sub // 4
        upper = sub % 4 >= 2
        odd = sub % 2 == 1
        xs = lax.broadcasted_iota(jnp.int32, (128, 128), 0)
        at = pl.ds(pl.multiple_of(n * 128, 128), 128)
        col = col_ref[:, at]
        fy = fy_ref[:, at]
        fx = fx_ref[:, at]
        d = xs - col
        w = jnp.where(d == 0, 1.0 - fx, jnp.where(d == 1, fx, 0.0))
        hi = w.astype(BF)
        lo = (w - hi.astype(F32)).astype(BF)
        z = jnp.dot(g[...].astype(BF), jnp.concatenate([hi, lo], axis=1), preferred_element_type=F32)
        parts = [jnp.zeros((8, 128), F32) for _ in range(4)]
        for i in range(64):
            keep = off == 2 * i
            for h in range(2):
                k = 2 * h + i % 2
                parts[k] = parts[k] + jnp.where(keep, z[8 * i : 8 * i + 8, h * 128 : h * 128 + 128], 0.0)
        total = (parts[0] + parts[1] + (parts[2] + parts[3])) * jnp.where(upper, fy, 1.0 - fy)
        o_ref[0:1, at] = jnp.sum(jnp.where(odd, 0.0, total), axis=0, keepdims=True)
        o_ref[1:2, at] = jnp.sum(jnp.where(odd, total, 0.0), axis=0, keepdims=True)

    fetch(0, ga)

    def chunk(n, carry):
        fetch(2 * n + 1, gb)
        mix(2 * n, ga)
        fetch(jnp.minimum(2 * n + 2, 63), ga)
        mix(2 * n + 1, gb)
        return carry

    lax.fori_loop(0, 32, chunk, 0)


def gather(base, a, b, col, fy, fx):
    return call(
        gather_kernel,
        jax.ShapeDtypeStruct((2, 8192), F32),
        [SM] + [VM] * 5,
        [pltpu.VMEM((32768, 128), F32)] + [pltpu.VMEM((512, 128), F32)] * 2,
        int(1e10), 30, "gather",
        base, a, b, col, fy, fx,
    )


AXES = ("wide", "narrow")


def spread(blocks):
    return lax.all_to_all(blocks, AXES, split_axis=0, concat_axis=0, tiled=True)


def swap_cores(x):
    n = lax.axis_size("narrow")
    return lax.ppermute(x, "narrow", [(i, i ^ 1) for i in range(n)])


def shards(stream_hat, dye, float_slot, float_row, float_col, float_frac, float_dye, tile_lists):
    device = lax.axis_index(AXES)
    group = lax.axis_index("wide")
    core = lax.axis_index("narrow") % 2
    wave = device * 64 + jnp.arange(64)
    wave = jnp.where(wave >= 4096, wave - 8192, wave).astype(F32)[None]
    spec = stream_send(stream_hat, wave)
    spec, float_slot, tile_lists = lax.optimization_barrier((spec, float_slot, tile_lists))
    spec = spread(spec.reshape(128, 2, 64, 128)).reshape(256, 64, 128)

    slot = float_slot.reshape(64, 128)
    row = float_row.reshape(64, 128)
    col = float_col.reshape(1, 8192)
    fy = float_frac[0:1]
    fx = float_frac[1:2]

    own_list = lax.dynamic_index_in_dim(tile_lists, group, 0, keepdims=False)
    holder = own_list // 64
    before = jnp.arange(256)[:, None] > jnp.arange(256)[None, :]
    rank = jnp.sum((before & (holder[:, None] == holder[None, :])).astype(jnp.int32), axis=1)
    position = jnp.where(own_list >= 0, jnp.where(rank == core, 0, 128) + holder, 0)
    pos = jnp.sum(
        jnp.where(jnp.arange(256)[:, None, None] == slot[None], position[:, None, None], 0), axis=0
    )

    mine = (tile_lists >= 0) & (tile_lists // 64 == device)
    place = jnp.cumsum(mine.astype(jnp.int32), axis=1) - 1
    local = tile_lists % 64 + 1
    entries = jnp.stack(
        [jnp.sum(jnp.where(mine & (place == e), local, 0), axis=1) for e in range(CAPO)], axis=1
    ).reshape(1, 32) - 1

    keep, send = deposit(pos * 64 + row, col, fy, fx, float_dye.reshape(1, 8192))
    dep = (keep.astype(F32) + swap_cores(send).astype(F32)).astype(BF)
    returned = spread(dep)
    spec, dep = lax.optimization_barrier((spec, dep))

    outgoing = stream_recv(entries, spec)
    outgoing, dye = lax.optimization_barrier((outgoing, dye))
    own = spread(outgoing)
    front = dye_send(entries, dye, returned)
    own, front = lax.optimization_barrier((own, front))
    other = swap_cores(own)
    front = spread(front.reshape(128, 2, 32, 128)).reshape(256, 32, 128)
    velocity = gather(pos * 128 + 2 * row, own, other, col, fy, fx)
    velocity, front = lax.optimization_barrier((velocity, front))
    dye_hat = dye_recv(front)
    return (velocity, dye_hat)


def solution(mesh):
    return jax.shard_map(
        shards,
        mesh=mesh,
        in_specs=(
            P(None, AXES, None),
            P(AXES, None),
            P(AXES),
            P(AXES),
            P(AXES),
            P(None, AXES),
            P(AXES),
            P(),
        ),
        out_specs=(P(None, AXES), P(None, AXES, None)),
        check_vma=False,
    )
```

```python
import numpy as np, math

import jax, jax.numpy as jnp
from jax import lax
from jax.sharding import PartitionSpec as P
from jax.experimental import pallas as pl
from jax.experimental.pallas import tpu as pltpu

BF = jnp.bfloat16
F32 = jnp.float32
NT = (((1,), (1,)), ((), ()))
PAD = 72
PAD2 = 136
PAD3 = 40


def cs(num, den, sign):
    ang = sign * 2.0 * math.pi * (num % den) / den
    return np.cos(ang), np.sin(ang)


def cplx(c, s):
    return np.stack([np.stack([c, -s]), np.stack([s, c])])


def bf(x):
    return np.asarray(x, np.float32).astype(jnp.bfloat16)


def send_tables(sign, stream):
    p = np.arange(64)
    q = np.arange(128)
    c, s = cs(p[:, None] * p[None, :], 64, sign)
    w = cplx(c, s).transpose(0, 2, 1, 3)
    if stream:
        a = w.reshape(128, 128)
        signed = np.where(p >= 32, p - 64, p) * 128.0
        b = (w * signed).reshape(128, 128)
        g = np.concatenate([a, b])
    else:
        g = w[:, :, 0, :].reshape(128, 64)
    tc, ts = cs(p[:, None] * q[None, :], 8192, sign)
    c, s = cs(q[:, None] * q[None, :], 128, sign)
    w2 = cplx(c, s).transpose(2, 0, 1, 3).reshape(256, 256)
    return bf(g), np.float32(tc), np.float32(ts), bf(w2)


def recv_tables(sign, stream):
    k = np.arange(128)
    r = np.arange(64)
    c, s = cs(k[:, None] * k[None, :], 128, sign)
    w1 = cplx(c, s).transpose(0, 2, 3, 1).reshape(256, 256)
    tc, ts = cs(k[:, None] * r[None, :], 8192, sign)
    tc = np.concatenate([tc, tc], 1)
    ts = np.concatenate([ts, ts], 1)
    c, s = cs(r[:, None] * r[None, :], 64, sign)
    w = cplx(c, s)
    v = np.zeros((2, 2, 64, 2, 2, 64))
    for e in range(2):
        v[:, e, :, :, e, :] = w.transpose(0, 2, 1, 3)
    if stream:
        v = v[0].reshape(128, 256)
    else:
        v = v.reshape(256, 256) / 8192.0
    return bf(w1), np.float32(tc), np.float32(ts), bf(v)


def stream_send_kernel(wa_ref, s_ref, g_ref, tc_ref, ts_ref, w2_ref, o_ref, xs, tre, tim, of):
    def load(p, carry):
        at = pl.multiple_of(p * 128, 128)
        for c in range(2):
            row = pl.multiple_of((c * 64 + p) * PAD, 8)
            xs[pl.ds(row, 64), :] = s_ref[c, :, pl.ds(at, 128)].astype(F32)
        return carry

    lax.fori_loop(0, 64, load, 0, unroll=4)
    q = lax.broadcasted_iota(jnp.int32, (64, 128), 1).astype(F32)

    def rows(n, carry):
        x = jnp.concatenate([xs[pl.ds(2 * n + h, 128, stride=PAD), :].astype(BF) for h in range(2)], axis=1)
        both = jnp.dot(g_ref[...], x, preferred_element_type=F32)
        tc = tc_ref[...]
        ts = ts_ref[...]
        for h in range(2):
            r = 2 * n + h
            z = both[:, h * 128 : h * 128 + 128]
            are, aim, bre, bim = z[:64], z[64:128], z[128:192], z[192:]
            ure = bre + q * are
            uim = bim + q * aim
            wa = wa_ref[0, r]
            base = pl.multiple_of(r * PAD2, 8)
            vre = are * tc - aim * ts
            vim = are * ts + aim * tc
            tre[pl.ds(base, 64), :] = ure * ts + uim * tc
            tim[pl.ds(base, 64), :] = uim * ts - ure * tc
            tre[pl.ds(base + 64, 64), :] = -wa * vim
            tim[pl.ds(base + 64, 64), :] = wa * vre
        return carry

    lax.fori_loop(0, 32, rows, 0, unroll=2)

    def cols(n, carry):
        parts = []
        for h in range(2):
            for f in range(2):
                at = pl.ds(f * 64 + 2 * n + h, 64, stride=PAD2)
                parts.append(jnp.concatenate([tre[at, :].astype(BF), tim[at, :].astype(BF)], axis=1))
        m = jnp.concatenate(parts, axis=0)
        out = lax.dot_general(w2_ref[...], m, NT, preferred_element_type=F32)
        for h in range(2):
            of[pl.ds(2 * n + h, 256, stride=PAD), :] = out[:, h * 128 : h * 128 + 128]
        return carry

    lax.fori_loop(0, 32, cols, 0, unroll=2)

    def store(i, carry):
        o_ref[i] = of[pl.ds(pl.multiple_of(i * PAD, 8), 64), :].astype(BF)
        return carry

    lax.fori_loop(0, 256, store, 0, unroll=8)


VM = pl.BlockSpec(memory_space=pltpu.VMEM)
SM = pl.BlockSpec(memory_space=pltpu.SMEM)


def call(kernel, outs, specs, scratch, cost, mib, name, *args):
    return pl.pallas_call(
        kernel,
        out_shape=outs,
        in_specs=specs,
        out_specs=jax.tree.map(lambda _: VM, outs),
        scratch_shapes=scratch,
        compiler_params=pltpu.CompilerParams(vmem_limit_bytes=mib << 20),
        cost_estimate=pl.CostEstimate(flops=cost, bytes_accessed=1 << 20, transcendentals=0),
        name=name,
    )(*args)


def stream_send(stream, wa):
    return call(
        stream_send_kernel,
        jax.ShapeDtypeStruct((256, 64, 128), BF),
        [SM] + [VM] * 5,
        [pltpu.VMEM((128 * PAD, 128), F32)] + [pltpu.VMEM((64 * PAD2, 128), F32)] * 2
        + [pltpu.VMEM((256 * PAD, 128), F32)],
        int(6e9), 60, "stream_send",
        wa, stream, *send_tables(1.0, True),
    )


def stream_recv_kernel(idx_ref, x_ref, w1_ref, tc_ref, ts_ref, v_ref, o_ref, xf, of):
    def load(i, carry):
        xf[pl.ds(pl.multiple_of(i * PAD, 8), 64), :] = x_ref[i].astype(F32)
        return carry

    lax.fori_loop(0, 256, load, 0, unroll=8)

    def step(n, carry):
        d = jnp.concatenate([xf[pl.ds(2 * n + h, 256, stride=PAD), :].astype(BF) for h in range(2)], axis=1)
        z = jnp.dot(w1_ref[...], d, preferred_element_type=F32)
        tc = tc_ref[...]
        ts = ts_ref[...]
        parts = []
        for h in range(2):
            re = z[:128, h * 128 : h * 128 + 128]
            im = z[128:, h * 128 : h * 128 + 128]
            parts.append(
                jnp.concatenate([(re * tc - im * ts).astype(BF), (re * ts + im * tc).astype(BF)], axis=1)
            )
        m = jnp.concatenate(parts, axis=0)
        out = lax.dot_general(v_ref[...], m, NT, preferred_element_type=F32)
        for h in range(2):
            for f in range(2):
                of[pl.ds(4 * n + 2 * h + f, 64, stride=PAD2), :] = out[f * 64 : f * 64 + 64, h * 128 : h * 128 + 128]
        return carry

    lax.fori_loop(0, 32, step, 0, unroll=2)

    def store(n, carry):
        tile = jnp.maximum(idx_ref[0, n], 0)
        o_ref[n] = of[pl.ds(pl.multiple_of(tile * PAD2, 8), 128), :].astype(BF)
        return carry

    lax.fori_loop(0, 32, store, 0, unroll=2)


def stream_recv(idx, x):
    return call(
        stream_recv_kernel,
        jax.ShapeDtypeStruct((32, 128, 128), BF),
        [SM] + [VM] * 5,
        [pltpu.VMEM((256 * PAD, 128), F32), pltpu.VMEM((64 * PAD2, 128), F32)],
        int(6e9), 28, "stream_recv",
        idx, x, *recv_tables(1.0, True),
    )


def dye_send_kernel(idx_ref, dye_ref, ret_ref, g_ref, tc_ref, ts_ref, w2_ref, o_ref, xs, tre, tim, of):
    def load(p, carry):
        at = pl.multiple_of(p * 128, 128)
        xs[pl.ds(pl.multiple_of(p * PAD, 8), 64), :] = dye_ref[:, pl.ds(at, 128)].astype(F32)
        return carry

    lax.fori_loop(0, 64, load, 0, unroll=4)

    def place(n, carry):
        tile = idx_ref[0, n]

        @pl.when(tile >= 0)
        def _():
            at = pl.ds(pl.multiple_of(tile * PAD, 8), 64)
            xs[at, :] = xs[at, :] + ret_ref[n].astype(F32)

        return carry

    lax.fori_loop(0, 32, place, 0)

    def rows(n, carry):
        x = jnp.concatenate([xs[pl.ds(4 * n + h, 64, stride=PAD), :].astype(BF) for h in range(4)], axis=1)
        z = jnp.dot(g_ref[...], x, preferred_element_type=F32)
        tc = tc_ref[...]
        ts = ts_ref[...]
        for h in range(4):
            re = z[:64, h * 128 : h * 128 + 128]
            im = z[64:, h * 128 : h * 128 + 128]
            base = pl.multiple_of((4 * n + h) * PAD, 8)
            tre[pl.ds(base, 64), :] = re * tc - im * ts
            tim[pl.ds(base, 64), :] = re * ts + im * tc
        return carry

    lax.fori_loop(0, 16, rows, 0, unroll=2)

    def cols(n, carry):
        parts = []
        for e in range(4):
            at = pl.ds(4 * n + e, 64, stride=PAD)
            parts.append(jnp.concatenate([tre[at, :].astype(BF), tim[at, :].astype(BF)], axis=1))
        m = jnp.concatenate(parts, axis=0)
        out = lax.dot_general(w2_ref[...], m, NT, preferred_element_type=F32)
        for h in range(2):
            of[pl.ds(2 * n + h, 256, stride=PAD3), :] = out[:, h * 128 : h * 128 + 128]
        return carry

    lax.fori_loop(0, 16, cols, 0, unroll=2)

    def store(i, carry):
        o_ref[i] = of[pl.ds(pl.multiple_of(i * PAD3, 8), 32), :].astype(BF)
        return carry

    lax.fori_loop(0, 256, store, 0, unroll=8)


def dye_send(idx, dye, ret):
    return call(
        dye_send_kernel,
        jax.ShapeDtypeStruct((256, 32, 128), BF),
        [SM] + [VM] * 6,
        [pltpu.VMEM((64 * PAD, 128), F32)] * 3 + [pltpu.VMEM((256 * PAD3, 128), F32)],
        int(4e9), 24, "dye_send",
        idx, dye, ret, *send_tables(-1.0, False),
    )


def dye_recv_kernel(x_ref, w1_ref, tc_ref, ts_ref, v_ref, o_ref, xf, of):
    def load(i, carry):
        xf[pl.ds(pl.multiple_of(i * PAD3, 8), 32), :] = x_ref[i].astype(F32)
        return carry

    lax.fori_loop(0, 256, load, 0, unroll=8)

    def step(n, carry):
        d = jnp.concatenate([xf[pl.ds(2 * n + h, 256, stride=PAD3), :].astype(BF) for h in range(2)], axis=1)
        z = jnp.dot(w1_ref[...], d, preferred_element_type=F32)
        tc = tc_ref[...]
        ts = ts_ref[...]
        parts = []
        for h in range(2):
            re = z[:128, h * 128 : h * 128 + 128]
            im = z[128:, h * 128 : h * 128 + 128]
            parts.append(
                jnp.concatenate([(re * tc - im * ts).astype(BF), (re * ts + im * tc).astype(BF)], axis=1)
            )
        m = jnp.concatenate(parts, axis=0)
        out = lax.dot_general(v_ref[...], m, NT, preferred_element_type=F32)
        for h in range(2):
            for c in range(2):
                for e in range(2):
                    row = c * 4096 + (n // 2) * 512 + (4 * n + 2 * h + e) % 8
                    of[pl.ds(row, 64, stride=8), :] = out[
                        (2 * c + e) * 64 : (2 * c + e) * 64 + 64, h * 128 : h * 128 + 128
                    ]
        return carry

    lax.fori_loop(0, 16, step, 0, unroll=2)

    def store(n, carry):
        c = n // 8
        t8 = n % 8
        base = pl.multiple_of(n * 512, 512)
        at = pl.ds(pl.multiple_of(t8 * 8, 8), 8)
        for j in range(64):
            o_ref[c, at, j * 128 : j * 128 + 128] = of[pl.ds(base + j * 8, 8), :]
        return carry

    lax.fori_loop(0, 16, store, 0)


def dye_recv(x):
    return call(
        dye_recv_kernel,
        jax.ShapeDtypeStruct((2, 64, 8192), F32),
        [VM] * 5,
        [pltpu.VMEM((256 * PAD3, 128), F32), pltpu.VMEM((8192, 128), F32)],
        int(4e9), 20, "dye_recv",
        x, *recv_tables(-1.0, False),
    )

CAPO = 2


def deposit_kernel(idx_ref, col_ref, fy_ref, fx_ref, am_ref, keep_ref, send_ref, wa, wb, *accs):
    ways = len(accs)

    def clear(i, carry):
        for acc in accs:
            acc[pl.ds(pl.multiple_of(i * 64, 64), 64), :] = jnp.zeros((64, 128), F32)
        return carry

    lax.fori_loop(0, 256, clear, 0, unroll=2)

    def weights(n, dst):
        xs = lax.broadcasted_iota(jnp.int32, (128, 128), 0)
        rows = lax.broadcasted_iota(jnp.int32, (256, 128), 0)
        off = rows // 2 - lax.broadcasted_iota(jnp.int32, (256, 128), 1)
        odd = rows % 2 == 1
        at = pl.ds(pl.multiple_of(n * 128, 128), 128)
        fx = fx_ref[:, at]
        am = am_ref[:, at]
        hi = am * fy_ref[:, at]
        lo = am - hi
        d = xs - col_ref[:, at]
        w = jnp.where(d == 0, 1.0 - fx, jnp.where(d == 1, fx, 0.0)).astype(BF)
        e = jnp.where(off == 0, jnp.where(odd, hi, lo), 0.0).astype(BF)
        dst[...] = lax.dot_general(e, w, NT, preferred_element_type=F32)

    def add(n, src):
        for f in range(0, 128, ways):
            at = [pl.ds(idx_ref[n, f + k], 2) for k in range(ways)]
            new = [accs[k][at[k], :] + src[2 * (f + k) : 2 * (f + k) + 2, :] for k in range(ways)]
            for k in range(ways):
                accs[k][at[k], :] = new[k]

    weights(0, wa)

    def chunk(n, carry):
        weights(2 * n + 1, wb)
        add(2 * n, wa)
        weights(jnp.minimum(2 * n + 2, 63), wa)
        add(2 * n + 1, wb)
        return carry

    lax.fori_loop(0, 32, chunk, 0)

    def store(i, carry):
        for ref, base in ((keep_ref, 0), (send_ref, 8192)):
            at = pl.ds(pl.multiple_of(i * 64 + base, 64), 64)
            total = accs[0][at, :]
            for acc in accs[1:]:
                total = total + acc[at, :]
            ref[i] = total.astype(BF)
        return carry

    lax.fori_loop(0, 128, store, 0, unroll=2)


def deposit(idx, col, fy, fx, am):
    return call(
        deposit_kernel,
        [jax.ShapeDtypeStruct((128, 64, 128), BF)] * 2,
        [SM] + [VM] * 4,
        [pltpu.VMEM((256, 128), F32)] * 2 + [pltpu.VMEM((16384, 128), F32)] * 4,
        int(1.2e10), 44, "deposit",
        idx, col, fy, fx, am,
    )


def gather_kernel(base_ref, col_ref, fy_ref, fx_ref, *refs):
    o_ref, st, ga, gb = refs[-4:]
    row = 0
    for ref in refs[:-4]:

        def load(i, carry, ref=ref, row=row):
            st[pl.ds(pl.multiple_of(row + i * 128, 128), 128), :] = ref[i].astype(F32)
            return carry

        lax.fori_loop(0, ref.shape[0], load, 0, unroll=4)
        row += ref.shape[0] * 128

    def fetch(n, g):
        for f in range(128):
            g[f * 4 : f * 4 + 4, :] = st[pl.ds(base_ref[n, f], 4), :]

    def mix(n, g):
        sub = lax.broadcasted_iota(jnp.int32, (8, 128), 0)
        off = lax.broadcasted_iota(jnp.int32, (8, 128), 1) - sub // 4
        upper = sub % 4 >= 2
        odd = sub % 2 == 1
        xs = lax.broadcasted_iota(jnp.int32, (128, 128), 0)
        at = pl.ds(pl.multiple_of(n * 128, 128), 128)
        col = col_ref[:, at]
        fy = fy_ref[:, at]
        fx = fx_ref[:, at]
        d = xs - col
        w = jnp.where(d == 0, 1.0 - fx, jnp.where(d == 1, fx, 0.0))
        hi = w.astype(BF)
        lo = (w - hi.astype(F32)).astype(BF)
        z = jnp.dot(g[...].astype(BF), jnp.concatenate([hi, lo], axis=1), preferred_element_type=F32)
        parts = [jnp.zeros((8, 128), F32) for _ in range(4)]
        for i in range(64):
            keep = off == 2 * i
            for h in range(2):
                k = 2 * h + i % 2
                parts[k] = parts[k] + jnp.where(keep, z[8 * i : 8 * i + 8, h * 128 : h * 128 + 128], 0.0)
        total = (parts[0] + parts[1] + (parts[2] + parts[3])) * jnp.where(upper, fy, 1.0 - fy)
        o_ref[0:1, at] = jnp.sum(jnp.where(odd, 0.0, total), axis=0, keepdims=True)
        o_ref[1:2, at] = jnp.sum(jnp.where(odd, total, 0.0), axis=0, keepdims=True)

    fetch(0, ga)

    def chunk(n, carry):
        fetch(2 * n + 1, gb)
        mix(2 * n, ga)
        fetch(jnp.minimum(2 * n + 2, 63), ga)
        mix(2 * n + 1, gb)
        return carry

    lax.fori_loop(0, 32, chunk, 0)


def gather(base, col, fy, fx, pieces):
    return call(
        gather_kernel,
        jax.ShapeDtypeStruct((2, 8192), F32),
        [SM] + [VM] * (3 + len(pieces)),
        [pltpu.VMEM((32768, 128), F32)] + [pltpu.VMEM((512, 128), F32)] * 2,
        int(1e10), 30, "gather",
        base, col, fy, fx, *pieces,
    )


AXES = ("wide", "narrow")


def spread(blocks, axes=AXES):
    return lax.all_to_all(blocks, axes, split_axis=0, concat_axis=0, tiled=True)


def swap_cores(x):
    n = lax.axis_size("narrow")
    return lax.ppermute(x, "narrow", [(i, i ^ 1) for i in range(n)])


def shift(x, chips):
    n = lax.axis_size("narrow")
    return lax.ppermute(x, "narrow", [(i, (i + 2 * chips) % n) for i in range(n)])


def add(*parts):
    return sum(part.astype(F32) for part in parts).astype(BF)


def chip_sum(keep, send):
    part = add(keep, swap_cores(send)).reshape(4, 2, 16, 64, 128)
    up = shift(part[2, 0], 1)
    down = shift(part[2, 1], -1)
    up_hi = shift(part[1, 1], 1)
    down_lo = shift(part[3, 0], -1)
    up_lo = shift(add(part[1, 0], up), 1)
    down_hi = shift(add(part[3, 1], down), -1)
    return jnp.concatenate([add(part[0, 0], up_lo, down_lo), add(part[0, 1], up_hi, down_hi)])


def chip_gather(own):
    down = shift(own, 1)
    up = shift(own, -1)
    far = [shift(down[:16], 1), shift(up[16:], -1)]
    mine = [own, up] + far + [down]
    return mine + [swap_cores(x) for x in mine]


def shards(stream_hat, dye, float_slot, float_row, float_col, float_frac, float_dye, tile_lists):
    device = lax.axis_index(AXES)
    group = lax.axis_index("wide")
    chip = lax.axis_index("narrow") // 2
    core = lax.axis_index("narrow") % 2
    wave = device * 64 + jnp.arange(64)
    wave = jnp.where(wave >= 4096, wave - 8192, wave).astype(F32)[None]
    spec = stream_send(stream_hat, wave)
    spec, float_slot, tile_lists = lax.optimization_barrier((spec, float_slot, tile_lists))
    spec = spread(spec.reshape(128, 2, 64, 128)).reshape(256, 64, 128)

    slot = float_slot.reshape(64, 128)
    row = float_row.reshape(64, 128)
    col = float_col.reshape(1, 8192)
    fy = float_frac[0:1]
    fx = float_frac[1:2]

    own_list = lax.dynamic_index_in_dim(tile_lists, group, 0, keepdims=False)
    holder = own_list // 64
    before = jnp.arange(256)[:, None] > jnp.arange(256)[None, :]
    rank = jnp.sum((before & (holder[:, None] == holder[None, :])).astype(jnp.int32), axis=1)
    away = (holder % 8 // 2 - chip) % 4
    other = (holder % 2 + core) % 2
    position = jnp.where(own_list >= 0, (other * 4 + away) * 32 + holder // 8 * 2 + rank, 0)
    pos = jnp.sum(
        jnp.where(jnp.arange(256)[:, None, None] == slot[None], position[:, None, None], 0), axis=0
    )

    mine = (tile_lists >= 0) & (tile_lists // 64 == device)
    place = jnp.cumsum(mine.astype(jnp.int32), axis=1) - 1
    local = tile_lists % 64 + 1
    entries = jnp.stack(
        [jnp.sum(jnp.where(mine & (place == e), local, 0), axis=1) for e in range(CAPO)], axis=1
    ).reshape(1, 32) - 1

    keep, send = deposit(pos * 64 + row, col, fy, fx, float_dye.reshape(1, 8192))
    dep = chip_sum(keep, send)
    returned = spread(dep.reshape(16, 2, 64, 128), "wide").reshape(32, 64, 128)
    spec, dep = lax.optimization_barrier((spec, dep))

    outgoing = stream_recv(entries, spec)
    outgoing, dye = lax.optimization_barrier((outgoing, dye))
    own = spread(outgoing.reshape(16, 2, 128, 128), "wide").reshape(32, 128, 128)
    front = dye_send(entries, dye, returned)
    own, front = lax.optimization_barrier((own, front))
    pieces = chip_gather(own)
    front = spread(front.reshape(128, 2, 32, 128)).reshape(256, 32, 128)
    velocity = gather(pos * 128 + 2 * row, col, fy, fx, pieces)
    velocity, front = lax.optimization_barrier((velocity, front))
    dye_hat = dye_recv(front)
    return (velocity, dye_hat)


def solution(mesh):
    return jax.shard_map(
        shards,
        mesh=mesh,
        in_specs=(
            P(None, AXES, None),
            P(AXES, None),
            P(AXES),
            P(AXES),
            P(AXES),
            P(None, AXES),
            P(AXES),
            P(),
        ),
        out_specs=(P(None, AXES), P(None, AXES, None)),
        check_vma=False,
    )
```

```python
import numpy as np, math

import jax, jax.numpy as jnp
from jax import lax
from jax.sharding import PartitionSpec as P
from jax.experimental import pallas as pl
from jax.experimental.pallas import tpu as pltpu

BF = jnp.bfloat16
F32 = jnp.float32
NT = (((1,), (1,)), ((), ()))
PAD = 72
PAD2 = 136
PAD3 = 40


def cs(num, den, sign):
    ang = sign * 2.0 * math.pi * (num % den) / den
    return np.cos(ang), np.sin(ang)


def cplx(c, s):
    return np.stack([np.stack([c, -s]), np.stack([s, c])])


def bf(x):
    return np.asarray(x, np.float32).astype(jnp.bfloat16)


def send_tables(sign, stream):
    p = np.arange(64)
    q = np.arange(128)
    c, s = cs(p[:, None] * p[None, :], 64, sign)
    w = cplx(c, s).transpose(0, 2, 1, 3)
    if stream:
        a = w.reshape(128, 128)
        signed = np.where(p >= 32, p - 64, p) * 128.0
        b = (w * signed).reshape(128, 128)
        g = np.concatenate([a, b])
    else:
        g = w[:, :, 0, :].reshape(128, 64)
    tc, ts = cs(p[:, None] * q[None, :], 8192, sign)
    c, s = cs(q[:, None] * q[None, :], 128, sign)
    w2 = cplx(c, s).transpose(2, 0, 1, 3).reshape(256, 256)
    return bf(g), np.float32(tc), np.float32(ts), bf(w2)


def recv_tables(sign, stream):
    k = np.arange(128)
    r = np.arange(64)
    c, s = cs(k[:, None] * k[None, :], 128, sign)
    w1 = cplx(c, s).transpose(0, 2, 3, 1).reshape(256, 256)
    tc, ts = cs(k[:, None] * r[None, :], 8192, sign)
    tc = np.concatenate([tc, tc], 1)
    ts = np.concatenate([ts, ts], 1)
    c, s = cs(r[:, None] * r[None, :], 64, sign)
    w = cplx(c, s)
    v = np.zeros((2, 2, 64, 2, 2, 64))
    for e in range(2):
        v[:, e, :, :, e, :] = w.transpose(0, 2, 1, 3)
    if stream:
        v = v[0].reshape(128, 256)
    else:
        v = v.reshape(256, 256) / 8192.0
    return bf(w1), np.float32(tc), np.float32(ts), bf(v)


def stream_send_kernel(wa_ref, s_ref, g_ref, tc_ref, ts_ref, w2_ref, o_ref, xs, tre, tim, of):
    def load(p, carry):
        at = pl.multiple_of(p * 128, 128)
        for c in range(2):
            row = pl.multiple_of((c * 64 + p) * PAD, 8)
            xs[pl.ds(row, 64), :] = s_ref[c, :, pl.ds(at, 128)].astype(F32)
        return carry

    lax.fori_loop(0, 64, load, 0, unroll=4)
    q = lax.broadcasted_iota(jnp.int32, (64, 128), 1).astype(F32)

    def rows(n, carry):
        x = jnp.concatenate([xs[pl.ds(2 * n + h, 128, stride=PAD), :].astype(BF) for h in range(2)], axis=1)
        both = jnp.dot(g_ref[...], x, preferred_element_type=F32)
        tc = tc_ref[...]
        ts = ts_ref[...]
        for h in range(2):
            r = 2 * n + h
            z = both[:, h * 128 : h * 128 + 128]
            are, aim, bre, bim = z[:64], z[64:128], z[128:192], z[192:]
            ure = bre + q * are
            uim = bim + q * aim
            wa = wa_ref[0, r]
            base = pl.multiple_of(r * PAD2, 8)
            vre = are * tc - aim * ts
            vim = are * ts + aim * tc
            tre[pl.ds(base, 64), :] = ure * ts + uim * tc
            tim[pl.ds(base, 64), :] = uim * ts - ure * tc
            tre[pl.ds(base + 64, 64), :] = -wa * vim
            tim[pl.ds(base + 64, 64), :] = wa * vre
        return carry

    lax.fori_loop(0, 32, rows, 0, unroll=2)

    def cols(n, carry):
        parts = []
        for h in range(2):
            for f in range(2):
                at = pl.ds(f * 64 + 2 * n + h, 64, stride=PAD2)
                parts.append(jnp.concatenate([tre[at, :].astype(BF), tim[at, :].astype(BF)], axis=1))
        m = jnp.concatenate(parts, axis=0)
        out = lax.dot_general(w2_ref[...], m, NT, preferred_element_type=F32)
        for h in range(2):
            of[pl.ds(2 * n + h, 256, stride=PAD), :] = out[:, h * 128 : h * 128 + 128]
        return carry

    lax.fori_loop(0, 32, cols, 0, unroll=2)

    def store(i, carry):
        o_ref[i] = of[pl.ds(pl.multiple_of(i * PAD, 8), 64), :].astype(BF)
        return carry

    lax.fori_loop(0, 256, store, 0, unroll=8)


VM = pl.BlockSpec(memory_space=pltpu.VMEM)
SM = pl.BlockSpec(memory_space=pltpu.SMEM)


def call(kernel, outs, specs, scratch, cost, mib, name, *args):
    return pl.pallas_call(
        kernel,
        out_shape=outs,
        in_specs=specs,
        out_specs=jax.tree.map(lambda _: VM, outs),
        scratch_shapes=scratch,
        compiler_params=pltpu.CompilerParams(vmem_limit_bytes=mib << 20),
        cost_estimate=pl.CostEstimate(flops=cost, bytes_accessed=1 << 20, transcendentals=0),
        name=name,
    )(*args)


def stream_send(stream, wa):
    return call(
        stream_send_kernel,
        jax.ShapeDtypeStruct((256, 64, 128), BF),
        [SM] + [VM] * 5,
        [pltpu.VMEM((128 * PAD, 128), F32)] + [pltpu.VMEM((64 * PAD2, 128), F32)] * 2
        + [pltpu.VMEM((256 * PAD, 128), F32)],
        int(6e9), 60, "stream_send",
        wa, stream, *send_tables(1.0, True),
    )


def stream_recv_kernel(idx_ref, x_ref, w1_ref, tc_ref, ts_ref, v_ref, o_ref, xf, of):
    def load(i, carry):
        xf[pl.ds(pl.multiple_of(i * PAD, 8), 64), :] = x_ref[i].astype(F32)
        return carry

    lax.fori_loop(0, 256, load, 0, unroll=8)

    def step(n, carry):
        d = jnp.concatenate([xf[pl.ds(2 * n + h, 256, stride=PAD), :].astype(BF) for h in range(2)], axis=1)
        z = jnp.dot(w1_ref[...], d, preferred_element_type=F32)
        tc = tc_ref[...]
        ts = ts_ref[...]
        parts = []
        for h in range(2):
            re = z[:128, h * 128 : h * 128 + 128]
            im = z[128:, h * 128 : h * 128 + 128]
            parts.append(
                jnp.concatenate([(re * tc - im * ts).astype(BF), (re * ts + im * tc).astype(BF)], axis=1)
            )
        m = jnp.concatenate(parts, axis=0)
        out = lax.dot_general(v_ref[...], m, NT, preferred_element_type=F32)
        for h in range(2):
            for f in range(2):
                of[pl.ds(64 * f + 2 * n + h, 64, stride=PAD2), :] = out[f * 64 : f * 64 + 64, h * 128 : h * 128 + 128]
        return carry

    lax.fori_loop(0, 32, step, 0, unroll=2)

    def store(n, carry):
        tile = jnp.maximum(idx_ref[0, n], 0)
        for f in range(2):
            data = of[pl.ds(pl.multiple_of(tile * PAD2, 8) + 64 * f, 64), :].astype(BF)
            for x in range(2):
                o_ref[n // 2 * 8 + 4 * x + 2 * f + n % 2] = data
        return carry

    lax.fori_loop(0, 32, store, 0, unroll=2)


def stream_recv(idx, x):
    return call(
        stream_recv_kernel,
        jax.ShapeDtypeStruct((128, 64, 128), BF),
        [SM] + [VM] * 5,
        [pltpu.VMEM((256 * PAD, 128), F32), pltpu.VMEM((64 * PAD2, 128), F32)],
        int(6e9), 28, "stream_recv",
        idx, x, *recv_tables(1.0, True),
    )


def dye_send_kernel(idx_ref, dye_ref, ret_ref, g_ref, tc_ref, ts_ref, w2_ref, o_ref, xs, tre, tim, of):
    def load(p, carry):
        at = pl.multiple_of(p * 128, 128)
        xs[pl.ds(pl.multiple_of(p * PAD, 8), 64), :] = dye_ref[:, pl.ds(at, 128)].astype(F32)
        return carry

    lax.fori_loop(0, 64, load, 0, unroll=4)

    def place(n, carry):
        tile = idx_ref[0, n]

        @pl.when(tile >= 0)
        def _():
            g = n // 2
            e = n % 2
            for half in range(2):
                at = pl.ds(pl.multiple_of(tile * PAD, 8) + 32 * half, 32)
                total = xs[at, :]
                for x in range(2):
                    total = total + ret_ref[g * 8 + 4 * x + 2 * half + e].astype(F32)
                xs[at, :] = total

        return carry

    lax.fori_loop(0, 32, place, 0)

    def rows(n, carry):
        x = jnp.concatenate([xs[pl.ds(4 * n + h, 64, stride=PAD), :].astype(BF) for h in range(4)], axis=1)
        z = jnp.dot(g_ref[...], x, preferred_element_type=F32)
        tc = tc_ref[...]
        ts = ts_ref[...]
        for h in range(4):
            re = z[:64, h * 128 : h * 128 + 128]
            im = z[64:, h * 128 : h * 128 + 128]
            base = pl.multiple_of((4 * n + h) * PAD, 8)
            tre[pl.ds(base, 64), :] = re * tc - im * ts
            tim[pl.ds(base, 64), :] = re * ts + im * tc
        return carry

    lax.fori_loop(0, 16, rows, 0, unroll=2)

    def cols(n, carry):
        parts = []
        for e in range(4):
            at = pl.ds(4 * n + e, 64, stride=PAD)
            parts.append(jnp.concatenate([tre[at, :].astype(BF), tim[at, :].astype(BF)], axis=1))
        m = jnp.concatenate(parts, axis=0)
        out = lax.dot_general(w2_ref[...], m, NT, preferred_element_type=F32)
        for h in range(2):
            of[pl.ds(2 * n + h, 256, stride=PAD3), :] = out[:, h * 128 : h * 128 + 128]
        return carry

    lax.fori_loop(0, 16, cols, 0, unroll=2)

    def store(i, carry):
        o_ref[i] = of[pl.ds(pl.multiple_of(i * PAD3, 8), 32), :].astype(BF)
        return carry

    lax.fori_loop(0, 256, store, 0, unroll=8)


def dye_send(idx, dye, ret):
    return call(
        dye_send_kernel,
        jax.ShapeDtypeStruct((256, 32, 128), BF),
        [SM] + [VM] * 6,
        [pltpu.VMEM((64 * PAD, 128), F32)] * 3 + [pltpu.VMEM((256 * PAD3, 128), F32)],
        int(4e9), 24, "dye_send",
        idx, dye, ret, *send_tables(-1.0, False),
    )


def dye_recv_kernel(x_ref, w1_ref, tc_ref, ts_ref, v_ref, o_ref, xf, of):
    def load(i, carry):
        xf[pl.ds(pl.multiple_of(i * PAD3, 8), 32), :] = x_ref[i].astype(F32)
        return carry

    lax.fori_loop(0, 256, load, 0, unroll=8)

    def step(n, carry):
        d = jnp.concatenate([xf[pl.ds(2 * n + h, 256, stride=PAD3), :].astype(BF) for h in range(2)], axis=1)
        z = jnp.dot(w1_ref[...], d, preferred_element_type=F32)
        tc = tc_ref[...]
        ts = ts_ref[...]
        parts = []
        for h in range(2):
            re = z[:128, h * 128 : h * 128 + 128]
            im = z[128:, h * 128 : h * 128 + 128]
            parts.append(
                jnp.concatenate([(re * tc - im * ts).astype(BF), (re * ts + im * tc).astype(BF)], axis=1)
            )
        m = jnp.concatenate(parts, axis=0)
        out = lax.dot_general(v_ref[...], m, NT, preferred_element_type=F32)
        for h in range(2):
            for c in range(2):
                for e in range(2):
                    row = c * 4096 + (n // 2) * 512 + (4 * n + 2 * h + e) % 8
                    of[pl.ds(row, 64, stride=8), :] = out[
                        (2 * c + e) * 64 : (2 * c + e) * 64 + 64, h * 128 : h * 128 + 128
                    ]
        return carry

    lax.fori_loop(0, 16, step, 0, unroll=2)

    def store(n, carry):
        c = n // 8
        t8 = n % 8
        base = pl.multiple_of(n * 512, 512)
        at = pl.ds(pl.multiple_of(t8 * 8, 8), 8)
        for j in range(64):
            o_ref[c, at, j * 128 : j * 128 + 128] = of[pl.ds(base + j * 8, 8), :]
        return carry

    lax.fori_loop(0, 16, store, 0)


def dye_recv(x):
    return call(
        dye_recv_kernel,
        jax.ShapeDtypeStruct((2, 64, 8192), F32),
        [VM] * 5,
        [pltpu.VMEM((256 * PAD3, 128), F32), pltpu.VMEM((8192, 128), F32)],
        int(4e9), 20, "dye_recv",
        x, *recv_tables(-1.0, False),
    )

CAPO = 2


def deposit_kernel(idx_ref, col_ref, fy_ref, fx_ref, am_ref, keep_ref, send_ref, wa, wb, *accs):
    ways = len(accs)

    def clear(i, carry):
        for acc in accs:
            acc[pl.ds(pl.multiple_of(i * 40, 8), 40), :] = jnp.zeros((40, 128), F32)
        return carry

    lax.fori_loop(0, 257, clear, 0)

    def weights(n, dst):
        xs = lax.broadcasted_iota(jnp.int32, (128, 128), 0)
        rows = lax.broadcasted_iota(jnp.int32, (256, 128), 0)
        off = rows // 2 - lax.broadcasted_iota(jnp.int32, (256, 128), 1)
        odd = rows % 2 == 1
        at = pl.ds(pl.multiple_of(n * 128, 128), 128)
        fx = fx_ref[:, at]
        am = am_ref[:, at]
        hi = am * fy_ref[:, at]
        lo = am - hi
        d = xs - col_ref[:, at]
        w = jnp.where(d == 0, 1.0 - fx, jnp.where(d == 1, fx, 0.0)).astype(BF)
        e = jnp.where(off == 0, jnp.where(odd, hi, lo), 0.0).astype(BF)
        dst[...] = lax.dot_general(e, w, NT, preferred_element_type=F32)

    def add(n, src):
        for f in range(0, 128, ways):
            at = [pl.ds(idx_ref[n, f + k], 2) for k in range(ways)]
            new = [accs[k][at[k], :] + src[2 * (f + k) : 2 * (f + k) + 2, :] for k in range(ways)]
            for k in range(ways):
                accs[k][at[k], :] = new[k]

    weights(0, wa)

    def chunk(n, carry):
        weights(2 * n + 1, wb)
        add(2 * n, wa)
        weights(jnp.minimum(2 * n + 2, 127), wa)
        add(2 * n + 1, wb)
        return carry

    lax.fori_loop(0, 64, chunk, 0)

    def store(i, carry):
        for ref, base in ((keep_ref, 8), (send_ref, 128 * 40 + 8)):
            at = pl.ds(pl.multiple_of(i * 40 + base, 8), 32)
            total = accs[0][at, :]
            for acc in accs[1:]:
                total = total + acc[at, :]
            ref[i] = total.astype(BF)
        return carry

    lax.fori_loop(0, 128, store, 0, unroll=2)


def deposit(idx, col, fy, fx, am):
    return call(
        deposit_kernel,
        [jax.ShapeDtypeStruct((128, 32, 128), BF)] * 2,
        [SM] + [VM] * 4,
        [pltpu.VMEM((256, 128), F32)] * 2 + [pltpu.VMEM((257 * 40, 128), F32)] * 4,
        int(2e10), 30, "deposit",
        idx, col, fy, fx, am,
    )


def gather_kernel(base_ref, a_ref, b_ref, col_ref, fy_ref, fx_ref, o_ref, st, ga, gb):
    def load(i, carry):
        at = pl.multiple_of(i * 64, 64)
        st[pl.ds(at, 64), :] = a_ref[i].astype(F32)
        st[pl.ds(at + 8192, 64), :] = b_ref[i].astype(F32)
        return carry

    lax.fori_loop(0, 128, load, 0, unroll=4)

    def fetch(n, g):
        for f in range(128):
            g[f * 2 : f * 2 + 2, :] = st[pl.ds(base_ref[n, f], 2), :]

    def mix(n, g):
        sub = lax.broadcasted_iota(jnp.int32, (8, 128), 0)
        off = lax.broadcasted_iota(jnp.int32, (8, 128), 1) - sub // 2
        xs = lax.broadcasted_iota(jnp.int32, (128, 128), 0)
        at = pl.ds(pl.multiple_of(n * 128, 128), 128)
        col = col_ref[:, at]
        fy = fy_ref[:, at]
        fx = fx_ref[:, at]
        d = xs - col
        w = jnp.where(d == 0, 1.0 - fx, jnp.where(d == 1, fx, 0.0))
        hi = w.astype(BF)
        lo = (w - hi.astype(F32)).astype(BF)
        z = jnp.dot(g[...].astype(BF), jnp.concatenate([hi, lo], axis=1), preferred_element_type=F32)
        parts = [jnp.zeros((8, 128), F32) for _ in range(4)]
        for i in range(32):
            keep = off == 4 * i
            for h in range(2):
                k = 2 * h + i % 2
                parts[k] = parts[k] + jnp.where(keep, z[8 * i : 8 * i + 8, h * 128 : h * 128 + 128], 0.0)
        total = (parts[0] + parts[1] + (parts[2] + parts[3])) * jnp.where(sub % 2 == 1, fy, 1.0 - fy)
        o_ref[:, at] = jnp.sum(total, axis=0, keepdims=True)

    fetch(0, ga)

    def chunk(n, carry):
        fetch(2 * n + 1, gb)
        mix(2 * n, ga)
        fetch(jnp.minimum(2 * n + 2, 127), ga)
        mix(2 * n + 1, gb)
        return carry

    lax.fori_loop(0, 64, chunk, 0)


def gather(base, a, b, col, fy, fx):
    return call(
        gather_kernel,
        jax.ShapeDtypeStruct((1, 16384), F32),
        [SM] + [VM] * 5,
        [pltpu.VMEM((16384, 128), F32)] + [pltpu.VMEM((256, 128), F32)] * 2,
        int(1e10), 20, "gather",
        base, a, b, col, fy, fx,
    )


AXES = ("wide", "narrow")


def spread(blocks):
    return lax.all_to_all(blocks, AXES, split_axis=0, concat_axis=0, tiled=True)


def swap_cores(x):
    n = lax.axis_size("narrow")
    return lax.ppermute(x, "narrow", [(i, i ^ 1) for i in range(n)])


def swap_chips(x):
    n = lax.axis_size("narrow")
    return lax.ppermute(x, "narrow", [(i, i ^ 2) for i in range(n)])


def shards(stream_hat, dye, float_slot, float_row, float_col, float_frac, float_dye, tile_lists):
    device = lax.axis_index(AXES)
    group = lax.axis_index("wide")
    core = lax.axis_index("narrow") % 2
    side = lax.axis_index("narrow") // 2 % 2
    wave = device * 64 + jnp.arange(64)
    wave = jnp.where(wave >= 4096, wave - 8192, wave).astype(F32)[None]

    floats = (float_slot, float_row, float_col, float_frac, float_dye)
    theirs = [swap_chips(x) for x in floats]
    spec = stream_send(stream_hat, wave)
    spec, theirs, tile_lists = lax.optimization_barrier((spec, theirs, tile_lists))
    spec = spread(spec.reshape(128, 2, 64, 128)).reshape(256, 64, 128)
    slot, row, col, frac, amount = [
        jnp.concatenate([x, y], axis=-1) for x, y in zip(floats, theirs)
    ]
    slot = slot.reshape(128, 128)
    row = row.reshape(128, 128)
    col = col.reshape(1, 16384)
    fy = frac[0:1]
    fx = frac[1:2]

    own_list = lax.dynamic_index_in_dim(tile_lists, group, 0, keepdims=False)
    holder = own_list // 64
    before = jnp.arange(256)[:, None] > jnp.arange(256)[None, :]
    rank = jnp.sum((before & (holder[:, None] == holder[None, :])).astype(jnp.int32), axis=1)
    position = jnp.where(own_list >= 0, jnp.where(rank == core, 0, 128) + holder, 0)
    pos = jnp.sum(
        jnp.where(jnp.arange(256)[:, None, None] == slot[None], position[:, None, None], 0), axis=0
    )

    mine = (tile_lists >= 0) & (tile_lists // 64 == device)
    place = jnp.cumsum(mine.astype(jnp.int32), axis=1) - 1
    local = tile_lists % 64 + 1
    entries = jnp.stack(
        [jnp.sum(jnp.where(mine & (place == e), local, 0), axis=1) for e in range(CAPO)], axis=1
    ).reshape(1, 32) - 1

    level = row - 32 * side
    base = jnp.where((level >= -1) & (level <= 31), pos * 40 + 8 + level, 0)
    keep, send = deposit(base, col, fy, fx, amount.reshape(1, 16384))
    dep = (keep.astype(F32) + swap_cores(send).astype(F32)).astype(BF)
    returned = spread(dep)
    spec, dep = lax.optimization_barrier((spec, dep))

    outgoing = stream_recv(entries, spec)
    outgoing, dye = lax.optimization_barrier((outgoing, dye))
    own = spread(outgoing)
    front = dye_send(entries, dye, returned)
    own, front = lax.optimization_barrier((own, front))
    other = swap_cores(own)
    front = spread(front.reshape(128, 2, 32, 128)).reshape(256, 32, 128)

    speed = gather(pos * 64 + row, own, other, col, fy, fx).reshape(2, 8192)
    speed, front = lax.optimization_barrier((speed, front))
    mine = speed[0]
    back = swap_chips(speed[1])
    velocity = jnp.stack([jnp.where(side == 0, mine, back), jnp.where(side == 0, back, mine)])
    dye_hat = dye_recv(front)
    return (velocity, dye_hat)


def solution(mesh):
    return jax.shard_map(
        shards,
        mesh=mesh,
        in_specs=(
            P(None, AXES, None),
            P(AXES, None),
            P(AXES),
            P(AXES),
            P(AXES),
            P(None, AXES),
            P(AXES),
            P(),
        ),
        out_specs=(P(None, AXES), P(None, AXES, None)),
        check_vma=False,
    )
```

```python
import numpy as np, math

import jax, jax.numpy as jnp
from jax import lax
from jax.sharding import PartitionSpec as P
from jax.experimental import pallas as pl
from jax.experimental.pallas import tpu as pltpu

BF = jnp.bfloat16
F32 = jnp.float32
NT = (((1,), (1,)), ((), ()))
PAD = 72
PAD2 = 136
PAD3 = 40


def cs(num, den, sign):
    ang = sign * 2.0 * math.pi * (num % den) / den
    return np.cos(ang), np.sin(ang)


def cplx(c, s):
    return np.stack([np.stack([c, -s]), np.stack([s, c])])


def bf(x):
    return np.asarray(x, np.float32).astype(jnp.bfloat16)


def send_tables(sign, stream):
    p = np.arange(64)
    q = np.arange(128)
    c, s = cs(p[:, None] * p[None, :], 64, sign)
    w = cplx(c, s).transpose(0, 2, 1, 3)
    if stream:
        a = w.reshape(128, 128)
        signed = np.where(p >= 32, p - 64, p) * 128.0
        b = (w * signed).reshape(128, 128)
        g = np.concatenate([a, b])
    else:
        g = w[:, :, 0, :].reshape(128, 64)
    tc, ts = cs(p[:, None] * q[None, :], 8192, sign)
    c, s = cs(q[:, None] * q[None, :], 128, sign)
    w2 = cplx(c, s).transpose(2, 0, 1, 3).reshape(256, 256)
    return bf(g), np.float32(tc), np.float32(ts), bf(w2)


def recv_tables(sign, stream):
    k = np.arange(128)
    r = np.arange(64)
    c, s = cs(k[:, None] * k[None, :], 128, sign)
    w1 = cplx(c, s).transpose(0, 2, 3, 1).reshape(256, 256)
    tc, ts = cs(k[:, None] * r[None, :], 8192, sign)
    tc = np.concatenate([tc, tc], 1)
    ts = np.concatenate([ts, ts], 1)
    c, s = cs(r[:, None] * r[None, :], 64, sign)
    w = cplx(c, s)
    v = np.zeros((2, 2, 64, 2, 2, 64))
    for e in range(2):
        v[:, e, :, :, e, :] = w.transpose(0, 2, 1, 3)
    if stream:
        v = v[0].reshape(128, 256)
    else:
        v = v.reshape(256, 256) / 8192.0
    return bf(w1), np.float32(tc), np.float32(ts), bf(v)


def stream_send_kernel(wa_ref, s_ref, g_ref, tc_ref, ts_ref, w2_ref, o_ref, xs, tre, tim, of):
    def load(p, carry):
        at = pl.multiple_of(p * 128, 128)
        for c in range(2):
            row = pl.multiple_of((c * 64 + p) * PAD, 8)
            xs[pl.ds(row, 64), :] = s_ref[c, :, pl.ds(at, 128)].astype(F32)
        return carry

    lax.fori_loop(0, 64, load, 0, unroll=4)
    q = lax.broadcasted_iota(jnp.int32, (64, 128), 1).astype(F32)

    def rows(n, carry):
        x = jnp.concatenate([xs[pl.ds(2 * n + h, 128, stride=PAD), :].astype(BF) for h in range(2)], axis=1)
        both = jnp.dot(g_ref[...], x, preferred_element_type=F32)
        tc = tc_ref[...]
        ts = ts_ref[...]
        for h in range(2):
            r = 2 * n + h
            z = both[:, h * 128 : h * 128 + 128]
            are, aim, bre, bim = z[:64], z[64:128], z[128:192], z[192:]
            ure = bre + q * are
            uim = bim + q * aim
            wa = wa_ref[0, r]
            base = pl.multiple_of(r * PAD2, 8)
            vre = are * tc - aim * ts
            vim = are * ts + aim * tc
            tre[pl.ds(base, 64), :] = ure * ts + uim * tc
            tim[pl.ds(base, 64), :] = uim * ts - ure * tc
            tre[pl.ds(base + 64, 64), :] = -wa * vim
            tim[pl.ds(base + 64, 64), :] = wa * vre
        return carry

    lax.fori_loop(0, 32, rows, 0, unroll=8)

    def cols(n, carry):
        parts = []
        for h in range(2):
            for f in range(2):
                at = pl.ds(f * 64 + 2 * n + h, 64, stride=PAD2)
                parts.append(jnp.concatenate([tre[at, :].astype(BF), tim[at, :].astype(BF)], axis=1))
        m = jnp.concatenate(parts, axis=0)
        out = lax.dot_general(w2_ref[...], m, NT, preferred_element_type=F32)
        for h in range(2):
            of[pl.ds(2 * n + h, 256, stride=PAD), :] = out[:, h * 128 : h * 128 + 128]
        return carry

    lax.fori_loop(0, 32, cols, 0, unroll=8)

    def store(i, carry):
        o_ref[i] = of[pl.ds(pl.multiple_of(i * PAD, 8), 64), :].astype(BF)
        return carry

    lax.fori_loop(0, 256, store, 0, unroll=8)


VM = pl.BlockSpec(memory_space=pltpu.VMEM)
SM = pl.BlockSpec(memory_space=pltpu.SMEM)


def call(kernel, outs, specs, scratch, cost, mib, name, *args):
    return pl.pallas_call(
        kernel,
        out_shape=outs,
        in_specs=specs,
        out_specs=jax.tree.map(lambda _: VM, outs),
        scratch_shapes=scratch,
        compiler_params=pltpu.CompilerParams(vmem_limit_bytes=mib << 20),
        cost_estimate=pl.CostEstimate(flops=cost, bytes_accessed=1 << 20, transcendentals=0),
        name=name,
    )(*args)


def stream_send(stream, wa):
    return call(
        stream_send_kernel,
        jax.ShapeDtypeStruct((256, 64, 128), BF),
        [SM] + [VM] * 5,
        [pltpu.VMEM((128 * PAD, 128), F32)] + [pltpu.VMEM((64 * PAD2, 128), F32)] * 2
        + [pltpu.VMEM((256 * PAD, 128), F32)],
        int(6e9), 60, "stream_send",
        wa, stream, *send_tables(1.0, True),
    )


def stream_recv_kernel(idx_ref, x_ref, w1_ref, tc_ref, ts_ref, v_ref, o_ref, xf, of):
    def load(i, carry):
        xf[pl.ds(pl.multiple_of(i * PAD, 8), 64), :] = x_ref[i].astype(F32)
        return carry

    lax.fori_loop(0, 256, load, 0, unroll=8)

    def step(n, carry):
        d = jnp.concatenate([xf[pl.ds(2 * n + h, 256, stride=PAD), :].astype(BF) for h in range(2)], axis=1)
        z = jnp.dot(w1_ref[...], d, preferred_element_type=F32)
        tc = tc_ref[...]
        ts = ts_ref[...]
        parts = []
        for h in range(2):
            re = z[:128, h * 128 : h * 128 + 128]
            im = z[128:, h * 128 : h * 128 + 128]
            parts.append(
                jnp.concatenate([(re * tc - im * ts).astype(BF), (re * ts + im * tc).astype(BF)], axis=1)
            )
        m = jnp.concatenate(parts, axis=0)
        out = lax.dot_general(v_ref[...], m, NT, preferred_element_type=F32)
        for h in range(2):
            for f in range(2):
                of[pl.ds(64 * f + 2 * n + h, 64, stride=PAD2), :] = out[f * 64 : f * 64 + 64, h * 128 : h * 128 + 128]
        return carry

    lax.fori_loop(0, 32, step, 0, unroll=8)

    def store(n, carry):
        tile = jnp.maximum(idx_ref[0, n], 0)
        for f in range(2):
            data = of[pl.ds(pl.multiple_of(tile * PAD2, 8) + 64 * f, 64), :].astype(BF)
            for x in range(2):
                o_ref[n // 2 * 8 + 4 * x + 2 * f + n % 2] = data
        return carry

    lax.fori_loop(0, 32, store, 0, unroll=2)


def stream_recv(idx, x):
    return call(
        stream_recv_kernel,
        jax.ShapeDtypeStruct((128, 64, 128), BF),
        [SM] + [VM] * 5,
        [pltpu.VMEM((256 * PAD, 128), F32), pltpu.VMEM((64 * PAD2, 128), F32)],
        int(6e9), 28, "stream_recv",
        idx, x, *recv_tables(1.0, True),
    )


def dye_send_kernel(idx_ref, dye_ref, ret_ref, g_ref, tc_ref, ts_ref, w2_ref, o_ref, xs, tre, tim, of):
    def load(p, carry):
        at = pl.multiple_of(p * 128, 128)
        xs[pl.ds(pl.multiple_of(p * PAD, 8), 64), :] = dye_ref[:, pl.ds(at, 128)].astype(F32)
        return carry

    lax.fori_loop(0, 64, load, 0, unroll=4)

    def place(n, carry):
        tile = idx_ref[0, n]

        @pl.when(tile >= 0)
        def _():
            g = n // 2
            e = n % 2
            for half in range(2):
                at = pl.ds(pl.multiple_of(tile * PAD, 8) + 32 * half, 32)
                total = xs[at, :]
                for x in range(2):
                    total = total + ret_ref[g * 8 + 4 * x + 2 * half + e].astype(F32)
                xs[at, :] = total

        return carry

    lax.fori_loop(0, 32, place, 0)

    def rows(n, carry):
        x = jnp.concatenate([xs[pl.ds(4 * n + h, 64, stride=PAD), :].astype(BF) for h in range(4)], axis=1)
        z = jnp.dot(g_ref[...], x, preferred_element_type=F32)
        tc = tc_ref[...]
        ts = ts_ref[...]
        for h in range(4):
            re = z[:64, h * 128 : h * 128 + 128]
            im = z[64:, h * 128 : h * 128 + 128]
            base = pl.multiple_of((4 * n + h) * PAD, 8)
            tre[pl.ds(base, 64), :] = re * tc - im * ts
            tim[pl.ds(base, 64), :] = re * ts + im * tc
        return carry

    lax.fori_loop(0, 16, rows, 0, unroll=8)

    def cols(n, carry):
        parts = []
        for e in range(4):
            at = pl.ds(4 * n + e, 64, stride=PAD)
            parts.append(jnp.concatenate([tre[at, :].astype(BF), tim[at, :].astype(BF)], axis=1))
        m = jnp.concatenate(parts, axis=0)
        out = lax.dot_general(w2_ref[...], m, NT, preferred_element_type=F32)
        for h in range(2):
            of[pl.ds(2 * n + h, 256, stride=PAD3), :] = out[:, h * 128 : h * 128 + 128]
        return carry

    lax.fori_loop(0, 16, cols, 0, unroll=8)

    def store(i, carry):
        o_ref[i] = of[pl.ds(pl.multiple_of(i * PAD3, 8), 32), :].astype(BF)
        return carry

    lax.fori_loop(0, 256, store, 0, unroll=8)


def dye_send(idx, dye, ret):
    return call(
        dye_send_kernel,
        jax.ShapeDtypeStruct((256, 32, 128), BF),
        [SM] + [VM] * 6,
        [pltpu.VMEM((64 * PAD, 128), F32)] * 3 + [pltpu.VMEM((256 * PAD3, 128), F32)],
        int(4e9), 24, "dye_send",
        idx, dye, ret, *send_tables(-1.0, False),
    )


def dye_recv_kernel(x_ref, w1_ref, tc_ref, ts_ref, v_ref, o_ref, xf, of):
    def load(i, carry):
        xf[pl.ds(pl.multiple_of(i * PAD3, 8), 32), :] = x_ref[i].astype(F32)
        return carry

    lax.fori_loop(0, 256, load, 0, unroll=8)

    def step(n, carry):
        d = jnp.concatenate([xf[pl.ds(2 * n + h, 256, stride=PAD3), :].astype(BF) for h in range(2)], axis=1)
        z = jnp.dot(w1_ref[...], d, preferred_element_type=F32)
        tc = tc_ref[...]
        ts = ts_ref[...]
        parts = []
        for h in range(2):
            re = z[:128, h * 128 : h * 128 + 128]
            im = z[128:, h * 128 : h * 128 + 128]
            parts.append(
                jnp.concatenate([(re * tc - im * ts).astype(BF), (re * ts + im * tc).astype(BF)], axis=1)
            )
        m = jnp.concatenate(parts, axis=0)
        out = lax.dot_general(v_ref[...], m, NT, preferred_element_type=F32)
        for h in range(2):
            for c in range(2):
                for e in range(2):
                    row = c * 4096 + (n // 2) * 512 + (4 * n + 2 * h + e) % 8
                    of[pl.ds(row, 64, stride=8), :] = out[
                        (2 * c + e) * 64 : (2 * c + e) * 64 + 64, h * 128 : h * 128 + 128
                    ]
        return carry

    lax.fori_loop(0, 16, step, 0, unroll=8)

    def store(n, carry):
        c = n // 8
        t8 = n % 8
        base = pl.multiple_of(n * 512, 512)
        at = pl.ds(pl.multiple_of(t8 * 8, 8), 8)
        for j in range(64):
            o_ref[c, at, j * 128 : j * 128 + 128] = of[pl.ds(base + j * 8, 8), :]
        return carry

    lax.fori_loop(0, 16, store, 0)


def dye_recv(x):
    return call(
        dye_recv_kernel,
        jax.ShapeDtypeStruct((2, 64, 8192), F32),
        [VM] * 5,
        [pltpu.VMEM((256 * PAD3, 128), F32), pltpu.VMEM((8192, 128), F32)],
        int(4e9), 20, "dye_recv",
        x, *recv_tables(-1.0, False),
    )

CAPO = 2


def deposit_kernel(idx_ref, col_ref, fy_ref, fx_ref, am_ref, keep_ref, send_ref, *refs):
    bufs = refs[:4]
    accs = refs[4:]
    ways = len(accs)

    def clear(i, carry):
        for acc in accs:
            acc[pl.ds(pl.multiple_of(i * 40, 8), 40), :] = jnp.zeros((40, 128), F32)
        return carry

    lax.fori_loop(0, 257, clear, 0)

    def weights(n, dst):
        xs = lax.broadcasted_iota(jnp.int32, (128, 128), 0)
        rows = lax.broadcasted_iota(jnp.int32, (256, 128), 0)
        off = rows // 2 - lax.broadcasted_iota(jnp.int32, (256, 128), 1)
        odd = rows % 2 == 1
        at = pl.ds(pl.multiple_of(n * 128, 128), 128)
        fx = fx_ref[:, at]
        am = am_ref[:, at]
        hi = am * fy_ref[:, at]
        lo = am - hi
        d = xs - col_ref[:, at]
        w = jnp.where(d == 0, 1.0 - fx, jnp.where(d == 1, fx, 0.0)).astype(BF)
        e = jnp.where(off == 0, jnp.where(odd, hi, lo), 0.0).astype(BF)
        dst[...] = lax.dot_general(e, w, NT, preferred_element_type=F32)

    def add(n, src):
        for f in range(0, 128, ways):
            at = [pl.ds(idx_ref[n, f + k], 2) for k in range(ways)]
            new = [accs[k][at[k], :] + src[2 * (f + k) : 2 * (f + k) + 2, :] for k in range(ways)]
            for k in range(ways):
                accs[k][at[k], :] = new[k]

    weights(0, bufs[0])

    def chunk(n, carry):
        for q in range(4):
            weights(jnp.minimum(4 * n + q + 1, 127), bufs[(q + 1) % 4])
            add(4 * n + q, bufs[q])
        return carry

    lax.fori_loop(0, 32, chunk, 0)

    def store(i, carry):
        for ref, base in ((keep_ref, 8), (send_ref, 128 * 40 + 8)):
            at = pl.ds(pl.multiple_of(i * 40 + base, 8), 32)
            total = accs[0][at, :]
            for acc in accs[1:]:
                total = total + acc[at, :]
            ref[i] = total.astype(BF)
        return carry

    lax.fori_loop(0, 128, store, 0, unroll=2)


def deposit(idx, col, fy, fx, am):
    return call(
        deposit_kernel,
        [jax.ShapeDtypeStruct((128, 32, 128), BF)] * 2,
        [SM] + [VM] * 4,
        [pltpu.VMEM((256, 128), F32)] * 4 + [pltpu.VMEM((257 * 40, 128), F32)] * 4,
        int(2e10), 30, "deposit",
        idx, col, fy, fx, am,
    )


def gather_kernel(base_ref, a_ref, b_ref, col_ref, fy_ref, fx_ref, mine_ref, theirs_ref, st, *bufs):
    def load(i, carry):
        at = pl.multiple_of(i * 64, 64)
        st[pl.ds(at, 64), :] = a_ref[i].astype(F32)
        st[pl.ds(at + 8192, 64), :] = b_ref[i].astype(F32)
        return carry

    lax.fori_loop(0, 128, load, 0, unroll=4)

    def fetch(n, g):
        for f in range(128):
            g[f * 2 : f * 2 + 2, :] = st[pl.ds(base_ref[n, f], 2), :]

    def mix(n, g, o_ref, to):
        sub = lax.broadcasted_iota(jnp.int32, (8, 128), 0)
        off = lax.broadcasted_iota(jnp.int32, (8, 128), 1) - sub // 2
        xs = lax.broadcasted_iota(jnp.int32, (128, 128), 0)
        at = pl.ds(pl.multiple_of(n * 128, 128), 128)
        col = col_ref[:, at]
        fy = fy_ref[:, at]
        fx = fx_ref[:, at]
        d = xs - col
        w = jnp.where(d == 0, 1.0 - fx, jnp.where(d == 1, fx, 0.0))
        hi = w.astype(BF)
        lo = (w - hi.astype(F32)).astype(BF)
        rows = g[...].astype(BF)
        z = jnp.dot(
            jnp.concatenate([rows, rows], axis=1),
            jnp.concatenate([hi, lo], axis=0),
            preferred_element_type=F32,
        )
        parts = [jnp.zeros((8, 128), F32) for _ in range(4)]
        for i in range(32):
            parts[i % 4] = jnp.where(off == 4 * i, z[8 * i : 8 * i + 8], parts[i % 4])
        total = (parts[0] + parts[1] + (parts[2] + parts[3])) * jnp.where(sub % 2 == 1, fy, 1.0 - fy)
        o_ref[:, pl.ds(pl.multiple_of(to * 128, 128), 128)] = jnp.sum(total, axis=0, keepdims=True)

    fetch(0, bufs[0])
    for half, o_ref in enumerate((mine_ref, theirs_ref)):

        def chunk(n, carry, half=half, o_ref=o_ref):
            for q in range(8):
                at = half * 64 + 8 * n + q
                fetch(jnp.minimum(at + 1, 127), bufs[(q + 1) % 8])
                mix(at, bufs[q], o_ref, 8 * n + q)
            return carry

        lax.fori_loop(0, 8, chunk, 0)


def gather(base, a, b, col, fy, fx):
    return call(
        gather_kernel,
        [jax.ShapeDtypeStruct((1, 8192), F32)] * 2,
        [SM] + [VM] * 5,
        [pltpu.VMEM((16384, 128), F32)] + [pltpu.VMEM((256, 128), F32)] * 8,
        int(1e10), 20, "gather",
        base, a, b, col, fy, fx,
    )


AXES = ("wide", "narrow")


def spread(blocks):
    return lax.all_to_all(blocks, AXES, split_axis=0, concat_axis=0, tiled=True)


def swap_cores(x):
    n = lax.axis_size("narrow")
    return lax.ppermute(x, "narrow", [(i, i ^ 1) for i in range(n)])


def swap_chips(x):
    n = lax.axis_size("narrow")
    return lax.ppermute(x, "narrow", [(i, i ^ 2) for i in range(n)])


def shards(stream_hat, dye, float_slot, float_row, float_col, float_frac, float_dye, tile_lists):
    device = lax.axis_index(AXES)
    group = lax.axis_index("wide")
    core = lax.axis_index("narrow") % 2
    side = lax.axis_index("narrow") // 2 % 2
    wave = device * 64 + jnp.arange(64)
    wave = jnp.where(wave >= 4096, wave - 8192, wave).astype(F32)[None]

    own_floats = jnp.concatenate(
        [jnp.stack([float_slot, float_row, float_col]).astype(F32), float_frac, float_dye[None]]
    )
    their_floats = swap_chips(own_floats)
    spec = stream_send(stream_hat, wave)
    spec, own_floats, their_floats, tile_lists = lax.optimization_barrier(
        (spec, own_floats, their_floats, tile_lists)
    )
    spec = spread(spec.reshape(128, 2, 64, 128)).reshape(256, 64, 128)
    floats = jnp.concatenate([own_floats, their_floats], axis=1)
    slot = floats[0].astype(jnp.int32).reshape(128, 128)
    row = floats[1].astype(jnp.int32).reshape(128, 128)
    col = floats[2:3].astype(jnp.int32)
    fy = floats[3:4]
    fx = floats[4:5]
    amount = floats[5:6]

    own_list = lax.dynamic_index_in_dim(tile_lists, group, 0, keepdims=False)
    holder = own_list // 64
    before = jnp.arange(256)[:, None] > jnp.arange(256)[None, :]
    rank = jnp.sum((before & (holder[:, None] == holder[None, :])).astype(jnp.int32), axis=1)
    position = jnp.where(own_list >= 0, jnp.where(rank == core, 0, 128) + holder, 0)
    pos = jnp.sum(
        jnp.where(jnp.arange(256)[:, None, None] == slot[None], position[:, None, None], 0), axis=0
    )

    mine = (tile_lists >= 0) & (tile_lists // 64 == device)
    place = jnp.cumsum(mine.astype(jnp.int32), axis=1) - 1
    local = tile_lists % 64 + 1
    entries = jnp.stack(
        [jnp.sum(jnp.where(mine & (place == e), local, 0), axis=1) for e in range(CAPO)], axis=1
    ).reshape(1, 32) - 1

    level = row - 32 * side
    base = jnp.where((level >= -1) & (level <= 31), pos * 40 + 8 + level, 0)
    keep, send = deposit(base, col, fy, fx, amount)
    dep = (keep.astype(F32) + swap_cores(send).astype(F32)).astype(BF)
    returned = spread(dep)
    spec, dep = lax.optimization_barrier((spec, dep))

    outgoing = stream_recv(entries, spec)
    outgoing, dye = lax.optimization_barrier((outgoing, dye))
    own = spread(outgoing)
    front = dye_send(entries, dye, returned)
    own, front = lax.optimization_barrier((own, front))
    other = swap_cores(own)
    front = spread(front.reshape(128, 2, 32, 128)).reshape(256, 32, 128)

    mine, theirs = gather(pos * 64 + row, own, other, col, fy, fx)
    mine, theirs, front = lax.optimization_barrier((mine, theirs, front))
    back = swap_chips(theirs)
    velocity = jnp.where(side == 0, jnp.concatenate([mine, back]), jnp.concatenate([back, mine]))
    dye_hat = dye_recv(front)
    return (velocity, dye_hat)


def solution(mesh):
    return jax.shard_map(
        shards,
        mesh=mesh,
        in_specs=(
            P(None, AXES, None),
            P(AXES, None),
            P(AXES),
            P(AXES),
            P(AXES),
            P(None, AXES),
            P(AXES),
            P(),
        ),
        out_specs=(P(None, AXES), P(None, AXES, None)),
        check_vma=False,
    )
```

```python
import numpy as np, math

import jax, jax.numpy as jnp
from jax import lax
from jax.sharding import PartitionSpec as P
from jax.experimental import pallas as pl
from jax.experimental.pallas import tpu as pltpu

BF = jnp.bfloat16
F32 = jnp.float32
NT = (((1,), (1,)), ((), ()))
PAD = 72
PAD2 = 136
PAD3 = 40


def cs(num, den, sign):
    ang = sign * 2.0 * math.pi * (num % den) / den
    return np.cos(ang), np.sin(ang)


def cplx(c, s):
    return np.stack([np.stack([c, -s]), np.stack([s, c])])


def bf(x):
    return np.asarray(x, np.float32).astype(jnp.bfloat16)


def send_tables(sign, stream):
    p = np.arange(64)
    q = np.arange(128)
    c, s = cs(p[:, None] * p[None, :], 64, sign)
    w = cplx(c, s).transpose(0, 2, 1, 3)
    if stream:
        a = w.reshape(128, 128)
        signed = np.where(p >= 32, p - 64, p) * 128.0
        b = (w * signed).reshape(128, 128)
        g = np.concatenate([a, b])
    else:
        g = w[:, :, 0, :].reshape(128, 64)
    tc, ts = cs(p[:, None] * q[None, :], 8192, sign)
    c, s = cs(q[:, None] * q[None, :], 128, sign)
    w2 = cplx(c, s).transpose(2, 0, 1, 3).reshape(256, 256)
    return bf(g), np.float32(tc), np.float32(ts), bf(w2)


def recv_tables(sign, stream):
    k = np.arange(128)
    r = np.arange(64)
    c, s = cs(k[:, None] * k[None, :], 128, sign)
    w1 = cplx(c, s).transpose(0, 2, 3, 1).reshape(256, 256)
    tc, ts = cs(k[:, None] * r[None, :], 8192, sign)
    tc = np.concatenate([tc, tc], 1)
    ts = np.concatenate([ts, ts], 1)
    c, s = cs(r[:, None] * r[None, :], 64, sign)
    w = cplx(c, s)
    v = np.zeros((2, 2, 64, 2, 2, 64))
    for e in range(2):
        v[:, e, :, :, e, :] = w.transpose(0, 2, 1, 3)
    if stream:
        v = v[0].reshape(128, 256)
    else:
        v = v.reshape(256, 256) / 8192.0
    return bf(w1), np.float32(tc), np.float32(ts), bf(v)


def stream_send_kernel(
    wa_ref, slot_ref, row_ref, col_ref, frac_ref, amount_ref, g_ref, tc_ref, ts_ref, w2_ref, s_hbm,
    floats_ref, o_hbm, s_ref, xs, tre, tim, of, o_ref, in_sem, out_sem,
):
    reads = []
    for k in range(4):
        lanes = pl.ds(2048 * k, 2048)
        reads.append(
            pltpu.make_async_copy(s_hbm.at[:, :, lanes], s_ref.at[:, :, lanes], in_sem.at[k])
        )
        reads[k].start()
    floats_ref[0:1, :] = slot_ref[...].astype(F32)
    floats_ref[1:2, :] = row_ref[...].astype(F32)
    floats_ref[2:3, :] = col_ref[...].astype(F32)
    floats_ref[3:5, :] = frac_ref[...]
    floats_ref[5:6, :] = amount_ref[...]

    def load(p, carry):
        at = pl.multiple_of(p * 128, 128)
        for c in range(2):
            row = pl.multiple_of((c * 64 + p) * PAD, 8)
            xs[pl.ds(row, 64), :] = s_ref[c, :, pl.ds(at, 128)].astype(F32)
        return carry

    for k in range(4):
        reads[k].wait()
        lax.fori_loop(16 * k, 16 * k + 16, load, 0, unroll=4)
    q = lax.broadcasted_iota(jnp.int32, (64, 128), 1).astype(F32)

    def rows(n, carry):
        x = jnp.concatenate([xs[pl.ds(2 * n + h, 128, stride=PAD), :].astype(BF) for h in range(2)], axis=1)
        both = jnp.dot(g_ref[...], x, preferred_element_type=F32)
        tc = tc_ref[...]
        ts = ts_ref[...]
        for h in range(2):
            r = 2 * n + h
            z = both[:, h * 128 : h * 128 + 128]
            are, aim, bre, bim = z[:64], z[64:128], z[128:192], z[192:]
            ure = bre + q * are
            uim = bim + q * aim
            wa = wa_ref[0, r]
            base = pl.multiple_of(r * PAD2, 8)
            vre = are * tc - aim * ts
            vim = are * ts + aim * tc
            tre[pl.ds(base, 64), :] = ure * ts + uim * tc
            tim[pl.ds(base, 64), :] = uim * ts - ure * tc
            tre[pl.ds(base + 64, 64), :] = -wa * vim
            tim[pl.ds(base + 64, 64), :] = wa * vre
        return carry

    lax.fori_loop(0, 32, rows, 0, unroll=8)

    def cols(n, carry):
        parts = []
        for h in range(2):
            for f in range(2):
                at = pl.ds(f * 64 + 2 * n + h, 64, stride=PAD2)
                parts.append(jnp.concatenate([tre[at, :].astype(BF), tim[at, :].astype(BF)], axis=1))
        m = jnp.concatenate(parts, axis=0)
        out = lax.dot_general(w2_ref[...], m, NT, preferred_element_type=F32)
        for h in range(2):
            of[pl.ds(2 * n + h, 256, stride=PAD), :] = out[:, h * 128 : h * 128 + 128]
        return carry

    writes = []
    for k in range(4):
        lax.fori_loop(8 * k, 8 * k + 8, cols, 0, unroll=8)

        def store(i, carry, k=k):
            o_ref[i, 16 * k : 16 * k + 16] = of[pl.ds(pl.multiple_of(i * PAD + 16 * k, 8), 16), :].astype(BF)
            return carry

        lax.fori_loop(0, 256, store, 0, unroll=8)
        levels = pl.ds(16 * k, 16)
        writes.append(pltpu.make_async_copy(o_ref.at[:, levels, :], o_hbm.at[:, levels, :], out_sem.at[k]))
        writes[k].start()
    for write in writes:
        write.wait()


VM = pl.BlockSpec(memory_space=pltpu.VMEM)
SM = pl.BlockSpec(memory_space=pltpu.SMEM)
HB = pl.BlockSpec(memory_space=pl.ANY)


def call(kernel, outs, specs, scratch, cost, mib, name, *args, out_specs=None):
    return pl.pallas_call(
        kernel,
        out_shape=outs,
        in_specs=specs,
        out_specs=out_specs or jax.tree.map(lambda _: VM, outs),
        scratch_shapes=scratch,
        compiler_params=pltpu.CompilerParams(vmem_limit_bytes=mib << 20),
        cost_estimate=pl.CostEstimate(flops=cost, bytes_accessed=1 << 20, transcendentals=0),
        name=name,
    )(*args)


def stream_send(stream, wa, floats):
    return call(
        stream_send_kernel,
        [jax.ShapeDtypeStruct((6, 8192), F32), jax.ShapeDtypeStruct((256, 64, 128), BF)],
        [SM] + [VM] * 9 + [HB],
        [pltpu.VMEM((2, 64, 8192), BF), pltpu.VMEM((128 * PAD, 128), F32)]
        + [pltpu.VMEM((64 * PAD2, 128), F32)] * 2
        + [pltpu.VMEM((256 * PAD, 128), F32), pltpu.VMEM((256, 64, 128), BF)]
        + [pltpu.SemaphoreType.DMA((4,))] * 2,
        int(6e9), 60, "stream_send",
        wa, *floats, *send_tables(1.0, True), stream, out_specs=[VM, HB],
    )


def stream_recv_kernel(idx_ref, x_ref, w1_ref, tc_ref, ts_ref, v_ref, o_ref, xf, of):
    def load(i, carry):
        xf[pl.ds(pl.multiple_of(i * PAD, 8), 64), :] = x_ref[i].astype(F32)
        return carry

    lax.fori_loop(0, 256, load, 0, unroll=8)

    def step(n, carry):
        d = jnp.concatenate([xf[pl.ds(2 * n + h, 256, stride=PAD), :].astype(BF) for h in range(2)], axis=1)
        z = jnp.dot(w1_ref[...], d, preferred_element_type=F32)
        tc = tc_ref[...]
        ts = ts_ref[...]
        parts = []
        for h in range(2):
            re = z[:128, h * 128 : h * 128 + 128]
            im = z[128:, h * 128 : h * 128 + 128]
            parts.append(
                jnp.concatenate([(re * tc - im * ts).astype(BF), (re * ts + im * tc).astype(BF)], axis=1)
            )
        m = jnp.concatenate(parts, axis=0)
        out = lax.dot_general(v_ref[...], m, NT, preferred_element_type=F32)
        for h in range(2):
            for f in range(2):
                of[pl.ds(64 * f + 2 * n + h, 64, stride=PAD2), :] = out[f * 64 : f * 64 + 64, h * 128 : h * 128 + 128]
        return carry

    lax.fori_loop(0, 32, step, 0, unroll=8)

    def store(n, carry):
        tile = jnp.maximum(idx_ref[0, n], 0)
        for f in range(2):
            data = of[pl.ds(pl.multiple_of(tile * PAD2, 8) + 64 * f, 64), :].astype(BF)
            for x in range(2):
                o_ref[n // 2 * 8 + 4 * x + 2 * f + n % 2] = data
        return carry

    lax.fori_loop(0, 32, store, 0, unroll=2)


def stream_recv(idx, x):
    return call(
        stream_recv_kernel,
        jax.ShapeDtypeStruct((128, 64, 128), BF),
        [SM] + [VM] * 5,
        [pltpu.VMEM((256 * PAD, 128), F32), pltpu.VMEM((64 * PAD2, 128), F32)],
        int(6e9), 28, "stream_recv",
        idx, x, *recv_tables(1.0, True),
    )


def dye_send_kernel(idx_ref, dye_ref, ret_ref, g_ref, tc_ref, ts_ref, w2_ref, o_ref, xs, tre, tim, of):
    def load(p, carry):
        at = pl.multiple_of(p * 128, 128)
        xs[pl.ds(pl.multiple_of(p * PAD, 8), 64), :] = dye_ref[:, pl.ds(at, 128)].astype(F32)
        return carry

    lax.fori_loop(0, 64, load, 0, unroll=4)

    def place(n, carry):
        tile = idx_ref[0, n]

        @pl.when(tile >= 0)
        def _():
            g = n // 2
            e = n % 2
            for half in range(2):
                at = pl.ds(pl.multiple_of(tile * PAD, 8) + 32 * half, 32)
                total = xs[at, :]
                for x in range(2):
                    total = total + ret_ref[g * 8 + 4 * x + 2 * half + e].astype(F32)
                xs[at, :] = total

        return carry

    lax.fori_loop(0, 32, place, 0)

    def rows(n, carry):
        x = jnp.concatenate([xs[pl.ds(4 * n + h, 64, stride=PAD), :].astype(BF) for h in range(4)], axis=1)
        z = jnp.dot(g_ref[...], x, preferred_element_type=F32)
        tc = tc_ref[...]
        ts = ts_ref[...]
        for h in range(4):
            re = z[:64, h * 128 : h * 128 + 128]
            im = z[64:, h * 128 : h * 128 + 128]
            base = pl.multiple_of((4 * n + h) * PAD, 8)
            tre[pl.ds(base, 64), :] = re * tc - im * ts
            tim[pl.ds(base, 64), :] = re * ts + im * tc
        return carry

    lax.fori_loop(0, 16, rows, 0, unroll=8)

    def cols(n, carry):
        parts = []
        for e in range(4):
            at = pl.ds(4 * n + e, 64, stride=PAD)
            parts.append(jnp.concatenate([tre[at, :].astype(BF), tim[at, :].astype(BF)], axis=1))
        m = jnp.concatenate(parts, axis=0)
        out = lax.dot_general(w2_ref[...], m, NT, preferred_element_type=F32)
        for h in range(2):
            of[pl.ds(2 * n + h, 256, stride=PAD3), :] = out[:, h * 128 : h * 128 + 128]
        return carry

    lax.fori_loop(0, 16, cols, 0, unroll=8)

    def store(i, carry):
        o_ref[i] = of[pl.ds(pl.multiple_of(i * PAD3, 8), 32), :].astype(BF)
        return carry

    lax.fori_loop(0, 256, store, 0, unroll=8)


def dye_send(idx, dye, ret):
    return call(
        dye_send_kernel,
        jax.ShapeDtypeStruct((256, 32, 128), BF),
        [SM] + [VM] * 6,
        [pltpu.VMEM((64 * PAD, 128), F32)] * 3 + [pltpu.VMEM((256 * PAD3, 128), F32)],
        int(4e9), 24, "dye_send",
        idx, dye, ret, *send_tables(-1.0, False),
    )


def dye_recv_kernel(x_ref, w1_ref, tc_ref, ts_ref, v_ref, o_hbm, xf, of, o_ref, out_sem):
    def load(i, carry):
        xf[pl.ds(pl.multiple_of(i * PAD3, 8), 32), :] = x_ref[i].astype(F32)
        return carry

    lax.fori_loop(0, 256, load, 0, unroll=8)

    def step(n, carry):
        d = jnp.concatenate([xf[pl.ds(2 * n + h, 256, stride=PAD3), :].astype(BF) for h in range(2)], axis=1)
        z = jnp.dot(w1_ref[...], d, preferred_element_type=F32)
        tc = tc_ref[...]
        ts = ts_ref[...]
        parts = []
        for h in range(2):
            re = z[:128, h * 128 : h * 128 + 128]
            im = z[128:, h * 128 : h * 128 + 128]
            parts.append(
                jnp.concatenate([(re * tc - im * ts).astype(BF), (re * ts + im * tc).astype(BF)], axis=1)
            )
        m = jnp.concatenate(parts, axis=0)
        out = lax.dot_general(v_ref[...], m, NT, preferred_element_type=F32)
        for h in range(2):
            for c in range(2):
                for e in range(2):
                    row = c * 4096 + (n // 2) * 512 + (4 * n + 2 * h + e) % 8
                    of[pl.ds(row, 64, stride=8), :] = out[
                        (2 * c + e) * 64 : (2 * c + e) * 64 + 64, h * 128 : h * 128 + 128
                    ]
        return carry

    writes = []
    for k in range(8):
        for n in range(2 * k, 2 * k + 2):
            step(n, 0)
        at = pl.ds(8 * k, 8)
        for c in range(2):
            for j in range(64):
                o_ref[c, at, j * 128 : j * 128 + 128] = of[pl.ds(c * 4096 + k * 512 + j * 8, 8), :]
        writes.append(pltpu.make_async_copy(o_ref.at[:, at, :], o_hbm.at[:, at, :], out_sem.at[k]))
        writes[k].start()
    for write in writes:
        write.wait()


def dye_recv(x):
    return call(
        dye_recv_kernel,
        jax.ShapeDtypeStruct((2, 64, 8192), F32),
        [VM] * 5,
        [pltpu.VMEM((256 * PAD3, 128), F32), pltpu.VMEM((8192, 128), F32)]
        + [pltpu.VMEM((2, 64, 8192), F32), pltpu.SemaphoreType.DMA((8,))],
        int(4e9), 20, "dye_recv",
        x, *recv_tables(-1.0, False), out_specs=HB,
    )

CAPO = 2


def deposit_kernel(idx_ref, col_ref, fy_ref, fx_ref, am_ref, keep_ref, send_ref, *refs):
    bufs = refs[:4]
    accs = refs[4:]
    ways = len(accs)

    def clear(i, carry):
        for acc in accs:
            acc[pl.ds(pl.multiple_of(i * 40, 8), 40), :] = jnp.zeros((40, 128), F32)
        return carry

    lax.fori_loop(0, 257, clear, 0)

    def weights(n, dst):
        xs = lax.broadcasted_iota(jnp.int32, (128, 128), 0)
        rows = lax.broadcasted_iota(jnp.int32, (256, 128), 0)
        off = rows // 2 - lax.broadcasted_iota(jnp.int32, (256, 128), 1)
        odd = rows % 2 == 1
        at = pl.ds(pl.multiple_of(n * 128, 128), 128)
        fx = fx_ref[:, at]
        am = am_ref[:, at]
        hi = am * fy_ref[:, at]
        lo = am - hi
        d = xs - col_ref[:, at]
        w = jnp.where(d == 0, 1.0 - fx, jnp.where(d == 1, fx, 0.0)).astype(BF)
        e = jnp.where(off == 0, jnp.where(odd, hi, lo), 0.0).astype(BF)
        dst[...] = lax.dot_general(e, w, NT, preferred_element_type=F32)

    def add(n, src):
        for f in range(0, 128, ways):
            at = [pl.ds(idx_ref[n, f + k], 2) for k in range(ways)]
            new = [accs[k][at[k], :] + src[2 * (f + k) : 2 * (f + k) + 2, :] for k in range(ways)]
            for k in range(ways):
                accs[k][at[k], :] = new[k]

    weights(0, bufs[0])

    def chunk(n, carry):
        for q in range(4):
            weights(jnp.minimum(4 * n + q + 1, 127), bufs[(q + 1) % 4])
            add(4 * n + q, bufs[q])
        return carry

    lax.fori_loop(0, 32, chunk, 0)

    def store(i, carry):
        for ref, base in ((keep_ref, 8), (send_ref, 128 * 40 + 8)):
            at = pl.ds(pl.multiple_of(i * 40 + base, 8), 32)
            total = accs[0][at, :]
            for acc in accs[1:]:
                total = total + acc[at, :]
            ref[i] = total.astype(BF)
        return carry

    lax.fori_loop(0, 128, store, 0, unroll=2)


def deposit(idx, col, fy, fx, am):
    return call(
        deposit_kernel,
        [jax.ShapeDtypeStruct((128, 32, 128), BF)] * 2,
        [SM] + [VM] * 4,
        [pltpu.VMEM((256, 128), F32)] * 4 + [pltpu.VMEM((257 * 40, 128), F32)] * 4,
        int(2e10), 30, "deposit",
        idx, col, fy, fx, am,
    )


def gather_kernel(base_ref, a_ref, b_ref, col_ref, fy_ref, fx_ref, mine_ref, theirs_ref, st, *bufs):
    def load(i, carry):
        at = pl.multiple_of(i * 64, 64)
        st[pl.ds(at, 64), :] = a_ref[i].astype(F32)
        st[pl.ds(at + 8192, 64), :] = b_ref[i].astype(F32)
        return carry

    lax.fori_loop(0, 128, load, 0, unroll=4)

    def fetch(n, g):
        for f in range(128):
            g[f * 2 : f * 2 + 2, :] = st[pl.ds(base_ref[n, f], 2), :]

    def mix(n, g, o_ref, to):
        sub = lax.broadcasted_iota(jnp.int32, (8, 128), 0)
        off = lax.broadcasted_iota(jnp.int32, (8, 128), 1) - sub // 2
        xs = lax.broadcasted_iota(jnp.int32, (128, 128), 0)
        at = pl.ds(pl.multiple_of(n * 128, 128), 128)
        col = col_ref[:, at]
        fy = fy_ref[:, at]
        fx = fx_ref[:, at]
        d = xs - col
        w = jnp.where(d == 0, 1.0 - fx, jnp.where(d == 1, fx, 0.0))
        hi = w.astype(BF)
        lo = (w - hi.astype(F32)).astype(BF)
        rows = g[...].astype(BF)
        z = jnp.dot(
            jnp.concatenate([rows, rows], axis=1),
            jnp.concatenate([hi, lo], axis=0),
            preferred_element_type=F32,
        )
        parts = [jnp.zeros((8, 128), F32) for _ in range(4)]
        for i in range(32):
            parts[i % 4] = jnp.where(off == 4 * i, z[8 * i : 8 * i + 8], parts[i % 4])
        total = (parts[0] + parts[1] + (parts[2] + parts[3])) * jnp.where(sub % 2 == 1, fy, 1.0 - fy)
        o_ref[:, pl.ds(pl.multiple_of(to * 128, 128), 128)] = jnp.sum(total, axis=0, keepdims=True)

    fetch(0, bufs[0])
    for half, o_ref in enumerate((mine_ref, theirs_ref)):

        def chunk(n, carry, half=half, o_ref=o_ref):
            for q in range(8):
                at = half * 64 + 8 * n + q
                fetch(jnp.minimum(at + 1, 127), bufs[(q + 1) % 8])
                mix(at, bufs[q], o_ref, 8 * n + q)
            return carry

        lax.fori_loop(0, 8, chunk, 0)


def gather(base, a, b, col, fy, fx):
    return call(
        gather_kernel,
        [jax.ShapeDtypeStruct((1, 8192), F32)] * 2,
        [SM] + [VM] * 5,
        [pltpu.VMEM((16384, 128), F32)] + [pltpu.VMEM((256, 128), F32)] * 8,
        int(1e10), 20, "gather",
        base, a, b, col, fy, fx,
    )


AXES = ("wide", "narrow")


def spread(blocks):
    return lax.all_to_all(blocks, AXES, split_axis=0, concat_axis=0, tiled=True)


def swap_cores(x):
    n = lax.axis_size("narrow")
    return lax.ppermute(x, "narrow", [(i, i ^ 1) for i in range(n)])


def swap_chips(x):
    n = lax.axis_size("narrow")
    return lax.ppermute(x, "narrow", [(i, i ^ 2) for i in range(n)])


def shards(stream_hat, dye, float_slot, float_row, float_col, float_frac, float_dye, tile_lists):
    device = lax.axis_index(AXES)
    group = lax.axis_index("wide")
    core = lax.axis_index("narrow") % 2
    side = lax.axis_index("narrow") // 2 % 2
    wave = device * 64 + jnp.arange(64)
    wave = jnp.where(wave >= 4096, wave - 8192, wave).astype(F32)[None]

    line = lambda x: x.reshape(1, 8192)
    own_floats, spec = stream_send(
        stream_hat,
        wave,
        (line(float_slot), line(float_row), line(float_col), float_frac, line(float_dye)),
    )
    their_floats = swap_chips(own_floats)
    spec, own_floats, tile_lists = lax.optimization_barrier((spec, own_floats, tile_lists))
    spec = spread(spec.reshape(128, 2, 64, 128)).reshape(256, 64, 128)
    floats = jnp.concatenate([own_floats, their_floats], axis=1)
    slot = floats[0].astype(jnp.int32).reshape(128, 128)
    row = floats[1].astype(jnp.int32).reshape(128, 128)
    col = floats[2:3].astype(jnp.int32)
    fy = floats[3:4]
    fx = floats[4:5]
    amount = floats[5:6]

    own_list = lax.dynamic_index_in_dim(tile_lists, group, 0, keepdims=False)
    holder = own_list // 64
    before = jnp.arange(256)[:, None] > jnp.arange(256)[None, :]
    rank = jnp.sum((before & (holder[:, None] == holder[None, :])).astype(jnp.int32), axis=1)
    position = jnp.where(own_list >= 0, jnp.where(rank == core, 0, 128) + holder, 0)
    pos = jnp.sum(
        jnp.where(jnp.arange(256)[:, None, None] == slot[None], position[:, None, None], 0), axis=0
    )

    mine = (tile_lists >= 0) & (tile_lists // 64 == device)
    place = jnp.cumsum(mine.astype(jnp.int32), axis=1) - 1
    local = tile_lists % 64 + 1
    entries = jnp.stack(
        [jnp.sum(jnp.where(mine & (place == e), local, 0), axis=1) for e in range(CAPO)], axis=1
    ).reshape(1, 32) - 1

    level = row - 32 * side
    base = jnp.where((level >= -1) & (level <= 31), pos * 40 + 8 + level, 0)
    keep, send = deposit(base, col, fy, fx, amount)
    dep = (keep.astype(F32) + swap_cores(send).astype(F32)).astype(BF)
    returned = spread(dep)
    spec, dep = lax.optimization_barrier((spec, dep))

    outgoing = stream_recv(entries, spec)
    outgoing, dye = lax.optimization_barrier((outgoing, dye))
    own = spread(outgoing)
    front = dye_send(entries, dye, returned)
    own, front = lax.optimization_barrier((own, front))
    other = swap_cores(own)
    front = spread(front.reshape(128, 2, 32, 128)).reshape(256, 32, 128)

    mine, theirs = gather(pos * 64 + row, own, other, col, fy, fx)
    mine, theirs, front = lax.optimization_barrier((mine, theirs, front))
    back = swap_chips(theirs)
    velocity = jnp.where(side == 0, jnp.concatenate([mine, back]), jnp.concatenate([back, mine]))
    dye_hat = dye_recv(front)
    return (velocity, dye_hat)


def solution(mesh):
    return jax.shard_map(
        shards,
        mesh=mesh,
        in_specs=(
            P(None, AXES, None),
            P(AXES, None),
            P(AXES),
            P(AXES),
            P(AXES),
            P(None, AXES),
            P(AXES),
            P(),
        ),
        out_specs=(P(None, AXES), P(None, AXES, None)),
        check_vma=False,
    )
```

```python
import numpy as np, math

import jax, jax.numpy as jnp
from jax import lax
from jax.sharding import PartitionSpec as P
from jax.experimental import pallas as pl
from jax.experimental.pallas import tpu as pltpu

BF = jnp.bfloat16
F32 = jnp.float32
NT = (((1,), (1,)), ((), ()))
PAD = 72
PAD2 = 136
PAD3 = 40


def cs(num, den, sign):
    ang = sign * 2.0 * math.pi * (num % den) / den
    return np.cos(ang), np.sin(ang)


def cplx(c, s):
    return np.stack([np.stack([c, -s]), np.stack([s, c])])


def bf(x):
    return np.asarray(x, np.float32).astype(jnp.bfloat16)


def send_tables(sign, stream):
    p = np.arange(64)
    q = np.arange(128)
    c, s = cs(p[:, None] * p[None, :], 64, sign)
    w = cplx(c, s).transpose(0, 2, 1, 3)
    if stream:
        a = w.reshape(128, 128)
        signed = np.where(p >= 32, p - 64, p) * 128.0
        b = (w * signed).reshape(128, 128)
        g = np.concatenate([a, b])
    else:
        g = w[:, :, 0, :].reshape(128, 64)
    tc, ts = cs(p[:, None] * q[None, :], 8192, sign)
    c, s = cs(q[:, None] * q[None, :], 128, sign)
    w2 = cplx(c, s).transpose(2, 0, 1, 3).reshape(256, 256)
    return bf(g), np.float32(tc), np.float32(ts), bf(w2)


def recv_tables(sign, stream):
    k = np.arange(128)
    r = np.arange(64)
    c, s = cs(k[:, None] * k[None, :], 128, sign)
    w1 = cplx(c, s).transpose(0, 2, 3, 1).reshape(256, 256)
    tc, ts = cs(k[:, None] * r[None, :], 8192, sign)
    tc = np.concatenate([tc, tc], 1)
    ts = np.concatenate([ts, ts], 1)
    c, s = cs(r[:, None] * r[None, :], 64, sign)
    w = cplx(c, s)
    v = np.zeros((2, 2, 64, 2, 2, 64))
    for e in range(2):
        v[:, e, :, :, e, :] = w.transpose(0, 2, 1, 3)
    if stream:
        v = v[0].reshape(128, 256)
    else:
        v = v.reshape(256, 256) / 8192.0
    return bf(w1), np.float32(tc), np.float32(ts), bf(v)


def stream_send_kernel(
    slot_ref, row_ref, col_ref, frac_ref, amount_ref, g_ref, tc_ref, ts_ref, w2_ref, s_hbm,
    floats_ref, o_hbm, s_ref, xs, tre, tim, of, o_ref, in_sem, out_sem,
):
    reads = []
    for k in range(4):
        lanes = pl.ds(2048 * k, 2048)
        reads.append(
            pltpu.make_async_copy(s_hbm.at[:, :, lanes], s_ref.at[:, :, lanes], in_sem.at[k])
        )
        reads[k].start()
    floats_ref[0:1, :] = slot_ref[...].astype(F32)
    floats_ref[1:2, :] = row_ref[...].astype(F32)
    floats_ref[2:3, :] = col_ref[...].astype(F32)
    floats_ref[3:5, :] = frac_ref[...]
    floats_ref[5:6, :] = amount_ref[...]

    def load(p, carry):
        at = pl.multiple_of(p * 128, 128)
        for c in range(2):
            row = pl.multiple_of((c * 64 + p) * PAD, 8)
            xs[pl.ds(row, 64), :] = s_ref[c, :, pl.ds(at, 128)].astype(F32)
        return carry

    for k in range(4):
        reads[k].wait()
        lax.fori_loop(16 * k, 16 * k + 16, load, 0, unroll=4)
    first = (lax.axis_index("wide") * 8 + lax.axis_index("narrow")) * 64
    q = lax.broadcasted_iota(jnp.int32, (64, 128), 1).astype(F32)

    def rows(n, carry):
        x = jnp.concatenate([xs[pl.ds(2 * n + h, 128, stride=PAD), :].astype(BF) for h in range(2)], axis=1)
        both = jnp.dot(g_ref[...], x, preferred_element_type=F32)
        tc = tc_ref[...]
        ts = ts_ref[...]
        for h in range(2):
            r = 2 * n + h
            z = both[:, h * 128 : h * 128 + 128]
            are, aim, bre, bim = z[:64], z[64:128], z[128:192], z[192:]
            ure = bre + q * are
            uim = bim + q * aim
            wa = jnp.where(first + r >= 4096, first + r - 8192, first + r).astype(F32)
            base = pl.multiple_of(r * PAD2, 8)
            vre = are * tc - aim * ts
            vim = are * ts + aim * tc
            tre[pl.ds(base, 64), :] = ure * ts + uim * tc
            tim[pl.ds(base, 64), :] = uim * ts - ure * tc
            tre[pl.ds(base + 64, 64), :] = -wa * vim
            tim[pl.ds(base + 64, 64), :] = wa * vre
        return carry

    lax.fori_loop(0, 32, rows, 0, unroll=8)

    def cols(n, carry):
        parts = []
        for h in range(2):
            for f in range(2):
                at = pl.ds(f * 64 + 2 * n + h, 64, stride=PAD2)
                parts.append(jnp.concatenate([tre[at, :].astype(BF), tim[at, :].astype(BF)], axis=1))
        m = jnp.concatenate(parts, axis=0)
        out = lax.dot_general(w2_ref[...], m, NT, preferred_element_type=F32)
        for h in range(2):
            of[pl.ds(2 * n + h, 256, stride=PAD), :] = out[:, h * 128 : h * 128 + 128]
        return carry

    writes = []
    for k in range(4):
        lax.fori_loop(8 * k, 8 * k + 8, cols, 0, unroll=8)

        def store(i, carry, k=k):
            o_ref[i, 16 * k : 16 * k + 16] = of[pl.ds(pl.multiple_of(i * PAD + 16 * k, 8), 16), :].astype(BF)
            return carry

        lax.fori_loop(0, 256, store, 0, unroll=8)
        levels = pl.ds(16 * k, 16)
        writes.append(pltpu.make_async_copy(o_ref.at[:, levels, :], o_hbm.at[:, levels, :], out_sem.at[k]))
        writes[k].start()
    for write in writes:
        write.wait()


VM = pl.BlockSpec(memory_space=pltpu.VMEM)
SM = pl.BlockSpec(memory_space=pltpu.SMEM)
HB = pl.BlockSpec(memory_space=pl.ANY)


def call(kernel, outs, specs, scratch, cost, mib, name, *args, out_specs=None):
    return pl.pallas_call(
        kernel,
        out_shape=outs,
        in_specs=specs,
        out_specs=out_specs or jax.tree.map(lambda _: VM, outs),
        scratch_shapes=scratch,
        compiler_params=pltpu.CompilerParams(vmem_limit_bytes=mib << 20),
        cost_estimate=pl.CostEstimate(flops=cost, bytes_accessed=1 << 20, transcendentals=0),
        name=name,
    )(*args)


def stream_send(stream, floats):
    return call(
        stream_send_kernel,
        [jax.ShapeDtypeStruct((6, 8192), F32), jax.ShapeDtypeStruct((256, 64, 128), BF)],
        [VM] * 9 + [HB],
        [pltpu.VMEM((2, 64, 8192), BF), pltpu.VMEM((129 * PAD, 128), F32)]
        + [pltpu.VMEM((65 * PAD2, 128), F32)] * 2
        + [pltpu.VMEM((257 * PAD, 128), F32), pltpu.VMEM((256, 64, 128), BF)]
        + [pltpu.SemaphoreType.DMA((4,))] * 2,
        int(6e9), 60, "stream_send",
        *floats, *send_tables(1.0, True), stream, out_specs=[VM, HB],
    )


def stream_recv_kernel(idx_ref, x_ref, w1_ref, tc_ref, ts_ref, v_ref, o_ref, xf, of):
    def load(i, carry):
        xf[pl.ds(pl.multiple_of(i * PAD, 8), 64), :] = x_ref[i].astype(F32)
        return carry

    lax.fori_loop(0, 256, load, 0, unroll=8)

    def step(n, carry):
        d = jnp.concatenate([xf[pl.ds(2 * n + h, 256, stride=PAD), :].astype(BF) for h in range(2)], axis=1)
        z = jnp.dot(w1_ref[...], d, preferred_element_type=F32)
        tc = tc_ref[...]
        ts = ts_ref[...]
        parts = []
        for h in range(2):
            re = z[:128, h * 128 : h * 128 + 128]
            im = z[128:, h * 128 : h * 128 + 128]
            parts.append(
                jnp.concatenate([(re * tc - im * ts).astype(BF), (re * ts + im * tc).astype(BF)], axis=1)
            )
        m = jnp.concatenate(parts, axis=0)
        out = lax.dot_general(v_ref[...], m, NT, preferred_element_type=F32)
        for h in range(2):
            for f in range(2):
                of[pl.ds(64 * f + 2 * n + h, 64, stride=PAD2), :] = out[f * 64 : f * 64 + 64, h * 128 : h * 128 + 128]
        return carry

    lax.fori_loop(0, 32, step, 0, unroll=8)

    def store(n, carry):
        tile = jnp.maximum(idx_ref[0, n], 0)
        for f in range(2):
            data = of[pl.ds(pl.multiple_of(tile * PAD2, 8) + 64 * f, 64), :].astype(BF)
            for x in range(2):
                o_ref[n // 2 * 8 + 4 * x + 2 * f + n % 2] = data
        return carry

    lax.fori_loop(0, 32, store, 0, unroll=2)


def stream_recv(idx, x):
    return call(
        stream_recv_kernel,
        jax.ShapeDtypeStruct((128, 64, 128), BF),
        [SM] + [VM] * 5,
        [pltpu.VMEM((257 * PAD, 128), F32), pltpu.VMEM((65 * PAD2, 128), F32)],
        int(6e9), 28, "stream_recv",
        idx, x, *recv_tables(1.0, True),
    )


def dye_send_kernel(idx_ref, dye_ref, ret_ref, g_ref, tc_ref, ts_ref, w2_ref, o_ref, xs, tre, tim, of):
    def load(p, carry):
        at = pl.multiple_of(p * 128, 128)
        xs[pl.ds(pl.multiple_of(p * PAD, 8), 64), :] = dye_ref[:, pl.ds(at, 128)].astype(F32)
        return carry

    lax.fori_loop(0, 64, load, 0, unroll=4)

    def place(n, carry):
        tile = idx_ref[0, n]

        @pl.when(tile >= 0)
        def _():
            g = n // 2
            e = n % 2
            for half in range(2):
                at = pl.ds(pl.multiple_of(tile * PAD, 8) + 32 * half, 32)
                total = xs[at, :]
                for x in range(2):
                    total = total + ret_ref[g * 8 + 4 * x + 2 * half + e].astype(F32)
                xs[at, :] = total

        return carry

    lax.fori_loop(0, 32, place, 0)

    def rows(n, carry):
        x = jnp.concatenate([xs[pl.ds(4 * n + h, 64, stride=PAD), :].astype(BF) for h in range(4)], axis=1)
        z = jnp.dot(g_ref[...], x, preferred_element_type=F32)
        tc = tc_ref[...]
        ts = ts_ref[...]
        for h in range(4):
            re = z[:64, h * 128 : h * 128 + 128]
            im = z[64:, h * 128 : h * 128 + 128]
            base = pl.multiple_of((4 * n + h) * PAD, 8)
            tre[pl.ds(base, 64), :] = re * tc - im * ts
            tim[pl.ds(base, 64), :] = re * ts + im * tc
        return carry

    lax.fori_loop(0, 16, rows, 0, unroll=8)

    def cols(n, carry):
        parts = []
        for e in range(4):
            at = pl.ds(4 * n + e, 64, stride=PAD)
            parts.append(jnp.concatenate([tre[at, :].astype(BF), tim[at, :].astype(BF)], axis=1))
        m = jnp.concatenate(parts, axis=0)
        out = lax.dot_general(w2_ref[...], m, NT, preferred_element_type=F32)
        for h in range(2):
            of[pl.ds(2 * n + h, 256, stride=PAD3), :] = out[:, h * 128 : h * 128 + 128]
        return carry

    lax.fori_loop(0, 16, cols, 0, unroll=8)

    def store(i, carry):
        o_ref[i] = of[pl.ds(pl.multiple_of(i * PAD3, 8), 32), :].astype(BF)
        return carry

    lax.fori_loop(0, 256, store, 0, unroll=8)


def dye_send(idx, dye, ret):
    return call(
        dye_send_kernel,
        jax.ShapeDtypeStruct((256, 32, 128), BF),
        [SM] + [VM] * 6,
        [pltpu.VMEM((65 * PAD, 128), F32)] * 3 + [pltpu.VMEM((257 * PAD3, 128), F32)],
        int(4e9), 24, "dye_send",
        idx, dye, ret, *send_tables(-1.0, False),
    )


def dye_recv_kernel(x_hbm, w1_ref, tc_ref, ts_ref, v_ref, o_hbm, xf, of, o_ref, x_ref, out_sem, in_sem):
    reads = []
    for h in range(2):
        levels = pl.ds(16 * h, 16)
        reads.append(
            pltpu.make_async_copy(x_hbm.at[:, levels, :], x_ref.at[:, levels, :], in_sem.at[h])
        )
        reads[h].start()

    def take(h):
        def load(i, carry):
            at = pl.ds(pl.multiple_of(i * PAD3 + 16 * h, 8), 16)
            xf[at, :] = x_ref[i, 16 * h : 16 * h + 16].astype(F32)
            return carry

        reads[h].wait()
        lax.fori_loop(0, 256, load, 0, unroll=8)

    def step(n, carry):
        d = jnp.concatenate([xf[pl.ds(2 * n + h, 256, stride=PAD3), :].astype(BF) for h in range(2)], axis=1)
        z = jnp.dot(w1_ref[...], d, preferred_element_type=F32)
        tc = tc_ref[...]
        ts = ts_ref[...]
        parts = []
        for h in range(2):
            re = z[:128, h * 128 : h * 128 + 128]
            im = z[128:, h * 128 : h * 128 + 128]
            parts.append(
                jnp.concatenate([(re * tc - im * ts).astype(BF), (re * ts + im * tc).astype(BF)], axis=1)
            )
        m = jnp.concatenate(parts, axis=0)
        out = lax.dot_general(v_ref[...], m, NT, preferred_element_type=F32)
        for h in range(2):
            for c in range(2):
                for e in range(2):
                    row = c * 4096 + (n // 2) * 512 + (4 * n + 2 * h + e) % 8
                    of[pl.ds(row, 64, stride=8), :] = out[
                        (2 * c + e) * 64 : (2 * c + e) * 64 + 64, h * 128 : h * 128 + 128
                    ]
        return carry

    writes = []
    for k in range(8):
        if k % 4 == 0:
            take(k // 4)
        for n in range(2 * k, 2 * k + 2):
            step(n, 0)
        at = pl.ds(8 * k, 8)
        for c in range(2):
            for j in range(64):
                o_ref[c, at, j * 128 : j * 128 + 128] = of[pl.ds(c * 4096 + k * 512 + j * 8, 8), :]
        writes.append(pltpu.make_async_copy(o_ref.at[:, at, :], o_hbm.at[:, at, :], out_sem.at[k]))
        writes[k].start()
    for write in writes:
        write.wait()


def dye_recv(x):
    return call(
        dye_recv_kernel,
        jax.ShapeDtypeStruct((2, 64, 8192), F32),
        [HB] + [VM] * 4,
        [pltpu.VMEM((257 * PAD3, 128), F32), pltpu.VMEM((8200, 128), F32)]
        + [pltpu.VMEM((2, 64, 8192), F32), pltpu.VMEM((256, 32, 128), BF)]
        + [pltpu.SemaphoreType.DMA((8,)), pltpu.SemaphoreType.DMA((2,))],
        int(4e9), 20, "dye_recv",
        x, *recv_tables(-1.0, False), out_specs=HB,
    )

CAPO = 2


def deposit_kernel(idx_ref, col_ref, fy_ref, fx_ref, am_ref, keep_ref, send_ref, *refs):
    bufs = refs[:4]
    accs = refs[4:]
    ways = len(accs)

    def clear(i, carry):
        for acc in accs:
            acc[pl.ds(pl.multiple_of(i * 40, 8), 40), :] = jnp.zeros((40, 128), F32)
        return carry

    lax.fori_loop(0, 257, clear, 0)

    def weights(n, dst):
        xs = lax.broadcasted_iota(jnp.int32, (128, 128), 0)
        rows = lax.broadcasted_iota(jnp.int32, (256, 128), 0)
        off = rows // 2 - lax.broadcasted_iota(jnp.int32, (256, 128), 1)
        odd = rows % 2 == 1
        at = pl.ds(pl.multiple_of(n * 128, 128), 128)
        fx = fx_ref[:, at]
        am = am_ref[:, at]
        hi = am * fy_ref[:, at]
        lo = am - hi
        d = xs - col_ref[:, at]
        w = jnp.where(d == 0, 1.0 - fx, jnp.where(d == 1, fx, 0.0)).astype(BF)
        e = jnp.where(off == 0, jnp.where(odd, hi, lo), 0.0).astype(BF)
        dst[...] = lax.dot_general(e, w, NT, preferred_element_type=F32)

    def add(n, src):
        for f in range(0, 128, ways):
            at = [pl.ds(idx_ref[n, f + k], 2) for k in range(ways)]
            new = [accs[k][at[k], :] + src[2 * (f + k) : 2 * (f + k) + 2, :] for k in range(ways)]
            for k in range(ways):
                accs[k][at[k], :] = new[k]

    weights(0, bufs[0])

    def chunk(n, carry):
        for q in range(4):
            weights(jnp.minimum(4 * n + q + 1, 127), bufs[(q + 1) % 4])
            add(4 * n + q, bufs[q])
        return carry

    lax.fori_loop(0, 32, chunk, 0)

    def store(i, carry):
        for ref, base in ((keep_ref, 8), (send_ref, 128 * 40 + 8)):
            at = pl.ds(pl.multiple_of(i * 40 + base, 8), 32)
            total = accs[0][at, :]
            for acc in accs[1:]:
                total = total + acc[at, :]
            ref[i] = total.astype(BF)
        return carry

    lax.fori_loop(0, 128, store, 0, unroll=2)


def deposit(idx, col, fy, fx, am):
    return call(
        deposit_kernel,
        [jax.ShapeDtypeStruct((128, 32, 128), BF)] * 2,
        [SM] + [VM] * 4,
        [pltpu.VMEM((256, 128), F32)] * 4 + [pltpu.VMEM((257 * 40, 128), F32)] * 4,
        int(2e10), 30, "deposit",
        idx, col, fy, fx, am,
    )


def gather_kernel(base_ref, a_ref, b_ref, col_ref, fy_ref, fx_ref, mine_ref, theirs_ref, st, *bufs):
    def load(i, carry):
        at = pl.multiple_of(i * 64, 64)
        st[pl.ds(at, 64), :] = a_ref[i].astype(F32)
        st[pl.ds(at + 8192, 64), :] = b_ref[i].astype(F32)
        return carry

    lax.fori_loop(0, 128, load, 0, unroll=4)

    def fetch(n, g):
        for f in range(128):
            g[f * 2 : f * 2 + 2, :] = st[pl.ds(base_ref[n, f], 2), :]

    def mix(n, g, o_ref, to):
        sub = lax.broadcasted_iota(jnp.int32, (8, 128), 0)
        off = lax.broadcasted_iota(jnp.int32, (8, 128), 1) - sub // 2
        xs = lax.broadcasted_iota(jnp.int32, (128, 128), 0)
        at = pl.ds(pl.multiple_of(n * 128, 128), 128)
        col = col_ref[:, at]
        fy = fy_ref[:, at]
        fx = fx_ref[:, at]
        d = xs - col
        w = jnp.where(d == 0, 1.0 - fx, jnp.where(d == 1, fx, 0.0))
        hi = w.astype(BF)
        lo = (w - hi.astype(F32)).astype(BF)
        rows = g[...].astype(BF)
        z = jnp.dot(
            jnp.concatenate([rows, rows], axis=1),
            jnp.concatenate([hi, lo], axis=0),
            preferred_element_type=F32,
        )
        parts = [jnp.zeros((8, 128), F32) for _ in range(4)]
        for i in range(32):
            parts[i % 4] = jnp.where(off == 4 * i, z[8 * i : 8 * i + 8], parts[i % 4])
        total = (parts[0] + parts[1] + (parts[2] + parts[3])) * jnp.where(sub % 2 == 1, fy, 1.0 - fy)
        o_ref[:, pl.ds(pl.multiple_of(to * 128, 128), 128)] = jnp.sum(total, axis=0, keepdims=True)

    fetch(0, bufs[0])
    for half, o_ref in enumerate((mine_ref, theirs_ref)):

        def chunk(n, carry, half=half, o_ref=o_ref):
            for q in range(8):
                at = half * 64 + 8 * n + q
                fetch(jnp.minimum(at + 1, 127), bufs[(q + 1) % 8])
                mix(at, bufs[q], o_ref, 8 * n + q)
            return carry

        lax.fori_loop(0, 8, chunk, 0)


def gather(base, a, b, col, fy, fx):
    return call(
        gather_kernel,
        [jax.ShapeDtypeStruct((1, 8192), F32)] * 2,
        [SM] + [VM] * 5,
        [pltpu.VMEM((16392, 128), F32)] + [pltpu.VMEM((256, 128), F32)] * 8,
        int(1e10), 20, "gather",
        base, a, b, col, fy, fx,
    )


AXES = ("wide", "narrow")


def spread(blocks):
    return lax.all_to_all(blocks, AXES, split_axis=0, concat_axis=0, tiled=True)


def swap_cores(x):
    n = lax.axis_size("narrow")
    return lax.ppermute(x, "narrow", [(i, i ^ 1) for i in range(n)])


def swap_chips(x):
    n = lax.axis_size("narrow")
    return lax.ppermute(x, "narrow", [(i, i ^ 2) for i in range(n)])


def shards(stream_hat, dye, float_slot, float_row, float_col, float_frac, float_dye, tile_lists):
    device = lax.axis_index(AXES)
    group = lax.axis_index("wide")
    core = lax.axis_index("narrow") % 2
    side = lax.axis_index("narrow") // 2 % 2

    line = lambda x: x.reshape(1, 8192)
    own_floats, spec = stream_send(
        stream_hat,
        (line(float_slot), line(float_row), line(float_col), float_frac, line(float_dye)),
    )
    their_floats = swap_chips(own_floats)
    spec, own_floats, tile_lists = lax.optimization_barrier((spec, own_floats, tile_lists))
    spec = spread(spec.reshape(128, 2, 64, 128)).reshape(256, 64, 128)
    floats = jnp.concatenate([own_floats, their_floats], axis=1)
    slot = floats[0].astype(jnp.int32).reshape(128, 128)
    row = floats[1].astype(jnp.int32).reshape(128, 128)
    col = floats[2:3].astype(jnp.int32)
    fy = floats[3:4]
    fx = floats[4:5]
    amount = floats[5:6]

    own_list = lax.dynamic_index_in_dim(tile_lists, group, 0, keepdims=False)
    holder = own_list // 64
    before = jnp.arange(256)[:, None] > jnp.arange(256)[None, :]
    rank = jnp.sum((before & (holder[:, None] == holder[None, :])).astype(jnp.int32), axis=1)
    position = jnp.where(own_list >= 0, jnp.where(rank == core, 0, 128) + holder, 0)
    pos = jnp.sum(
        jnp.where(jnp.arange(256)[:, None, None] == slot[None], position[:, None, None], 0), axis=0
    )

    mine = (tile_lists >= 0) & (tile_lists // 64 == device)
    place = jnp.cumsum(mine.astype(jnp.int32), axis=1) - 1
    local = tile_lists % 64 + 1
    entries = jnp.stack(
        [jnp.sum(jnp.where(mine & (place == e), local, 0), axis=1) for e in range(CAPO)], axis=1
    ).reshape(1, 32) - 1

    level = row - 32 * side
    base = jnp.where((level >= -1) & (level <= 31), pos * 40 + 8 + level, 0)
    keep, send = deposit(base, col, fy, fx, amount)
    dep = (keep.astype(F32) + swap_cores(send).astype(F32)).astype(BF)
    returned = spread(dep)
    spec, dep = lax.optimization_barrier((spec, dep))

    outgoing = stream_recv(entries, spec)
    outgoing, dye = lax.optimization_barrier((outgoing, dye))
    own = spread(outgoing)
    front = dye_send(entries, dye, returned)
    own, front = lax.optimization_barrier((own, front))
    other = swap_cores(own)
    front = spread(front.reshape(128, 2, 32, 128)).reshape(256, 32, 128)

    mine, theirs = gather(pos * 64 + row, own, other, col, fy, fx)
    mine, theirs, front = lax.optimization_barrier((mine, theirs, front))
    back = swap_chips(theirs)
    velocity = jnp.where(side == 0, jnp.concatenate([mine, back]), jnp.concatenate([back, mine]))
    dye_hat = dye_recv(front)
    return (velocity, dye_hat)


def solution(mesh):
    return jax.shard_map(
        shards,
        mesh=mesh,
        in_specs=(
            P(None, AXES, None),
            P(AXES, None),
            P(AXES),
            P(AXES),
            P(AXES),
            P(None, AXES),
            P(AXES),
            P(),
        ),
        out_specs=(P(None, AXES), P(None, AXES, None)),
        check_vma=False,
    )
```

```python
import numpy as np, math

import jax, jax.numpy as jnp
from jax import lax
from jax.sharding import PartitionSpec as P
from jax.experimental import pallas as pl
from jax.experimental.pallas import tpu as pltpu

BF = jnp.bfloat16
F32 = jnp.float32
NT = (((1,), (1,)), ((), ()))
PAD = 73
PAD2 = 137
PAD3 = 41


def cs(num, den, sign):
    ang = sign * 2.0 * math.pi * (num % den) / den
    return np.cos(ang), np.sin(ang)


def cplx(c, s):
    return np.stack([np.stack([c, -s]), np.stack([s, c])])


def bf(x):
    return np.asarray(x, np.float32).astype(jnp.bfloat16)


def send_tables(sign, stream):
    p = np.arange(64)
    q = np.arange(128)
    c, s = cs(p[:, None] * p[None, :], 64, sign)
    w = cplx(c, s).transpose(0, 2, 1, 3)
    if stream:
        a = w.reshape(128, 128)
        signed = np.where(p >= 32, p - 64, p) * 128.0
        b = (w * signed).reshape(128, 128)
        g = np.concatenate([a, b])
    else:
        g = w[:, :, 0, :].reshape(128, 64)
    tc, ts = cs(p[:, None] * q[None, :], 8192, sign)
    c, s = cs(q[:, None] * q[None, :], 128, sign)
    w2 = cplx(c, s).transpose(2, 0, 1, 3).reshape(256, 256)
    return bf(g), np.float32(tc), np.float32(ts), bf(w2)


def recv_tables(sign, stream):
    k = np.arange(128)
    r = np.arange(64)
    c, s = cs(k[:, None] * k[None, :], 128, sign)
    w1 = cplx(c, s).transpose(0, 2, 3, 1).reshape(256, 256)
    tc, ts = cs(k[:, None] * r[None, :], 8192, sign)
    tc = np.concatenate([tc, tc], 1)
    ts = np.concatenate([ts, ts], 1)
    c, s = cs(r[:, None] * r[None, :], 64, sign)
    w = cplx(c, s)
    v = np.zeros((2, 2, 64, 2, 2, 64))
    for e in range(2):
        v[:, e, :, :, e, :] = w.transpose(0, 2, 1, 3)
    if stream:
        v = v[0].reshape(128, 256)
    else:
        v = v.reshape(256, 256) / 8192.0
    return bf(w1), np.float32(tc), np.float32(ts), bf(v)


def stream_send_kernel(
    slot_ref, row_ref, col_ref, frac_ref, amount_ref, g_ref, tc_ref, ts_ref, w2_ref, s_hbm,
    floats_ref, o_hbm, s_ref, xs, tre, tim, of, o_ref, in_sem, out_sem,
):
    reads = []
    for k in range(4):
        lanes = pl.ds(2048 * k, 2048)
        reads.append(
            pltpu.make_async_copy(s_hbm.at[:, :, lanes], s_ref.at[:, :, lanes], in_sem.at[k])
        )
        reads[k].start()
    floats_ref[0:1, :] = slot_ref[...].astype(F32)
    floats_ref[1:2, :] = row_ref[...].astype(F32)
    floats_ref[2:3, :] = col_ref[...].astype(F32)
    floats_ref[3:5, :] = frac_ref[...]
    floats_ref[5:6, :] = amount_ref[...]

    def load(p, carry):
        at = pl.multiple_of(p * 128, 128)
        for c in range(2):
            row = (c * 64 + p) * PAD
            xs[pl.ds(row, 64), :] = s_ref[c, :, pl.ds(at, 128)].astype(F32)
        return carry

    for k in range(4):
        reads[k].wait()
        lax.fori_loop(16 * k, 16 * k + 16, load, 0, unroll=4)
    first = (lax.axis_index("wide") * 8 + lax.axis_index("narrow")) * 64
    q = lax.broadcasted_iota(jnp.int32, (64, 128), 1).astype(F32)

    def rows(n, carry):
        x = jnp.concatenate([xs[pl.ds(2 * n + h, 128, stride=PAD), :].astype(BF) for h in range(2)], axis=1)
        both = jnp.dot(g_ref[...], x, preferred_element_type=F32)
        tc = tc_ref[...]
        ts = ts_ref[...]
        for h in range(2):
            r = 2 * n + h
            z = both[:, h * 128 : h * 128 + 128]
            are, aim, bre, bim = z[:64], z[64:128], z[128:192], z[192:]
            ure = bre + q * are
            uim = bim + q * aim
            wa = jnp.where(first + r >= 4096, first + r - 8192, first + r).astype(F32)
            base = r * PAD2
            vre = are * tc - aim * ts
            vim = are * ts + aim * tc
            tre[pl.ds(base, 64), :] = ure * ts + uim * tc
            tim[pl.ds(base, 64), :] = uim * ts - ure * tc
            tre[pl.ds(base + 64, 64), :] = -wa * vim
            tim[pl.ds(base + 64, 64), :] = wa * vre
        return carry

    lax.fori_loop(0, 32, rows, 0, unroll=8)

    def cols(n, carry):
        parts = []
        for h in range(2):
            for f in range(2):
                at = pl.ds(f * 64 + 2 * n + h, 64, stride=PAD2)
                parts.append(jnp.concatenate([tre[at, :].astype(BF), tim[at, :].astype(BF)], axis=1))
        m = jnp.concatenate(parts, axis=0)
        out = lax.dot_general(w2_ref[...], m, NT, preferred_element_type=F32)
        for h in range(2):
            of[pl.ds(2 * n + h, 256, stride=PAD), :] = out[:, h * 128 : h * 128 + 128]
        return carry

    writes = []
    for k in range(4):
        lax.fori_loop(8 * k, 8 * k + 8, cols, 0, unroll=8)

        def store(i, carry, k=k):
            o_ref[i, 16 * k : 16 * k + 16] = of[pl.ds(i * PAD + 16 * k, 16), :].astype(BF)
            return carry

        lax.fori_loop(0, 256, store, 0, unroll=16)
        levels = pl.ds(16 * k, 16)
        writes.append(pltpu.make_async_copy(o_ref.at[:, levels, :], o_hbm.at[:, levels, :], out_sem.at[k]))
        writes[k].start()
    for write in writes:
        write.wait()


VM = pl.BlockSpec(memory_space=pltpu.VMEM)
SM = pl.BlockSpec(memory_space=pltpu.SMEM)
HB = pl.BlockSpec(memory_space=pl.ANY)


def call(kernel, outs, specs, scratch, cost, mib, name, *args, out_specs=None):
    return pl.pallas_call(
        kernel,
        out_shape=outs,
        in_specs=specs,
        out_specs=out_specs or jax.tree.map(lambda _: VM, outs),
        scratch_shapes=scratch,
        compiler_params=pltpu.CompilerParams(vmem_limit_bytes=mib << 20),
        cost_estimate=pl.CostEstimate(flops=cost, bytes_accessed=1 << 20, transcendentals=0),
        name=name,
    )(*args)


def stream_send(stream, floats):
    return call(
        stream_send_kernel,
        [jax.ShapeDtypeStruct((6, 8192), F32), jax.ShapeDtypeStruct((256, 64, 128), BF)],
        [VM] * 9 + [HB],
        [pltpu.VMEM((2, 64, 8192), BF), pltpu.VMEM((129 * PAD, 128), F32)]
        + [pltpu.VMEM((65 * PAD2, 128), F32)] * 2
        + [pltpu.VMEM((257 * PAD, 128), F32), pltpu.VMEM((256, 64, 128), BF)]
        + [pltpu.SemaphoreType.DMA((4,))] * 2,
        int(6e9), 60, "stream_send",
        *floats, *send_tables(1.0, True), stream, out_specs=[VM, HB],
    )


def stream_recv_kernel(idx_ref, x_ref, w1_ref, tc_ref, ts_ref, v_ref, o_ref, xf, of):
    def load(i, carry):
        xf[pl.ds(i * PAD, 64), :] = x_ref[i].astype(F32)
        return carry

    lax.fori_loop(0, 256, load, 0, unroll=8)

    def step(n, carry):
        d = jnp.concatenate([xf[pl.ds(2 * n + h, 256, stride=PAD), :].astype(BF) for h in range(2)], axis=1)
        z = jnp.dot(w1_ref[...], d, preferred_element_type=F32)
        tc = tc_ref[...]
        ts = ts_ref[...]
        parts = []
        for h in range(2):
            re = z[:128, h * 128 : h * 128 + 128]
            im = z[128:, h * 128 : h * 128 + 128]
            parts.append(
                jnp.concatenate([(re * tc - im * ts).astype(BF), (re * ts + im * tc).astype(BF)], axis=1)
            )
        m = jnp.concatenate(parts, axis=0)
        out = lax.dot_general(v_ref[...], m, NT, preferred_element_type=F32)
        for h in range(2):
            for f in range(2):
                of[pl.ds(64 * f + 2 * n + h, 64, stride=PAD2), :] = out[f * 64 : f * 64 + 64, h * 128 : h * 128 + 128]
        return carry

    lax.fori_loop(0, 32, step, 0, unroll=8)

    def store(n, carry):
        tile = jnp.maximum(idx_ref[0, n], 0)
        for f in range(2):
            data = of[pl.ds(tile * PAD2 + 64 * f, 64), :].astype(BF)
            for x in range(2):
                o_ref[n // 2 * 8 + 4 * x + 2 * f + n % 2] = data
        return carry

    lax.fori_loop(0, 32, store, 0, unroll=2)


def stream_recv(idx, x):
    return call(
        stream_recv_kernel,
        jax.ShapeDtypeStruct((128, 64, 128), BF),
        [SM] + [VM] * 5,
        [pltpu.VMEM((257 * PAD, 128), F32), pltpu.VMEM((65 * PAD2, 128), F32)],
        int(6e9), 28, "stream_recv",
        idx, x, *recv_tables(1.0, True),
    )


def dye_send_kernel(idx_ref, dye_ref, ret_ref, g_ref, tc_ref, ts_ref, w2_ref, o_ref, xs, tre, tim, of):
    def load(p, carry):
        at = pl.multiple_of(p * 128, 128)
        xs[pl.ds(p * PAD, 64), :] = dye_ref[:, pl.ds(at, 128)].astype(F32)
        return carry

    lax.fori_loop(0, 64, load, 0, unroll=4)

    def place(n, carry):
        tile = idx_ref[0, n]

        @pl.when(tile >= 0)
        def _():
            g = n // 2
            e = n % 2
            for half in range(2):
                at = pl.ds(tile * PAD + 32 * half, 32)
                total = xs[at, :]
                for x in range(2):
                    total = total + ret_ref[g * 8 + 4 * x + 2 * half + e].astype(F32)
                xs[at, :] = total

        return carry

    lax.fori_loop(0, 32, place, 0)

    def rows(n, carry):
        x = jnp.concatenate([xs[pl.ds(4 * n + h, 64, stride=PAD), :].astype(BF) for h in range(4)], axis=1)
        z = jnp.dot(g_ref[...], x, preferred_element_type=F32)
        tc = tc_ref[...]
        ts = ts_ref[...]
        for h in range(4):
            re = z[:64, h * 128 : h * 128 + 128]
            im = z[64:, h * 128 : h * 128 + 128]
            base = (4 * n + h) * PAD
            tre[pl.ds(base, 64), :] = re * tc - im * ts
            tim[pl.ds(base, 64), :] = re * ts + im * tc
        return carry

    lax.fori_loop(0, 16, rows, 0, unroll=8)

    def cols(n, carry):
        parts = []
        for e in range(4):
            at = pl.ds(4 * n + e, 64, stride=PAD)
            parts.append(jnp.concatenate([tre[at, :].astype(BF), tim[at, :].astype(BF)], axis=1))
        m = jnp.concatenate(parts, axis=0)
        out = lax.dot_general(w2_ref[...], m, NT, preferred_element_type=F32)
        for h in range(2):
            of[pl.ds(2 * n + h, 256, stride=PAD3), :] = out[:, h * 128 : h * 128 + 128]
        return carry

    lax.fori_loop(0, 16, cols, 0, unroll=8)

    def store(i, carry):
        o_ref[i] = of[pl.ds(i * PAD3, 32), :].astype(BF)
        return carry

    lax.fori_loop(0, 256, store, 0, unroll=8)


def dye_send(idx, dye, ret):
    return call(
        dye_send_kernel,
        jax.ShapeDtypeStruct((256, 32, 128), BF),
        [SM] + [VM] * 6,
        [pltpu.VMEM((65 * PAD, 128), F32)] * 3 + [pltpu.VMEM((257 * PAD3, 128), F32)],
        int(4e9), 24, "dye_send",
        idx, dye, ret, *send_tables(-1.0, False),
    )


def dye_recv_kernel(x_hbm, w1_ref, tc_ref, ts_ref, v_ref, o_hbm, xf, of, o_ref, x_ref, out_sem, in_sem):
    reads = []
    for h in range(2):
        levels = pl.ds(16 * h, 16)
        reads.append(
            pltpu.make_async_copy(x_hbm.at[:, levels, :], x_ref.at[:, levels, :], in_sem.at[h])
        )
        reads[h].start()

    def take(h):
        def load(i, carry):
            at = pl.ds(i * PAD3 + 16 * h, 16)
            xf[at, :] = x_ref[i, 16 * h : 16 * h + 16].astype(F32)
            return carry

        reads[h].wait()
        lax.fori_loop(0, 256, load, 0, unroll=8)

    def step(n, carry):
        d = jnp.concatenate([xf[pl.ds(2 * n + h, 256, stride=PAD3), :].astype(BF) for h in range(2)], axis=1)
        z = jnp.dot(w1_ref[...], d, preferred_element_type=F32)
        tc = tc_ref[...]
        ts = ts_ref[...]
        parts = []
        for h in range(2):
            re = z[:128, h * 128 : h * 128 + 128]
            im = z[128:, h * 128 : h * 128 + 128]
            parts.append(
                jnp.concatenate([(re * tc - im * ts).astype(BF), (re * ts + im * tc).astype(BF)], axis=1)
            )
        m = jnp.concatenate(parts, axis=0)
        out = lax.dot_general(v_ref[...], m, NT, preferred_element_type=F32)
        for h in range(2):
            for c in range(2):
                for e in range(2):
                    row = c * 4096 + (n // 2) * 512 + (4 * n + 2 * h + e) % 8
                    of[pl.ds(row, 64, stride=8), :] = out[
                        (2 * c + e) * 64 : (2 * c + e) * 64 + 64, h * 128 : h * 128 + 128
                    ]
        return carry

    writes = []
    for k in range(8):
        if k % 4 == 0:
            take(k // 4)
        for n in range(2 * k, 2 * k + 2):
            step(n, 0)
        at = pl.ds(8 * k, 8)
        for c in range(2):
            for j in range(64):
                o_ref[c, at, j * 128 : j * 128 + 128] = of[pl.ds(c * 4096 + k * 512 + j * 8, 8), :]
        writes.append(pltpu.make_async_copy(o_ref.at[:, at, :], o_hbm.at[:, at, :], out_sem.at[k]))
        writes[k].start()
    for write in writes:
        write.wait()


def dye_recv(x):
    return call(
        dye_recv_kernel,
        jax.ShapeDtypeStruct((2, 64, 8192), F32),
        [HB] + [VM] * 4,
        [pltpu.VMEM((257 * PAD3, 128), F32), pltpu.VMEM((8200, 128), F32)]
        + [pltpu.VMEM((2, 64, 8192), F32), pltpu.VMEM((256, 32, 128), BF)]
        + [pltpu.SemaphoreType.DMA((8,)), pltpu.SemaphoreType.DMA((2,))],
        int(4e9), 20, "dye_recv",
        x, *recv_tables(-1.0, False), out_specs=HB,
    )

CAPO = 2


def deposit_kernel(idx_ref, col_ref, fy_ref, fx_ref, am_ref, keep_ref, send_ref, *refs):
    bufs = refs[:4]
    accs = refs[4:]
    ways = len(accs)

    def clear(i, carry):
        for acc in accs:
            acc[pl.ds(pl.multiple_of(i * 40, 8), 40), :] = jnp.zeros((40, 128), F32)
        return carry

    lax.fori_loop(0, 257, clear, 0)

    def weights(n, dst):
        xs = lax.broadcasted_iota(jnp.int32, (128, 128), 0)
        rows = lax.broadcasted_iota(jnp.int32, (256, 128), 0)
        off = rows // 2 - lax.broadcasted_iota(jnp.int32, (256, 128), 1)
        odd = rows % 2 == 1
        at = pl.ds(pl.multiple_of(n * 128, 128), 128)
        fx = fx_ref[:, at]
        am = am_ref[:, at]
        hi = am * fy_ref[:, at]
        lo = am - hi
        d = xs - col_ref[:, at]
        w = jnp.where(d == 0, 1.0 - fx, jnp.where(d == 1, fx, 0.0)).astype(BF)
        e = jnp.where(off == 0, jnp.where(odd, hi, lo), 0.0).astype(BF)
        dst[...] = lax.dot_general(e, w, NT, preferred_element_type=F32)

    def add(n, src):
        for f in range(0, 128, ways):
            at = [pl.ds(idx_ref[n, f + k], 2) for k in range(ways)]
            new = [accs[k][at[k], :] + src[2 * (f + k) : 2 * (f + k) + 2, :] for k in range(ways)]
            for k in range(ways):
                accs[k][at[k], :] = new[k]

    weights(0, bufs[0])

    def chunk(n, carry):
        for q in range(4):
            weights(jnp.minimum(4 * n + q + 1, 127), bufs[(q + 1) % 4])
            add(4 * n + q, bufs[q])
        return carry

    lax.fori_loop(0, 32, chunk, 0)

    def store(i, carry):
        for ref, base in ((keep_ref, 8), (send_ref, 128 * 40 + 8)):
            at = pl.ds(pl.multiple_of(i * 40 + base, 8), 32)
            total = accs[0][at, :]
            for acc in accs[1:]:
                total = total + acc[at, :]
            ref[i] = total.astype(BF)
        return carry

    lax.fori_loop(0, 128, store, 0, unroll=2)


def deposit(idx, col, fy, fx, am):
    return call(
        deposit_kernel,
        [jax.ShapeDtypeStruct((128, 32, 128), BF)] * 2,
        [SM] + [VM] * 4,
        [pltpu.VMEM((256, 128), F32)] * 4 + [pltpu.VMEM((257 * 40, 128), F32)] * 4,
        int(2e10), 30, "deposit",
        idx, col, fy, fx, am,
    )


def gather_kernel(base_ref, a_ref, b_ref, col_ref, fy_ref, fx_ref, mine_ref, theirs_ref, st, *bufs):
    def load(i, carry):
        at = pl.multiple_of(i * 64, 64)
        st[pl.ds(at, 64), :] = a_ref[i].astype(F32)
        st[pl.ds(at + 8192, 64), :] = b_ref[i].astype(F32)
        return carry

    lax.fori_loop(0, 128, load, 0, unroll=4)

    def fetch(n, g):
        for f in range(128):
            g[f * 2 : f * 2 + 2, :] = st[pl.ds(base_ref[n, f], 2), :]

    def mix(n, g, o_ref, to):
        sub = lax.broadcasted_iota(jnp.int32, (8, 128), 0)
        off = lax.broadcasted_iota(jnp.int32, (8, 128), 1) - sub // 2
        xs = lax.broadcasted_iota(jnp.int32, (128, 128), 0)
        at = pl.ds(pl.multiple_of(n * 128, 128), 128)
        col = col_ref[:, at]
        fy = fy_ref[:, at]
        fx = fx_ref[:, at]
        d = xs - col
        w = jnp.where(d == 0, 1.0 - fx, jnp.where(d == 1, fx, 0.0))
        hi = w.astype(BF)
        lo = (w - hi.astype(F32)).astype(BF)
        rows = g[...].astype(BF)
        z = jnp.dot(
            jnp.concatenate([rows, rows], axis=1),
            jnp.concatenate([hi, lo], axis=0),
            preferred_element_type=F32,
        )
        parts = [jnp.zeros((8, 128), F32) for _ in range(4)]
        for i in range(32):
            parts[i % 4] = jnp.where(off == 4 * i, z[8 * i : 8 * i + 8], parts[i % 4])
        total = (parts[0] + parts[1] + (parts[2] + parts[3])) * jnp.where(sub % 2 == 1, fy, 1.0 - fy)
        o_ref[:, pl.ds(pl.multiple_of(to * 128, 128), 128)] = jnp.sum(total, axis=0, keepdims=True)

    fetch(0, bufs[0])
    for half, o_ref in enumerate((mine_ref, theirs_ref)):

        def chunk(n, carry, half=half, o_ref=o_ref):
            for q in range(8):
                at = half * 64 + 8 * n + q
                fetch(jnp.minimum(at + 1, 127), bufs[(q + 1) % 8])
                mix(at, bufs[q], o_ref, 8 * n + q)
            return carry

        lax.fori_loop(0, 8, chunk, 0)


def gather(base, a, b, col, fy, fx):
    return call(
        gather_kernel,
        [jax.ShapeDtypeStruct((1, 8192), F32)] * 2,
        [SM] + [VM] * 5,
        [pltpu.VMEM((16392, 128), F32)] + [pltpu.VMEM((256, 128), F32)] * 8,
        int(1e10), 20, "gather",
        base, a, b, col, fy, fx,
    )


AXES = ("wide", "narrow")


def spread(blocks):
    return lax.all_to_all(blocks, AXES, split_axis=0, concat_axis=0, tiled=True)


def swap_cores(x):
    n = lax.axis_size("narrow")
    return lax.ppermute(x, "narrow", [(i, i ^ 1) for i in range(n)])


def swap_chips(x):
    n = lax.axis_size("narrow")
    return lax.ppermute(x, "narrow", [(i, i ^ 2) for i in range(n)])


def shards(stream_hat, dye, float_slot, float_row, float_col, float_frac, float_dye, tile_lists):
    device = lax.axis_index(AXES)
    group = lax.axis_index("wide")
    core = lax.axis_index("narrow") % 2
    side = lax.axis_index("narrow") // 2 % 2

    line = lambda x: x.reshape(1, 8192)
    own_floats, spec = stream_send(
        stream_hat,
        (line(float_slot), line(float_row), line(float_col), float_frac, line(float_dye)),
    )
    their_floats = swap_chips(own_floats)
    spec, own_floats, tile_lists = lax.optimization_barrier((spec, own_floats, tile_lists))
    spec = spread(spec.reshape(128, 2, 64, 128)).reshape(256, 64, 128)
    floats = jnp.concatenate([own_floats, their_floats], axis=1)
    slot = floats[0].astype(jnp.int32).reshape(128, 128)
    row = floats[1].astype(jnp.int32).reshape(128, 128)
    col = floats[2:3].astype(jnp.int32)
    fy = floats[3:4]
    fx = floats[4:5]
    amount = floats[5:6]

    own_list = lax.dynamic_index_in_dim(tile_lists, group, 0, keepdims=False)
    holder = own_list // 64
    before = jnp.arange(256)[:, None] > jnp.arange(256)[None, :]
    rank = jnp.sum((before & (holder[:, None] == holder[None, :])).astype(jnp.int32), axis=1)
    position = jnp.where(own_list >= 0, jnp.where(rank == core, 0, 128) + holder, 0)
    pos = jnp.sum(
        jnp.where(jnp.arange(256)[:, None, None] == slot[None], position[:, None, None], 0), axis=0
    )

    mine = (tile_lists >= 0) & (tile_lists // 64 == device)
    place = jnp.cumsum(mine.astype(jnp.int32), axis=1) - 1
    local = tile_lists % 64 + 1
    entries = jnp.stack(
        [jnp.sum(jnp.where(mine & (place == e), local, 0), axis=1) for e in range(CAPO)], axis=1
    ).reshape(1, 32) - 1

    level = row - 32 * side
    base = jnp.where((level >= -1) & (level <= 31), pos * 40 + 8 + level, 0)
    keep, send = deposit(base, col, fy, fx, amount)
    dep = (keep.astype(F32) + swap_cores(send).astype(F32)).astype(BF)
    returned = spread(dep)
    spec, dep = lax.optimization_barrier((spec, dep))

    outgoing = stream_recv(entries, spec)
    outgoing, dye = lax.optimization_barrier((outgoing, dye))
    own = spread(outgoing)
    front = dye_send(entries, dye, returned)
    own, front = lax.optimization_barrier((own, front))
    other = swap_cores(own)
    front = spread(front.reshape(128, 2, 32, 128)).reshape(256, 32, 128)

    mine, theirs = gather(pos * 64 + row, own, other, col, fy, fx)
    mine, theirs, front = lax.optimization_barrier((mine, theirs, front))
    back = swap_chips(theirs)
    velocity = jnp.where(side == 0, jnp.concatenate([mine, back]), jnp.concatenate([back, mine]))
    dye_hat = dye_recv(front)
    return (velocity, dye_hat)


def solution(mesh):
    return jax.shard_map(
        shards,
        mesh=mesh,
        in_specs=(
            P(None, AXES, None),
            P(AXES, None),
            P(AXES),
            P(AXES),
            P(AXES),
            P(None, AXES),
            P(AXES),
            P(),
        ),
        out_specs=(P(None, AXES), P(None, AXES, None)),
        check_vma=False,
    )
```

```python
import numpy as np, math

import jax, jax.numpy as jnp
from jax import lax
from jax.sharding import PartitionSpec as P
from jax.experimental import pallas as pl
from jax.experimental.pallas import tpu as pltpu

BF = jnp.bfloat16
F32 = jnp.float32
NT = (((1,), (1,)), ((), ()))
PAD = 73
PAD2 = 137
PAD3 = 41


def cs(num, den, sign):
    ang = sign * 2.0 * math.pi * (num % den) / den
    return np.cos(ang), np.sin(ang)


def cplx(c, s):
    return np.stack([np.stack([c, -s]), np.stack([s, c])])


def bf(x):
    return np.asarray(x, np.float32).astype(jnp.bfloat16)


def send_tables(sign, stream):
    p = np.arange(64)
    q = np.arange(128)
    c, s = cs(p[:, None] * p[None, :], 64, sign)
    w = cplx(c, s).transpose(0, 2, 1, 3)
    if stream:
        a = w.reshape(128, 128)
        signed = np.where(p >= 32, p - 64, p) * 128.0
        b = (w * signed).reshape(128, 128)
        g = np.concatenate([a, b])
    else:
        g = w[:, :, 0, :].reshape(128, 64)
    tc, ts = cs(p[:, None] * q[None, :], 8192, sign)
    c, s = cs(q[:, None] * q[None, :], 128, sign)
    w2 = cplx(c, s).transpose(2, 0, 1, 3).reshape(256, 256)
    return bf(g), np.float32(tc), np.float32(ts), bf(w2)


def recv_tables(sign, stream):
    k = np.arange(128)
    r = np.arange(64)
    c, s = cs(k[:, None] * k[None, :], 128, sign)
    w1 = cplx(c, s).transpose(0, 2, 3, 1).reshape(256, 256)
    tc, ts = cs(k[:, None] * r[None, :], 8192, sign)
    tc = np.concatenate([tc, tc], 1)
    ts = np.concatenate([ts, ts], 1)
    c, s = cs(r[:, None] * r[None, :], 64, sign)
    w = cplx(c, s)
    v = np.zeros((2, 2, 64, 2, 2, 64))
    for e in range(2):
        v[:, e, :, :, e, :] = w.transpose(0, 2, 1, 3)
    if stream:
        v = v[0].reshape(128, 256)
    else:
        v = v.reshape(256, 256) / 8192.0
    return bf(w1), np.float32(tc), np.float32(ts), bf(v)


def stream_send_kernel(
    slot_ref, row_ref, col_ref, frac_ref, amount_ref, g_ref, tc_ref, ts_ref, w2_ref, s_hbm,
    floats_ref, o_hbm, s_ref, xs, tre, tim, of, o_ref, in_sem, out_sem,
):
    reads = []
    for k in range(4):
        lanes = pl.ds(2048 * k, 2048)
        reads.append(
            pltpu.make_async_copy(s_hbm.at[:, :, lanes], s_ref.at[:, :, lanes], in_sem.at[k])
        )
        reads[k].start()
    floats_ref[0:1, :] = slot_ref[...].astype(F32)
    floats_ref[1:2, :] = row_ref[...].astype(F32)
    floats_ref[2:3, :] = col_ref[...].astype(F32)
    floats_ref[3:5, :] = frac_ref[...]
    floats_ref[5:6, :] = amount_ref[...]

    def load(p, carry):
        at = pl.multiple_of(p * 128, 128)
        for c in range(2):
            row = (c * 64 + p) * PAD
            xs[pl.ds(row, 64), :] = s_ref[c, :, pl.ds(at, 128)].astype(F32)
        return carry

    for k in range(4):
        reads[k].wait()
        lax.fori_loop(16 * k, 16 * k + 16, load, 0, unroll=4)
    first = (lax.axis_index("wide") * 8 + lax.axis_index("narrow")) * 64
    q = lax.broadcasted_iota(jnp.int32, (64, 128), 1).astype(F32)

    def rows(n, carry):
        x = jnp.concatenate([xs[pl.ds(2 * n + h, 128, stride=PAD), :].astype(BF) for h in range(2)], axis=1)
        both = jnp.dot(g_ref[...], x, preferred_element_type=F32)
        tc = tc_ref[...]
        ts = ts_ref[...]
        for h in range(2):
            r = 2 * n + h
            z = both[:, h * 128 : h * 128 + 128]
            are, aim, bre, bim = z[:64], z[64:128], z[128:192], z[192:]
            ure = bre + q * are
            uim = bim + q * aim
            wa = jnp.where(first + r >= 4096, first + r - 8192, first + r).astype(F32)
            base = r * PAD2
            vre = are * tc - aim * ts
            vim = are * ts + aim * tc
            tre[pl.ds(base, 64), :] = ure * ts + uim * tc
            tim[pl.ds(base, 64), :] = uim * ts - ure * tc
            tre[pl.ds(base + 64, 64), :] = -wa * vim
            tim[pl.ds(base + 64, 64), :] = wa * vre
        return carry

    lax.fori_loop(0, 32, rows, 0, unroll=8)

    def cols(n, carry):
        parts = []
        for h in range(2):
            for f in range(2):
                at = pl.ds(f * 64 + 2 * n + h, 64, stride=PAD2)
                parts.append(jnp.concatenate([tre[at, :].astype(BF), tim[at, :].astype(BF)], axis=1))
        m = jnp.concatenate(parts, axis=0)
        out = lax.dot_general(w2_ref[...], m, NT, preferred_element_type=F32)
        for h in range(2):
            of[pl.ds(2 * n + h, 256, stride=PAD), :] = out[:, h * 128 : h * 128 + 128]
        return carry

    writes = []
    for k in range(4):
        lax.fori_loop(8 * k, 8 * k + 8, cols, 0, unroll=8)

        def store(i, carry, k=k):
            o_ref[i, 16 * k : 16 * k + 16] = of[pl.ds(i * PAD + 16 * k, 16), :].astype(BF)
            return carry

        lax.fori_loop(0, 256, store, 0, unroll=16)
        levels = pl.ds(16 * k, 16)
        writes.append(pltpu.make_async_copy(o_ref.at[:, levels, :], o_hbm.at[:, levels, :], out_sem.at[k]))
        writes[k].start()
    for write in writes:
        write.wait()


VM = pl.BlockSpec(memory_space=pltpu.VMEM)
SM = pl.BlockSpec(memory_space=pltpu.SMEM)
HB = pl.BlockSpec(memory_space=pl.ANY)


def call(kernel, outs, specs, scratch, cost, mib, name, *args, out_specs=None):
    return pl.pallas_call(
        kernel,
        out_shape=outs,
        in_specs=specs,
        out_specs=out_specs or jax.tree.map(lambda _: VM, outs),
        scratch_shapes=scratch,
        compiler_params=pltpu.CompilerParams(vmem_limit_bytes=mib << 20),
        cost_estimate=pl.CostEstimate(flops=cost, bytes_accessed=1 << 20, transcendentals=0),
        name=name,
    )(*args)


def stream_send(stream, floats):
    return call(
        stream_send_kernel,
        [jax.ShapeDtypeStruct((6, 8192), F32), jax.ShapeDtypeStruct((256, 64, 128), BF)],
        [VM] * 9 + [HB],
        [pltpu.VMEM((2, 64, 8192), BF), pltpu.VMEM((129 * PAD, 128), F32)]
        + [pltpu.VMEM((65 * PAD2, 128), F32)] * 2
        + [pltpu.VMEM((257 * PAD, 128), F32), pltpu.VMEM((256, 64, 128), BF)]
        + [pltpu.SemaphoreType.DMA((4,))] * 2,
        int(6e9), 60, "stream_send",
        *floats, *send_tables(1.0, True), stream, out_specs=[VM, HB],
    )


def stream_recv_kernel(idx_ref, x_ref, w1_ref, tc_ref, ts_ref, v_ref, o_ref, xf, of):
    def load(i, carry):
        xf[pl.ds(i * PAD, 64), :] = x_ref[i].astype(F32)
        return carry

    lax.fori_loop(0, 256, load, 0, unroll=8)

    def step(n, carry):
        d = jnp.concatenate([xf[pl.ds(2 * n + h, 256, stride=PAD), :].astype(BF) for h in range(2)], axis=1)
        z = jnp.dot(w1_ref[...], d, preferred_element_type=F32)
        tc = tc_ref[...]
        ts = ts_ref[...]
        parts = []
        for h in range(2):
            re = z[:128, h * 128 : h * 128 + 128]
            im = z[128:, h * 128 : h * 128 + 128]
            parts.append(
                jnp.concatenate([(re * tc - im * ts).astype(BF), (re * ts + im * tc).astype(BF)], axis=1)
            )
        m = jnp.concatenate(parts, axis=0)
        out = lax.dot_general(v_ref[...], m, NT, preferred_element_type=F32)
        for h in range(2):
            for f in range(2):
                of[pl.ds(64 * f + 2 * n + h, 64, stride=PAD2), :] = out[f * 64 : f * 64 + 64, h * 128 : h * 128 + 128]
        return carry

    lax.fori_loop(0, 32, step, 0, unroll=8)

    def store(n, carry):
        tile = jnp.maximum(idx_ref[0, n], 0)
        for f in range(2):
            data = of[pl.ds(tile * PAD2 + 64 * f, 64), :].astype(BF)
            for x in range(2):
                o_ref[n // 2 * 8 + 4 * x + 2 * f + n % 2] = data
        return carry

    lax.fori_loop(0, 32, store, 0, unroll=2)


def stream_recv(idx, x):
    return call(
        stream_recv_kernel,
        jax.ShapeDtypeStruct((128, 64, 128), BF),
        [SM] + [VM] * 5,
        [pltpu.VMEM((257 * PAD, 128), F32), pltpu.VMEM((65 * PAD2, 128), F32)],
        int(6e9), 28, "stream_recv",
        idx, x, *recv_tables(1.0, True),
    )


def dye_send_kernel(idx_ref, dye_ref, ret_ref, g_ref, tc_ref, ts_ref, w2_ref, o_ref, xs, tre, tim, of):
    def load(p, carry):
        at = pl.multiple_of(p * 128, 128)
        xs[pl.ds(p * PAD, 64), :] = dye_ref[:, pl.ds(at, 128)].astype(F32)
        return carry

    lax.fori_loop(0, 64, load, 0, unroll=4)

    def place(n, carry):
        tile = idx_ref[0, n]

        @pl.when(tile >= 0)
        def _():
            g = n // 2
            e = n % 2
            for half in range(2):
                at = pl.ds(tile * PAD + 32 * half, 32)
                total = xs[at, :]
                for x in range(2):
                    total = total + ret_ref[g * 8 + 4 * x + 2 * half + e].astype(F32)
                xs[at, :] = total

        return carry

    lax.fori_loop(0, 32, place, 0)

    def rows(n, carry):
        x = jnp.concatenate([xs[pl.ds(4 * n + h, 64, stride=PAD), :].astype(BF) for h in range(4)], axis=1)
        z = jnp.dot(g_ref[...], x, preferred_element_type=F32)
        tc = tc_ref[...]
        ts = ts_ref[...]
        for h in range(4):
            re = z[:64, h * 128 : h * 128 + 128]
            im = z[64:, h * 128 : h * 128 + 128]
            base = (4 * n + h) * PAD
            tre[pl.ds(base, 64), :] = re * tc - im * ts
            tim[pl.ds(base, 64), :] = re * ts + im * tc
        return carry

    lax.fori_loop(0, 16, rows, 0, unroll=8)

    def cols(n, carry):
        parts = []
        for e in range(4):
            at = pl.ds(4 * n + e, 64, stride=PAD)
            parts.append(jnp.concatenate([tre[at, :].astype(BF), tim[at, :].astype(BF)], axis=1))
        m = jnp.concatenate(parts, axis=0)
        out = lax.dot_general(w2_ref[...], m, NT, preferred_element_type=F32)
        for h in range(2):
            of[pl.ds(2 * n + h, 256, stride=PAD3), :] = out[:, h * 128 : h * 128 + 128]
        return carry

    lax.fori_loop(0, 16, cols, 0, unroll=8)

    def store(i, carry):
        o_ref[i] = of[pl.ds(i * PAD3, 32), :].astype(BF)
        return carry

    lax.fori_loop(0, 256, store, 0, unroll=8)


def dye_send(idx, dye, ret):
    return call(
        dye_send_kernel,
        jax.ShapeDtypeStruct((256, 32, 128), BF),
        [SM] + [VM] * 6,
        [pltpu.VMEM((65 * PAD, 128), F32)] * 3 + [pltpu.VMEM((257 * PAD3, 128), F32)],
        int(4e9), 24, "dye_send",
        idx, dye, ret, *send_tables(-1.0, False),
    )


def dye_recv_kernel(x_hbm, w1_ref, tc_ref, ts_ref, v_ref, o_hbm, xf, of, o_ref, x_ref, out_sem, in_sem):
    reads = []
    for h in range(2):
        levels = pl.ds(16 * h, 16)
        reads.append(
            pltpu.make_async_copy(x_hbm.at[:, levels, :], x_ref.at[:, levels, :], in_sem.at[h])
        )
        reads[h].start()

    def take(h):
        def load(i, carry):
            at = pl.ds(i * PAD3 + 16 * h, 16)
            xf[at, :] = x_ref[i, 16 * h : 16 * h + 16].astype(F32)
            return carry

        reads[h].wait()
        lax.fori_loop(0, 256, load, 0, unroll=8)

    def step(n, carry):
        d = jnp.concatenate([xf[pl.ds(2 * n + h, 256, stride=PAD3), :].astype(BF) for h in range(2)], axis=1)
        z = jnp.dot(w1_ref[...], d, preferred_element_type=F32)
        tc = tc_ref[...]
        ts = ts_ref[...]
        parts = []
        for h in range(2):
            re = z[:128, h * 128 : h * 128 + 128]
            im = z[128:, h * 128 : h * 128 + 128]
            parts.append(
                jnp.concatenate([(re * tc - im * ts).astype(BF), (re * ts + im * tc).astype(BF)], axis=1)
            )
        m = jnp.concatenate(parts, axis=0)
        out = lax.dot_general(v_ref[...], m, NT, preferred_element_type=F32)
        for h in range(2):
            for c in range(2):
                for e in range(2):
                    row = c * 4096 + (n // 2) * 512 + (4 * n + 2 * h + e) % 8
                    of[pl.ds(row, 64, stride=8), :] = out[
                        (2 * c + e) * 64 : (2 * c + e) * 64 + 64, h * 128 : h * 128 + 128
                    ]
        return carry

    writes = []
    for k in range(8):
        if k % 4 == 0:
            take(k // 4)
        for n in range(2 * k, 2 * k + 2):
            step(n, 0)
        at = pl.ds(8 * k, 8)
        for c in range(2):
            for j in range(64):
                o_ref[c, at, j * 128 : j * 128 + 128] = of[pl.ds(c * 4096 + k * 512 + j * 8, 8), :]
        writes.append(pltpu.make_async_copy(o_ref.at[:, at, :], o_hbm.at[:, at, :], out_sem.at[k]))
        writes[k].start()
    for write in writes:
        write.wait()


def dye_recv(x):
    return call(
        dye_recv_kernel,
        jax.ShapeDtypeStruct((2, 64, 8192), F32),
        [HB] + [VM] * 4,
        [pltpu.VMEM((257 * PAD3, 128), F32), pltpu.VMEM((8200, 128), F32)]
        + [pltpu.VMEM((2, 64, 8192), F32), pltpu.VMEM((256, 32, 128), BF)]
        + [pltpu.SemaphoreType.DMA((8,)), pltpu.SemaphoreType.DMA((2,))],
        int(4e9), 20, "dye_recv",
        x, *recv_tables(-1.0, False), out_specs=HB,
    )

CAPO = 2


def deposit_kernel(idx_ref, col_ref, fy_ref, fx_ref, am_ref, keep_ref, send_ref, *refs):
    bufs = refs[:4]
    accs = refs[4:]
    ways = len(accs)

    def clear(i, carry):
        for acc in accs:
            acc[pl.ds(pl.multiple_of(i * 40, 8), 40), :] = jnp.zeros((40, 128), F32)
        return carry

    lax.fori_loop(0, 257, clear, 0)

    def weights(n, dst):
        xs = lax.broadcasted_iota(jnp.int32, (128, 128), 0)
        rows = lax.broadcasted_iota(jnp.int32, (256, 128), 0)
        off = rows // 2 - lax.broadcasted_iota(jnp.int32, (256, 128), 1)
        odd = rows % 2 == 1
        at = pl.ds(pl.multiple_of(n * 128, 128), 128)
        fx = fx_ref[:, at]
        am = am_ref[:, at]
        hi = am * fy_ref[:, at]
        lo = am - hi
        d = xs - col_ref[:, at]
        w = jnp.where(d == 0, 1.0 - fx, jnp.where(d == 1, fx, 0.0)).astype(BF)
        e = jnp.where(off == 0, jnp.where(odd, hi, lo), 0.0).astype(BF)
        dst[...] = lax.dot_general(e, w, NT, preferred_element_type=F32)

    def add(n, src):
        for f in range(0, 128, ways):
            at = [pl.ds(idx_ref[n, f + k], 2) for k in range(ways)]
            new = [accs[k][at[k], :] + src[2 * (f + k) : 2 * (f + k) + 2, :] for k in range(ways)]
            for k in range(ways):
                accs[k][at[k], :] = new[k]

    weights(0, bufs[0])

    def chunk(n, carry):
        for q in range(4):
            weights(jnp.minimum(4 * n + q + 1, 127), bufs[(q + 1) % 4])
            add(4 * n + q, bufs[q])
        return carry

    lax.fori_loop(0, 32, chunk, 0)

    def store(i, carry):
        for ref, base in ((keep_ref, 8), (send_ref, 128 * 40 + 8)):
            at = pl.ds(pl.multiple_of(i * 40 + base, 8), 32)
            total = accs[0][at, :]
            for acc in accs[1:]:
                total = total + acc[at, :]
            ref[i] = total.astype(BF)
        return carry

    lax.fori_loop(0, 128, store, 0, unroll=2)


def deposit(idx, col, fy, fx, am):
    return call(
        deposit_kernel,
        [jax.ShapeDtypeStruct((128, 32, 128), BF)] * 2,
        [SM] + [VM] * 4,
        [pltpu.VMEM((256, 128), F32)] * 4 + [pltpu.VMEM((257 * 40, 128), F32)] * 4,
        int(2e10), 30, "deposit",
        idx, col, fy, fx, am,
    )


def gather_kernel(base_ref, a_ref, b_ref, col_ref, fy_ref, fx_ref, mine_ref, theirs_ref, st, *bufs):
    def load(i, carry):
        at = pl.multiple_of(i * 64, 64)
        st[pl.ds(at, 64), :] = a_ref[i].astype(F32)
        st[pl.ds(at + 8192, 64), :] = b_ref[i].astype(F32)
        return carry

    lax.fori_loop(0, 128, load, 0, unroll=4)

    def fetch(n, g):
        for f in range(128):
            g[f * 2 : f * 2 + 2, :] = st[pl.ds(base_ref[n, f], 2), :]

    def mix(n, g, o_ref, to):
        sub = lax.broadcasted_iota(jnp.int32, (8, 128), 0)
        off = lax.broadcasted_iota(jnp.int32, (8, 128), 1) - sub // 2
        xs = lax.broadcasted_iota(jnp.int32, (128, 128), 0)
        at = pl.ds(pl.multiple_of(n * 128, 128), 128)
        col = col_ref[:, at]
        fy = fy_ref[:, at]
        fx = fx_ref[:, at]
        d = xs - col
        w = jnp.where(d == 0, 1.0 - fx, jnp.where(d == 1, fx, 0.0))
        hi = w.astype(BF)
        lo = (w - hi.astype(F32)).astype(BF)
        rows = g[...].astype(BF)
        z = jnp.dot(
            jnp.concatenate([rows, rows], axis=1),
            jnp.concatenate([hi, lo], axis=0),
            preferred_element_type=F32,
        )
        parts = [jnp.zeros((8, 128), F32) for _ in range(4)]
        for i in range(32):
            parts[i % 4] = jnp.where(off == 4 * i, z[8 * i : 8 * i + 8], parts[i % 4])
        total = (parts[0] + parts[1] + (parts[2] + parts[3])) * jnp.where(sub % 2 == 1, fy, 1.0 - fy)
        o_ref[:, pl.ds(pl.multiple_of(to * 128, 128), 128)] = jnp.sum(total, axis=0, keepdims=True)

    fetch(0, bufs[0])
    for half, o_ref in enumerate((mine_ref, theirs_ref)):

        def chunk(n, carry, half=half, o_ref=o_ref):
            for q in range(8):
                at = half * 64 + 8 * n + q
                fetch(jnp.minimum(at + 1, 127), bufs[(q + 1) % 8])
                mix(at, bufs[q], o_ref, 8 * n + q)
            return carry

        lax.fori_loop(0, 8, chunk, 0)


def gather(base, a, b, col, fy, fx):
    return call(
        gather_kernel,
        [jax.ShapeDtypeStruct((1, 8192), F32)] * 2,
        [SM] + [VM] * 5,
        [pltpu.VMEM((16392, 128), F32)] + [pltpu.VMEM((256, 128), F32)] * 8,
        int(1e10), 20, "gather",
        base, a, b, col, fy, fx,
    )


AXES = ("wide", "narrow")


def spread(blocks):
    return lax.all_to_all(blocks, AXES, split_axis=0, concat_axis=0, tiled=True)


def swap_cores(x):
    n = lax.axis_size("narrow")
    return lax.ppermute(x, "narrow", [(i, i ^ 1) for i in range(n)])


def swap_chips(x):
    n = lax.axis_size("narrow")
    return lax.ppermute(x, "narrow", [(i, i ^ 2) for i in range(n)])


def shards(stream_hat, dye, float_slot, float_row, float_col, float_frac, float_dye, tile_lists):
    device = lax.axis_index(AXES)
    group = lax.axis_index("wide")
    core = lax.axis_index("narrow") % 2
    side = lax.axis_index("narrow") // 2 % 2

    line = lambda x: x.reshape(1, 8192)
    own_floats, spec = stream_send(
        stream_hat,
        (line(float_slot), line(float_row), line(float_col), float_frac, line(float_dye)),
    )
    their_floats = swap_chips(own_floats)
    spec, own_floats, tile_lists = lax.optimization_barrier((spec, own_floats, tile_lists))
    spec = spread(spec.reshape(128, 2, 64, 128)).reshape(256, 64, 128)
    floats = jnp.concatenate([own_floats, their_floats], axis=1)
    slot = floats[0].astype(jnp.int32).reshape(128, 128)
    row = floats[1].astype(jnp.int32).reshape(128, 128)
    col = floats[2:3].astype(jnp.int32)
    fy = floats[3:4]
    fx = floats[4:5]
    amount = floats[5:6]

    own_list = lax.dynamic_index_in_dim(tile_lists, group, 0, keepdims=False)
    holder = own_list // 64
    before = jnp.arange(256)[:, None] > jnp.arange(256)[None, :]
    rank = jnp.sum((before & (holder[:, None] == holder[None, :])).astype(jnp.int32), axis=1)
    position = jnp.where(own_list >= 0, jnp.where(rank == core, 0, 128) + holder, 0)
    pos = jnp.sum(
        jnp.where(jnp.arange(256)[:, None, None] == slot[None], position[:, None, None], 0), axis=0
    )

    mine = (tile_lists >= 0) & (tile_lists // 64 == device)
    place = jnp.cumsum(mine.astype(jnp.int32), axis=1) - 1
    local = tile_lists % 64 + 1
    entries = jnp.stack(
        [jnp.sum(jnp.where(mine & (place == e), local, 0), axis=1) for e in range(CAPO)], axis=1
    ).reshape(1, 32) - 1

    level = row - 32 * side
    base = jnp.where((level >= -1) & (level <= 31), pos * 40 + 8 + level, 0)
    keep, send = deposit(base, col, fy, fx, amount)
    dep = (keep.astype(F32) + swap_cores(send).astype(F32)).astype(BF)
    returned = spread(dep)
    spec, dep = lax.optimization_barrier((spec, dep))

    outgoing = stream_recv(entries, spec)
    outgoing, dye = lax.optimization_barrier((outgoing, dye))
    own = spread(outgoing)
    front = dye_send(entries, dye, returned)
    own, front = lax.optimization_barrier((own, front))
    other = swap_cores(own)
    front = spread(front.reshape(128, 2, 32, 128)).reshape(256, 32, 128)

    mine, theirs = gather(pos * 64 + row, own, other, col, fy, fx)
    back = swap_chips(theirs)
    mine, front = lax.optimization_barrier((mine, front))
    velocity = jnp.where(side == 0, jnp.concatenate([mine, back]), jnp.concatenate([back, mine]))
    dye_hat = dye_recv(front)
    return (velocity, dye_hat)


def solution(mesh):
    return jax.shard_map(
        shards,
        mesh=mesh,
        in_specs=(
            P(None, AXES, None),
            P(AXES, None),
            P(AXES),
            P(AXES),
            P(AXES),
            P(None, AXES),
            P(AXES),
            P(),
        ),
        out_specs=(P(None, AXES), P(None, AXES, None)),
        check_vma=False,
    )
```
